32 devices in a mesh: blk: 8 (over y, x, core), rep: 4 (over z).
Axes of the slice: x: 2, y: 2, z: 4, core: 2. Of those that a mesh axis runs over, the one named last changes fastest.
Arguments:
- cotangent: bfloat16 [256, 256, 128], P('blk', 'rep'), may hold values from -6 to 6
- relu_mask: int32 [256, 256, 128], P('blk', 'rep'), may hold values 0 or 1
- aggregated: bfloat16 [256, 256, 128], P('blk', 'rep'), may hold values from -6 to 6
- weight: bfloat16 [256, 256], P('rep'), may hold values from -0.375 to 0.375
- tiles: bfloat16 [256, 16, 128, 128], P('blk'), may hold values from -0.125 to 0.125
- col_block: int32 [256, 16], P('blk'), may hold values from 0 to 255, as said below
- live_count: int32 [256], P('blk'), may hold values from 1 to 16, as said below
Outputs:
- input_grad: bfloat16 [256, 256, 128], P('blk', 'rep')
- weight_grad: float32 [256, 256], P('rep')
The draws below stay inside these ranges and needn't reach their ends.
Inputs may be any that keep to these rules, and one draw needn't show every extreme that they name: The slab of a row block b is b // 32; the slab of col_block[b, s] lies at most 2 slabs from it around the closed cycle of the 8 slabs, and both distance 2 directions occur. `live_count`: row blocks of one slab share a density level, so live counts differ from slab to slab; some row block has all 16 slots live.
All inputs are finite; a program needn't handle non-finite values. No bound on the sum of `relu_mask` on one device may be relied on, other than what follows from the above.
Results may differ from the reference program's by a relative error of at most 0.0049.
Values may be sent and summed in bfloat16 or wider, within the bound.
No kernel may reach another device: no remote copies, remote signals or barrier semaphores. Data moves between devices by JAX's collectives and lax.ppermute only.
A program may use at most 128 MiB of HBM per device.

```python
import math
import jax
import jax.numpy as jnp
from jax import lax

WIDTH = 256
TILE = 128
SLOTS = 16
REACH = 2
BLOCKS_DEV = 32
BLOCKS = 256
NODES = 32768


def draw_col_block(key, part):
    slabs = BLOCKS // BLOCKS_DEV
    key_off = jax.random.fold_in(key, 11)
    key_in = jax.random.fold_in(key, 12)
    offsets = jax.random.randint(key_off, (BLOCKS, SLOTS), -REACH, REACH + 1, dtype=jnp.int32)
    offsets = offsets.at[0, 0].set(REACH)
    offsets = offsets.at[0, 1].set(-REACH)
    within = jax.random.randint(key_in, (BLOCKS, SLOTS), 0, BLOCKS_DEV, dtype=jnp.int32)
    row_slab = (jnp.arange(BLOCKS, dtype=jnp.int32) // BLOCKS_DEV)[:, None]
    target = (row_slab + offsets) % slabs * BLOCKS_DEV + within
    return target.astype(jnp.int32)


def draw_live_count(key, part):
    slabs = BLOCKS // BLOCKS_DEV
    key_level = jax.random.fold_in(key, 21)
    key_each = jax.random.fold_in(key, 22)
    level = jax.random.randint(key_level, (slabs,), max(1, SLOTS // 4), SLOTS + 1, dtype=jnp.int32)
    level = jnp.repeat(level, BLOCKS_DEV)
    lowest = jnp.maximum(level // 2, 1)
    spread = jax.random.randint(key_each, (BLOCKS,), 0, 1 << 20, dtype=jnp.int32)
    counts = lowest + spread % (level - lowest + 1)
    counts = counts.at[0].set(SLOTS)
    return counts.astype(jnp.int32)


def plant(values, stream_key, smallest, top_value):
    longest = values.shape.index(max(values.shape))
    spots = []
    for shift in (0, 1):
        where = [jax.random.randint(jax.random.fold_in(stream_key, axis), (), 0, length) for axis, length in enumerate(values.shape)]
        where[longest] = (where[longest] + shift) % values.shape[longest]
        spots.append(tuple(where))
    return values.at[spots[0]].set(smallest).at[spots[1]].set(top_value)


def steps_of(stream_key, dims, split, smallest, largest):
    def one(dim, shards_of):
        steps = jax.random.uniform(jax.random.fold_in(jax.random.fold_in(stream_key, 6), dim), (shards_of,), jnp.float32, smallest / len(split), largest / len(split))
        return jnp.repeat(jnp.exp(steps), dims[dim] // shards_of).reshape((-1,) + (1,) * (len(dims) - dim - 1))

    loudness = one(*split[0])
    for cut in split[1:]:
        loudness = loudness * one(*cut)
    return loudness


def centred(own_key, extent, width, reach, pieces=(), kind=jnp.bfloat16):
    gain = steps_of(own_key, extent, pieces, -0.22, 0.18) if pieces else 1.0
    values = jax.random.normal(own_key, extent, jnp.float32) * width * gain
    return jnp.minimum(jnp.maximum(values, -reach), reach).astype(kind)


def setup_inputs(seed: int = 0) -> dict:
    key_list = jax.random.split(jax.random.key(seed), 8)
    return {
        "cotangent": centred(key_list[0], (BLOCKS, WIDTH, TILE), 1.0, 6.0, ((0, 8), (1, 4))),
        "relu_mask": plant((jax.random.randint(key_list[1], (BLOCKS, WIDTH, TILE), 0, 2) < 1).astype(jnp.int32), jax.random.fold_in(key_list[1], 1), 0, 1),
        "aggregated": centred(key_list[2], (BLOCKS, WIDTH, TILE), 1.0, 6.0, ((0, 8), (1, 4))),
        "weight": centred(key_list[3], (WIDTH, WIDTH), WIDTH ** -0.5, 0.375, ((0, 4),)),
        "tiles": centred(key_list[4], (BLOCKS, SLOTS, TILE, TILE), (TILE * SLOTS) ** -0.5, 0.125, ((0, 8),)),
        "col_block": draw_col_block(jax.random.fold_in(key_list[7], 71), 0),
        "live_count": draw_live_count(jax.random.fold_in(key_list[7], 71), 0),
    }


def reference(cotangent, relu_mask, aggregated, weight, tiles, col_block, live_count):
    grad_z = cotangent * relu_mask.astype(jnp.bfloat16)
    grad_zf = grad_z.astype(jnp.float32)
    grad_h = jnp.einsum('io,bon->bin', weight.astype(jnp.float32), grad_zf).astype(jnp.bfloat16)
    weight_grad = jnp.einsum('bin,bon->io', aggregated.astype(jnp.float32), grad_zf) * (1.0 / math.sqrt(NODES))
    grad_hf = grad_h.astype(jnp.float32)
    slot_tiles = jnp.moveaxis(tiles, 1, 0)
    slot_cols = jnp.transpose(col_block)
    slot_ids = jnp.arange(SLOTS, dtype=jnp.int32)

    def one_slot(total_grad, inputs):
        tile_set, cols, slot_id = inputs
        live = (slot_id < live_count).astype(jnp.float32)
        masked = tile_set.astype(jnp.float32) * live[:, None, None]
        terms = jnp.einsum('bij,bfi->bfj', masked, grad_hf)
        total_grad = total_grad + jax.ops.segment_sum(terms, cols, num_segments=BLOCKS)
        return (total_grad, None)
    start_grad = jnp.zeros((BLOCKS, WIDTH, TILE), jnp.float32)
    input_grad, unused = lax.scan(one_slot, start_grad, (slot_tiles, slot_cols, slot_ids))
    return (input_grad.astype(jnp.bfloat16), weight_grad)
```

```python
import functools
import math

import jax
import jax.numpy as jnp
from jax import lax
from jax.experimental import pallas as pl
from jax.experimental.pallas import tpu as pltpu
from jax.sharding import PartitionSpec as P

REACH = 2
CHUNKS = 2
BF16 = jnp.bfloat16
F32 = jnp.float32


def vmem():
    return pl.BlockSpec(memory_space=pltpu.VMEM)


def smem():
    return pl.BlockSpec(memory_space=pltpu.SMEM)


def hbm():
    return pl.BlockSpec(memory_space=pl.ANY)


def tiles_kernel(slabs, chunk, where, cols, z_ref, tiles_ref, *rest):
    outs, (held, total, sems) = rest[:-3], rest[-3:]
    blocks, slots = tiles_ref.shape[:2]
    window = (2 * REACH + 1) * blocks
    for b in range(blocks):
        pltpu.make_async_copy(tiles_ref.at[b], held.at[b], sems.at[b]).start()

    def clear(i, carry):
        total[i] = jnp.zeros(total.shape[1:], F32)
        return carry

    lax.fori_loop(0, window, clear, 0)
    own = where[0]
    sign = 2 * lax.rem(own, 2) - 1

    def row_block(b, carry):
        pltpu.make_async_copy(tiles_ref.at[b], held.at[b], sems.at[b]).wait()
        z = z_ref[b]
        live = cols[b, slots]
        for s in range(slots):
            col = cols[b, s]
            slab = lax.div(col, blocks)
            offset = lax.rem(slab - own + REACH + slabs, slabs) - REACH
            place = (offset * sign + REACH) * blocks + lax.rem(col, blocks)
            place = jnp.where(s < live, place, window)
            total[place] += jnp.dot(z, held[b, s], preferred_element_type=F32)
        return carry

    lax.fori_loop(0, blocks, row_block, 0)

    parts = 2 * REACH + 1
    chunks = blocks // chunk
    for part in range(parts):
        for k in range(chunks):

            def store(i, carry, out=outs[part * chunks + k], base=part * blocks + k * chunk):
                out[i] = total[base + i].astype(BF16)
                return carry

            lax.fori_loop(0, chunk, store, 0)


def contributions(where, cols, z, tiles, slabs, chunk):
    blocks, features, nodes = z.shape
    slots = tiles.shape[1]
    chunks = blocks // chunk
    parts = 2 * REACH + 1
    window = parts * blocks
    outs = pl.pallas_call(
        functools.partial(tiles_kernel, slabs, chunk),
        out_shape=[jax.ShapeDtypeStruct((chunk, features, nodes), BF16)] * (parts * chunks),
        in_specs=[smem(), smem(), vmem(), hbm()],
        out_specs=[vmem()] * (parts * chunks),
        scratch_shapes=[
            pltpu.VMEM(tiles.shape, BF16),
            pltpu.VMEM((window + 1, features, nodes), F32),
            pltpu.SemaphoreType.DMA((blocks,)),
        ],
        compiler_params=pltpu.CompilerParams(vmem_limit_bytes=40 << 20),
        cost_estimate=pl.CostEstimate(
            flops=2 * blocks * slots * features * nodes * nodes,
            bytes_accessed=tiles.size * 2 + 6 * z.size * 2,
            transcendentals=0,
        ),
    )(where, cols, z, tiles)
    return [outs[part * chunks : (part + 1) * chunks] for part in range(parts)]


def lay_features(where, shares, whole, reps):
    width = shares[0].shape[1]
    for s, share in enumerate(shares):
        first = lax.rem(where[1] - s + reps, reps) * width
        whole[:, pl.ds(pl.multiple_of(first, width), width), :] = share[...]


def weight_kernel(reps, where, *rest):
    aggs, shares = rest[:reps], rest[reps : 2 * reps]
    outs, whole = rest[2 * reps : 3 * reps], rest[3 * reps]
    lay_features(where, shares, whole, reps)
    blocks = whole.shape[0]
    for s in range(reps):
        total = jnp.zeros(outs[s].shape, F32)
        for b in range(blocks):
            total += lax.dot_general(
                aggs[s][b], whole[b], (((1,), (1,)), ((), ())), preferred_element_type=F32
            )
        outs[s][...] = total.astype(outs[s].dtype)


def weight_partial(where, aggs, shares):
    reps = len(shares)
    blocks, features, nodes = shares[0].shape
    width = reps * features
    return pl.pallas_call(
        functools.partial(weight_kernel, reps),
        out_shape=[jax.ShapeDtypeStruct((features, width), F32)] * reps,
        in_specs=[smem()] + [vmem()] * (2 * reps),
        out_specs=[vmem()] * reps,
        scratch_shapes=[pltpu.VMEM((blocks, width, nodes), BF16)],
        cost_estimate=pl.CostEstimate(
            flops=2 * blocks * nodes * width * width,
            bytes_accessed=4 * blocks * nodes * width + 4 * width * width,
            transcendentals=0,
        ),
    )(where, *aggs, *shares)


def mix_kernel(reps, where, *rest):
    weights, shares = rest[:reps], rest[reps : 2 * reps]
    outs, whole = rest[2 * reps : 3 * reps], rest[3 * reps]
    lay_features(where, shares, whole, reps)
    for b in range(whole.shape[0]):
        for s in range(reps):
            mixed = jnp.dot(weights[s][...], whole[b], preferred_element_type=F32)
            outs[s][b] = mixed.astype(BF16)


def mix(where, weights, shares):
    reps = len(shares)
    blocks, features, nodes = shares[0].shape
    width = reps * features
    return pl.pallas_call(
        functools.partial(mix_kernel, reps),
        out_shape=[jax.ShapeDtypeStruct((blocks, features, nodes), BF16)] * reps,
        in_specs=[smem()] + [vmem()] * (2 * reps),
        out_specs=[vmem()] * reps,
        scratch_shapes=[pltpu.VMEM((blocks, width, nodes), BF16)],
        cost_estimate=pl.CostEstimate(
            flops=2 * blocks * nodes * width * width,
            bytes_accessed=4 * blocks * nodes * width,
            transcendentals=0,
        ),
    )(where, *weights, *shares)


def lay_kernel(reps, chunks, where, *rest):
    shares, out, sems = rest[: reps * chunks], rest[-2], rest[-1]
    copies = []
    for k in range(chunks):
        for s in range(reps):
            share = shares[k * reps + s]
            blocks = share.shape[0]
            first = (k * reps + lax.rem(where[1] - s + reps, reps)) * blocks
            copy = pltpu.make_async_copy(share, out.at[pl.ds(first, blocks)], sems.at[k * reps + s])
            copy.start()
            copies.append(copy)
    for copy in copies:
        copy.wait()


def lay_blocks(where, shares, shape):
    chunks, reps = len(shares), len(shares[0])
    return pl.pallas_call(
        functools.partial(lay_kernel, reps, chunks),
        out_shape=jax.ShapeDtypeStruct(shape, BF16),
        in_specs=[smem()] + [hbm()] * (reps * chunks),
        out_specs=hbm(),
        scratch_shapes=[pltpu.SemaphoreType.DMA((reps * chunks,))],
    )(where, *[share for chunk in shares for share in chunk])


def shift(value, axis, steps):
    count = lax.axis_size(axis)
    if steps % count == 0:
        return value
    return lax.ppermute(value, axis, [(i, (i + steps) % count) for i in range(count)])


def node_share(value, steps):
    reps = lax.axis_size("rep")
    blocks = value.shape[0] // reps
    first = lax.rem(lax.axis_index("rep") + steps, reps) * blocks
    return lax.dynamic_slice_in_dim(value, first, blocks, 0)


def to_node_shares(value):
    return [shift(node_share(value, s), "rep", s) for s in range(lax.axis_size("rep"))]


def on_device(cotangent, relu_mask, aggregated, weight, tiles, col_block, live_count):
    blocks = cotangent.shape[0]
    nodes = cotangent.shape[2]
    slabs, reps = lax.axis_size("blk"), lax.axis_size("rep")
    chunk = blocks // CHUNKS
    where = jnp.stack([lax.axis_index("blk"), lax.axis_index("rep")]).astype(jnp.int32)
    cols = jnp.concatenate([col_block, live_count[:, None]], axis=1)

    grad_z = cotangent * relu_mask.astype(BF16)
    aggs = to_node_shares(aggregated)
    shares = to_node_shares(grad_z)
    weights = [shift(weight, "rep", -s) for s in range(reps)]

    near, beside, own, first, second = contributions(where, cols, grad_z, tiles, slabs, chunk)

    grad_w = weight_partial(where, aggs, shares)
    grad_w = sum(shift(part.astype(BF16), "rep", -s).astype(F32) for s, part in enumerate(grad_w))
    step = 1
    while step < slabs:
        pairs = [(i, i ^ step) for i in range(slabs)]
        grad_w = grad_w + lax.ppermute(grad_w, "blk", pairs)
        step *= 2
    weight_grad = grad_w * (1.0 / math.sqrt(slabs * blocks * nodes))

    pair = [(i, i ^ 1) for i in range(slabs)]
    across = [(i, (i - 3) % slabs) for i in range(slabs) if i % 4 == 0]
    across += [(i, (i + 3) % slabs) for i in range(slabs) if i % 4 == 3]
    to_one = [(i, (i + 1) % slabs) for i in range(slabs) if i % 4 == 1]
    to_one += [(i, (i - 1) % slabs) for i in range(slabs) if i % 4 == 2]
    to_two = [(i, (i + 2) % slabs) for i in range(slabs) if i % 4 == 1]
    to_two += [(i, (i - 2) % slabs) for i in range(slabs) if i % 4 == 2]

    def add(*terms):
        return sum(term.astype(F32) for term in terms).astype(BF16)

    mixed = []
    for k in range(CHUNKS):
        one = add(first[k], lax.ppermute(near[k], "blk", pair))
        two = second[k]
        held = lax.ppermute(beside[k], "blk", pair)
        one_over = lax.ppermute(one, "blk", across)
        two_over = lax.ppermute(two, "blk", across)
        one_in = lax.ppermute(add(one, two_over), "blk", to_one)
        two_in = lax.ppermute(add(two, one_over), "blk", to_two)
        sums = add(own[k], held, one_in, two_in)
        outs = mix(where, weights, to_node_shares(sums))
        mixed.append([shift(part, "rep", s) for s, part in enumerate(outs)])
    return lay_blocks(where, mixed, cotangent.shape), weight_grad


def solution(mesh):
    placed = (
        P("blk", "rep", None),
        P("blk", "rep", None),
        P("blk", "rep", None),
        P("rep", None),
        P("blk", None, None, None),
        P("blk", None),
        P("blk"),
    )
    return jax.shard_map(
        on_device,
        mesh=mesh,
        in_specs=placed,
        out_specs=(P("blk", "rep", None), P("rep", None)),
        check_vma=False,
    )
```

```python
import functools
import math

import jax
import jax.numpy as jnp
from jax import lax
from jax.experimental import pallas as pl
from jax.experimental.pallas import tpu as pltpu
from jax.sharding import PartitionSpec as P

REACH = 2
CHUNKS = 2
BF16 = jnp.bfloat16
F32 = jnp.float32


def vmem():
    return pl.BlockSpec(memory_space=pltpu.VMEM)


def smem():
    return pl.BlockSpec(memory_space=pltpu.SMEM)


def hbm():
    return pl.BlockSpec(memory_space=pl.ANY)


def tiles_kernel(slabs, chunk, where, cols, z_ref, tiles_ref, *rest):
    outs, (held, total, sems) = rest[:-3], rest[-3:]
    blocks, slots = tiles_ref.shape[:2]
    window = (2 * REACH + 1) * blocks
    for b in range(blocks):
        pltpu.make_async_copy(tiles_ref.at[b], held.at[b], sems.at[b]).start()

    def clear(i, carry):
        total[i] = jnp.zeros(total.shape[1:], F32)
        return carry

    lax.fori_loop(0, window, clear, 0)
    own = where[0]
    sign = 2 * lax.rem(own, 2) - 1

    def row_block(b, carry):
        pltpu.make_async_copy(tiles_ref.at[b], held.at[b], sems.at[b]).wait()
        z = z_ref[b]
        live = cols[b, slots]
        for s in range(slots):
            col = cols[b, s]
            slab = lax.div(col, blocks)
            offset = lax.rem(slab - own + REACH + slabs, slabs) - REACH
            place = (offset * sign + REACH) * blocks + lax.rem(col, blocks)
            place = jnp.where(s < live, place, window)
            total[place] += jnp.dot(z, held[b, s], preferred_element_type=F32)
        return carry

    lax.fori_loop(0, blocks, row_block, 0)

    parts = 2 * REACH + 1
    chunks = blocks // chunk
    for part in range(parts):
        for k in range(chunks):

            def store(i, carry, out=outs[part * chunks + k], base=part * blocks + k * chunk):
                out[i] = total[base + i].astype(BF16)
                return carry

            lax.fori_loop(0, chunk, store, 0)


def contributions(where, cols, z, tiles, slabs, chunk):
    blocks, features, nodes = z.shape
    slots = tiles.shape[1]
    chunks = blocks // chunk
    parts = 2 * REACH + 1
    window = parts * blocks
    outs = pl.pallas_call(
        functools.partial(tiles_kernel, slabs, chunk),
        out_shape=[jax.ShapeDtypeStruct((chunk, features, nodes), BF16)] * (parts * chunks),
        in_specs=[smem(), smem(), vmem(), hbm()],
        out_specs=[vmem()] * (parts * chunks),
        scratch_shapes=[
            pltpu.VMEM(tiles.shape, BF16),
            pltpu.VMEM((window + 1, features, nodes), F32),
            pltpu.SemaphoreType.DMA((blocks,)),
        ],
        compiler_params=pltpu.CompilerParams(vmem_limit_bytes=40 << 20),
        cost_estimate=pl.CostEstimate(
            flops=2 * blocks * slots * features * nodes * nodes,
            bytes_accessed=tiles.size * 2 + 6 * z.size * 2,
            transcendentals=0,
        ),
    )(where, cols, z, tiles)
    return [outs[part * chunks : (part + 1) * chunks] for part in range(parts)]


def weight_kernel(reps, parts, packed, out, whole_z, whole_a):
    blocks, features = packed.shape[1] // parts, packed.shape[2]
    for q in range(reps):
        rows = pl.ds(q * features, features)
        whole_z[:, rows, :] = packed[q, :blocks]
        whole_a[:, rows, :] = packed[q, blocks : 2 * blocks]
    total = jnp.zeros((reps * features, reps * features), F32)
    for b in range(blocks):
        total += lax.dot_general(
            whole_a[b], whole_z[b], (((1,), (1,)), ((), ())), preferred_element_type=F32
        )
    out[...] = total.astype(BF16)


def weight_partial(packed, parts):
    reps, packs, features, nodes = packed.shape
    blocks = packs // parts
    width = reps * features
    return pl.pallas_call(
        functools.partial(weight_kernel, reps, parts),
        out_shape=jax.ShapeDtypeStruct((width, width), BF16),
        in_specs=[vmem()],
        out_specs=vmem(),
        scratch_shapes=[pltpu.VMEM((blocks, width, nodes), BF16)] * 2,
        cost_estimate=pl.CostEstimate(
            flops=2 * blocks * nodes * width * width,
            bytes_accessed=4 * blocks * nodes * width + 2 * width * width,
            transcendentals=0,
        ),
    )(packed)


def mix_kernel(reps, weights, shares, out, whole):
    blocks, features = shares.shape[1:3]
    for q in range(reps):
        whole[:, pl.ds(q * features, features), :] = shares[q]
    for b in range(blocks):
        mixed = jnp.dot(weights[...], whole[b], preferred_element_type=F32)
        for q in range(reps):
            out[q, b] = mixed[q * features : (q + 1) * features].astype(BF16)


def mix(weights, shares):
    reps, blocks, features, nodes = shares.shape
    width = reps * features
    return pl.pallas_call(
        functools.partial(mix_kernel, reps),
        out_shape=jax.ShapeDtypeStruct(shares.shape, BF16),
        in_specs=[vmem(), vmem()],
        out_specs=vmem(),
        scratch_shapes=[pltpu.VMEM((blocks, width, nodes), BF16)],
        cost_estimate=pl.CostEstimate(
            flops=2 * blocks * nodes * width * width,
            bytes_accessed=4 * blocks * nodes * width,
            transcendentals=0,
        ),
    )(weights, shares)


def exchange(value, axis):
    return lax.all_to_all(value, axis, 0, 0, tiled=True)


def on_device(cotangent, relu_mask, aggregated, weight, tiles, col_block, live_count):
    blocks, features, nodes = cotangent.shape
    slabs, reps = lax.axis_size("blk"), lax.axis_size("rep")
    width = weight.shape[1]
    chunk = blocks // CHUNKS
    share = blocks // reps
    where = lax.axis_index("blk").astype(jnp.int32)[None]
    cols = jnp.concatenate([col_block, live_count[:, None]], axis=1)

    grad_z = cotangent * relu_mask.astype(BF16)
    by_share = (reps, share, features, nodes)
    packed = jnp.concatenate([grad_z.reshape(by_share), aggregated.reshape(by_share)], axis=1)
    packed = exchange(packed, "rep")
    weights = exchange(jnp.broadcast_to(weight[None], (reps, features, width)), "rep")
    weights = weights.reshape(reps * features, width)

    near, beside, own, first, second = contributions(where, cols, grad_z, tiles, slabs, chunk)

    pair = [(i, i ^ 1) for i in range(slabs)]
    to_one = [(i, (i + (1 if i % 2 else -1)) % slabs) for i in range(slabs)]
    to_two = [(i, (i + (2 if i % 2 else -2)) % slabs) for i in range(slabs)]

    def add(*terms):
        return sum(term.astype(F32) for term in terms).astype(BF16)

    grad_w = weight_partial(packed, 2).reshape(reps, features, width)
    mixed = []
    for k in range(CHUNKS):
        one = add(first[k], lax.ppermute(near[k], "blk", pair))
        held = lax.ppermute(beside[k], "blk", pair)
        two_in = lax.ppermute(second[k], "blk", to_two)
        one_in = lax.ppermute(one, "blk", to_one)
        sums = add(own[k], held, one_in, two_in)
        shares = exchange(sums.reshape(reps, chunk // reps, features, nodes), "rep")
        mixed.append(exchange(mix(weights, shares), "rep").reshape(chunk, features, nodes))

    grad_w = exchange(grad_w, "rep").astype(F32).sum(0)
    step = 1
    while step < slabs:
        grad_w = grad_w + lax.ppermute(grad_w, "blk", [(i, i ^ step) for i in range(slabs)])
        step *= 2
    weight_grad = grad_w * (1.0 / math.sqrt(slabs * blocks * nodes))
    return jnp.concatenate(mixed, axis=0), weight_grad


def solution(mesh):
    placed = (
        P("blk", "rep", None),
        P("blk", "rep", None),
        P("blk", "rep", None),
        P("rep", None),
        P("blk", None, None, None),
        P("blk", None),
        P("blk"),
    )
    return jax.shard_map(
        on_device,
        mesh=mesh,
        in_specs=placed,
        out_specs=(P("blk", "rep", None), P("rep", None)),
        check_vma=False,
    )
```

```python
import functools
import math

import jax
import jax.numpy as jnp
from jax import lax
from jax.experimental import pallas as pl
from jax.experimental.pallas import tpu as pltpu
from jax.sharding import PartitionSpec as P

REACH = 2
CHUNKS = 2
BF16 = jnp.bfloat16
F32 = jnp.float32


def vmem():
    return pl.BlockSpec(memory_space=pltpu.VMEM)


def smem():
    return pl.BlockSpec(memory_space=pltpu.SMEM)


def hbm():
    return pl.BlockSpec(memory_space=pl.ANY)


def tiles_kernel(slabs, where, cols, z_ref, tiles_ref, aside, own_out, *rest):
    leave, (held, total, sems) = rest[:-3], rest[-3:]
    blocks, slots = tiles_ref.shape[:2]
    nodes = z_ref.shape[2]
    window = (2 * REACH + 1) * blocks
    for b in range(blocks):
        pltpu.make_async_copy(tiles_ref.at[b], held.at[b], sems.at[b]).start()

    def clear(i, carry):
        total[i] = jnp.zeros(total.shape[1:], F32)
        return carry

    lax.fori_loop(0, window, clear, 0)
    own = where[0]
    sign = 2 * lax.rem(own, 2) - 1

    def row_block(b, carry):
        pltpu.make_async_copy(tiles_ref.at[b], held.at[b], sems.at[b]).wait()
        z = z_ref[b]
        live = cols[b, slots]
        for s in range(0, slots, 2):
            both = jnp.concatenate([held[b, s], held[b, s + 1]], axis=1)
            terms = jnp.dot(z, both, preferred_element_type=F32)
            for half in range(2):
                col = cols[b, s + half]
                slab = lax.div(col, blocks)
                offset = lax.rem(slab - own + REACH + slabs, slabs) - REACH
                place = (offset * sign + REACH) * blocks + lax.rem(col, blocks)
                place = jnp.where(s + half < live, place, window)
                total[place] += terms[:, half * nodes : (half + 1) * nodes]
        return carry

    lax.fori_loop(0, blocks, row_block, 0)

    def store(out, base):
        def one(i, carry):
            out[i] = total[base + i].astype(BF16)
            return carry

        lax.fori_loop(0, out.shape[0], one, 0)

    store(aside, 0)
    store(own_out, REACH * blocks)
    chunk = leave[0].shape[0]
    for i, out in enumerate(leave):
        store(out, (REACH + 1) * blocks + i * chunk)


def contributions(where, cols, z, tiles, slabs):
    blocks, features, nodes = z.shape
    chunk = blocks // CHUNKS
    window = (2 * REACH + 1) * blocks
    counts = [REACH * blocks, blocks] + [chunk] * (REACH * CHUNKS)
    aside, own, *leave = pl.pallas_call(
        functools.partial(tiles_kernel, slabs),
        out_shape=[jax.ShapeDtypeStruct((count, features, nodes), BF16) for count in counts],
        in_specs=[smem(), smem(), vmem(), hbm()],
        out_specs=[vmem()] * len(counts),
        scratch_shapes=[
            pltpu.VMEM(tiles.shape, BF16),
            pltpu.VMEM((window + 1, features, nodes), F32),
            pltpu.SemaphoreType.DMA((blocks,)),
        ],
        compiler_params=pltpu.CompilerParams(vmem_limit_bytes=40 << 20),
        cost_estimate=pl.CostEstimate(flops=0, bytes_accessed=0, transcendentals=0),
    )(where, cols, z, tiles)
    return aside, own, leave[:CHUNKS], leave[CHUNKS:]


def weight_kernel(packed, out, whole_z, whole_a):
    blocks, features = whole_z.shape[0], packed.shape[2]
    for q in range(packed.shape[0]):
        rows = pl.ds(q * features, features)
        whole_z[:, rows, :] = packed[q, :blocks]
        whole_a[:, rows, :] = packed[q, blocks : 2 * blocks]
    total = jnp.zeros((whole_a.shape[1], whole_z.shape[1]), F32)
    for b in range(blocks):
        total += lax.dot_general(
            whole_a[b], whole_z[b], (((1,), (1,)), ((), ())), preferred_element_type=F32
        )
    nodes = out.shape[3]
    for q in range(out.shape[0]):
        for h in range(out.shape[1]):
            part = total[q * features : (q + 1) * features, h * nodes : (h + 1) * nodes]
            out[q, h] = part.astype(BF16)


def weight_partial(packed, blocks):
    reps, _, features, nodes = packed.shape
    width = reps * features
    return pl.pallas_call(
        weight_kernel,
        out_shape=jax.ShapeDtypeStruct((reps, width // nodes, features, nodes), BF16),
        in_specs=[vmem()],
        out_specs=vmem(),
        scratch_shapes=[pltpu.VMEM((blocks, width, nodes), BF16)] * 2,
        cost_estimate=pl.CostEstimate(
            flops=2 * blocks * nodes * width * width,
            bytes_accessed=4 * blocks * nodes * width + 2 * width * width,
            transcendentals=0,
        ),
    )(packed)


def lay_weight(packed, first, whole):
    features, nodes = packed.shape[2:]
    for q in range(packed.shape[0]):
        for h in range(whole.shape[1] // nodes):
            whole[pl.ds(q * features, features), pl.ds(h * nodes, nodes)] = packed[q, first + h]


def mix_kernel(first, packed, shares, out, weights, whole):
    lay_weight(packed, first, weights)
    reps, blocks, features = shares.shape[:3]
    for q in range(reps):
        whole[:, pl.ds(q * features, features), :] = shares[q]
    for b in range(blocks):
        mixed = jnp.dot(weights[...], whole[b], preferred_element_type=F32)
        for q in range(reps):
            out[q, b] = mixed[q * features : (q + 1) * features].astype(BF16)


def mix(packed, first, shares):
    reps, blocks, features, nodes = shares.shape
    width = reps * features
    return pl.pallas_call(
        functools.partial(mix_kernel, first),
        out_shape=jax.ShapeDtypeStruct(shares.shape, BF16),
        in_specs=[vmem(), vmem()],
        out_specs=vmem(),
        scratch_shapes=[pltpu.VMEM((width, width), BF16), pltpu.VMEM((blocks, width, nodes), BF16)],
        cost_estimate=pl.CostEstimate(
            flops=2 * blocks * nodes * width * width,
            bytes_accessed=4 * blocks * nodes * width,
            transcendentals=0,
        ),
    )(packed, shares)


def mix_apart_kernel(first, reps, where, packed, *rest):
    shares, outs, (weights, whole) = rest[:reps], rest[reps : 2 * reps], rest[2 * reps :]
    lay_weight(packed, first, weights)
    features = shares[0].shape[1]
    blocks = whole.shape[0]
    for s in range(reps):
        rows = pl.multiple_of(lax.rem(where[1] - s + reps, reps) * features, features)
        whole[:, pl.ds(rows, features), :] = shares[s][:blocks]
    for s in range(reps):
        rows = pl.multiple_of(lax.rem(where[1] + s, reps) * features, features)
        part = weights[pl.ds(rows, features), :]
        for b in range(blocks):
            outs[s][b] = jnp.dot(part, whole[b], preferred_element_type=F32).astype(BF16)


def mix_apart(where, packed, first, shares, blocks):
    reps = len(shares)
    _, features, nodes = shares[0].shape
    width = reps * features
    return pl.pallas_call(
        functools.partial(mix_apart_kernel, first, reps),
        out_shape=[jax.ShapeDtypeStruct((blocks, features, nodes), BF16)] * reps,
        in_specs=[smem()] + [vmem()] * (1 + reps),
        out_specs=[vmem()] * reps,
        scratch_shapes=[pltpu.VMEM((width, width), BF16), pltpu.VMEM((blocks, width, nodes), BF16)],
        cost_estimate=pl.CostEstimate(
            flops=2 * blocks * nodes * width * width,
            bytes_accessed=4 * blocks * nodes * width,
            transcendentals=0,
        ),
    )(where, packed, *shares)


def lay_kernel(where, done, *rest):
    shares, out = rest[:-1], rest[-1]
    reps, blocks = len(shares), shares[0].shape[0]
    start = done.shape[0]
    out[:start] = done[...]
    for s in range(reps):
        first = start + lax.rem(where[1] - s + reps, reps) * blocks
        out[pl.ds(first, blocks)] = shares[s][...]


def lay_blocks(where, done, shares, shape):
    return pl.pallas_call(
        lay_kernel,
        out_shape=jax.ShapeDtypeStruct(shape, BF16),
        in_specs=[smem()] + [vmem()] * (1 + len(shares)),
        out_specs=vmem(),
    )(where, done, *shares)


def exchange(value):
    return lax.all_to_all(value, "rep", 0, 0, tiled=True)


def shift(value, steps):
    reps = lax.axis_size("rep")
    if steps % reps == 0:
        return value
    return lax.ppermute(value, "rep", [(i, (i + steps) % reps) for i in range(reps)])


def on_device(cotangent, relu_mask, aggregated, weight, tiles, col_block, live_count):
    blocks, features, nodes = cotangent.shape
    slabs, reps = lax.axis_size("blk"), lax.axis_size("rep")
    width = weight.shape[1]
    pieces = width // nodes
    chunk = blocks // CHUNKS
    share = blocks // reps
    rep = lax.axis_index("rep")
    where = jnp.stack([lax.axis_index("blk"), rep]).astype(jnp.int32)
    cols = jnp.concatenate([col_block, live_count[:, None]], axis=1)

    grad_z = cotangent * relu_mask.astype(BF16)
    by_share = (reps, share, features, nodes)
    weight_pieces = weight.reshape(features, pieces, nodes).transpose(1, 0, 2)
    weight_pieces = jnp.broadcast_to(weight_pieces[None], (reps, pieces, features, nodes))
    packed = jnp.concatenate(
        [grad_z.reshape(by_share), aggregated.reshape(by_share), weight_pieces], axis=1
    )
    packed, grad_z = lax.optimization_barrier((packed, grad_z))
    packed = exchange(packed)

    aside, own, first, second = contributions(where, cols, grad_z, tiles, slabs)

    to_one = [(i, (i + (1 if i % 2 else -1)) % slabs) for i in range(slabs)]
    to_two = [(i, (i + (2 if i % 2 else -2)) % slabs) for i in range(slabs)]

    def add(*terms):
        return sum(term.astype(F32) for term in terms).astype(BF16)

    aside = lax.ppermute(aside, "blk", [(i, i ^ 1) for i in range(slabs)])
    sums = []
    for k in range(CHUNKS):
        span = slice(k * chunk, (k + 1) * chunk)
        two_in = lax.ppermute(second[k], "blk", to_two)
        one_in = lax.ppermute(add(first[k], aside[span]), "blk", to_one)
        sums.append(add(own[span], aside[blocks:][span], one_in, two_in))

    sums[0], packed = lax.optimization_barrier((sums[0], packed))
    part = chunk // reps
    mixed = mix(packed, 2 * share, exchange(sums[0].reshape(reps, part, features, nodes)))
    mixed = exchange(mixed).reshape(chunk, features, nodes)

    grad_w = weight_partial(packed, share)
    both = jnp.concatenate([sums[1].reshape(reps, part, features, nodes), grad_w], axis=1)

    def for_target(s):
        return lax.dynamic_index_in_dim(both, lax.rem(rep + s, reps), 0, keepdims=False)

    shares = [shift(for_target(s), s) for s in range(reps)]
    outs = mix_apart(where, packed, 2 * share, shares, part)
    outs = [shift(out, s) for s, out in enumerate(outs)]

    grad_w = sum(part_in[part:].astype(F32) for part_in in shares)
    step = 1
    while step < slabs:
        grad_w = grad_w + lax.ppermute(grad_w, "blk", [(i, i ^ step) for i in range(slabs)])
        step *= 2
    grad_w = grad_w.transpose(1, 0, 2).reshape(features, width)
    weight_grad = grad_w * (1.0 / math.sqrt(slabs * blocks * nodes))
    return lay_blocks(where, mixed, outs, cotangent.shape), weight_grad


def solution(mesh):
    placed = (
        P("blk", "rep", None),
        P("blk", "rep", None),
        P("blk", "rep", None),
        P("rep", None),
        P("blk", None, None, None),
        P("blk", None),
        P("blk"),
    )
    return jax.shard_map(
        on_device,
        mesh=mesh,
        in_specs=placed,
        out_specs=(P("blk", "rep", None), P("rep", None)),
        check_vma=False,
    )
```

```python
import functools
import math

import jax
import jax.numpy as jnp
from jax import lax
from jax.experimental import pallas as pl
from jax.experimental.pallas import tpu as pltpu
from jax.sharding import PartitionSpec as P

REACH = 2
CHUNKS = 2
STEP = 4
BF16 = jnp.bfloat16
F32 = jnp.float32


def vmem():
    return pl.BlockSpec(memory_space=pltpu.VMEM)


def smem():
    return pl.BlockSpec(memory_space=pltpu.SMEM)


def hbm():
    return pl.BlockSpec(memory_space=pl.ANY)


def tiles_kernel(slabs, where, cols, z_ref, tiles_ref, aside, own_out, *rest):
    leave, (held, total, sems) = rest[:-3], rest[-3:]
    blocks, slots = tiles_ref.shape[:2]
    nodes = z_ref.shape[2]
    window = (2 * REACH + 1) * blocks
    for b in range(blocks):
        pltpu.make_async_copy(tiles_ref.at[b], held.at[b], sems.at[b]).start()

    def clear(i, carry):
        total[i] = jnp.zeros(total.shape[1:], F32)
        return carry

    lax.fori_loop(0, window, clear, 0)
    own = where[0]
    sign = 2 * lax.rem(own, 2) - 1

    def row_block(b):
        pltpu.make_async_copy(tiles_ref.at[b], held.at[b], sems.at[b]).wait()
        z = z_ref[b]
        live = cols[b, slots]
        for s in range(0, slots, 2):
            both = jnp.concatenate([held[b, s], held[b, s + 1]], axis=1)
            terms = jnp.dot(z, both, preferred_element_type=F32)
            for half in range(2):
                col = cols[b, s + half]
                slab = lax.div(col, blocks)
                offset = lax.rem(slab - own + REACH + slabs, slabs) - REACH
                place = (offset * sign + REACH) * blocks + lax.rem(col, blocks)
                place = jnp.where(s + half < live, place, window)
                total[place] += terms[:, half * nodes : (half + 1) * nodes]

    def step(i, carry):
        for b in range(STEP):
            row_block(i * STEP + b)
        return carry

    lax.fori_loop(0, blocks // STEP, step, 0)

    def store(out, base):
        def one(i, carry):
            out[i] = total[base + i].astype(BF16)
            return carry

        lax.fori_loop(0, out.shape[0], one, 0)

    store(aside, 0)
    store(own_out, REACH * blocks)
    chunk = leave[0].shape[0]
    for i, out in enumerate(leave):
        store(out, (REACH + 1) * blocks + i * chunk)


def contributions(where, cols, z, tiles, slabs):
    blocks, features, nodes = z.shape
    chunk = blocks // CHUNKS
    window = (2 * REACH + 1) * blocks
    counts = [REACH * blocks, blocks] + [chunk] * (REACH * CHUNKS)
    aside, own, *leave = pl.pallas_call(
        functools.partial(tiles_kernel, slabs),
        out_shape=[jax.ShapeDtypeStruct((count, features, nodes), BF16) for count in counts],
        in_specs=[smem(), smem(), vmem(), hbm()],
        out_specs=[vmem()] * len(counts),
        scratch_shapes=[
            pltpu.VMEM(tiles.shape, BF16),
            pltpu.VMEM((window + 1, features, nodes), F32),
            pltpu.SemaphoreType.DMA((blocks,)),
        ],
        compiler_params=pltpu.CompilerParams(vmem_limit_bytes=40 << 20),
        cost_estimate=pl.CostEstimate(flops=0, bytes_accessed=0, transcendentals=0),
    )(where, cols, z, tiles)
    return aside, own, leave[:CHUNKS], leave[CHUNKS:]


def weight_kernel(packed, out, whole_z, whole_a):
    blocks, features = whole_z.shape[0], packed.shape[2]
    for q in range(packed.shape[0]):
        rows = pl.ds(q * features, features)
        whole_z[:, rows, :] = packed[q, :blocks]
        whole_a[:, rows, :] = packed[q, blocks : 2 * blocks]
    total = jnp.zeros((whole_a.shape[1], whole_z.shape[1]), F32)
    for b in range(blocks):
        total += lax.dot_general(
            whole_a[b], whole_z[b], (((1,), (1,)), ((), ())), preferred_element_type=F32
        )
    nodes = out.shape[3]
    for q in range(out.shape[0]):
        for h in range(out.shape[1]):
            part = total[q * features : (q + 1) * features, h * nodes : (h + 1) * nodes]
            out[q, h] = part.astype(BF16)


def weight_partial(packed, blocks):
    reps, _, features, nodes = packed.shape
    width = reps * features
    return pl.pallas_call(
        weight_kernel,
        out_shape=jax.ShapeDtypeStruct((reps, width // nodes, features, nodes), BF16),
        in_specs=[vmem()],
        out_specs=vmem(),
        scratch_shapes=[pltpu.VMEM((blocks, width, nodes), BF16)] * 2,
        cost_estimate=pl.CostEstimate(
            flops=2 * blocks * nodes * width * width,
            bytes_accessed=4 * blocks * nodes * width + 2 * width * width,
            transcendentals=0,
        ),
    )(packed)


def lay_weight(packed, first, whole):
    features, nodes = packed.shape[2:]
    for q in range(packed.shape[0]):
        for h in range(whole.shape[1] // nodes):
            whole[pl.ds(q * features, features), pl.ds(h * nodes, nodes)] = packed[q, first + h]


def mix_kernel(first, packed, shares, out, weights, whole):
    lay_weight(packed, first, weights)
    reps, blocks, features = shares.shape[:3]
    for q in range(reps):
        whole[:, pl.ds(q * features, features), :] = shares[q]
    for b in range(blocks):
        mixed = jnp.dot(weights[...], whole[b], preferred_element_type=F32)
        for q in range(reps):
            out[q, b] = mixed[q * features : (q + 1) * features].astype(BF16)


def mix(packed, first, shares):
    reps, blocks, features, nodes = shares.shape
    width = reps * features
    return pl.pallas_call(
        functools.partial(mix_kernel, first),
        out_shape=jax.ShapeDtypeStruct(shares.shape, BF16),
        in_specs=[vmem(), vmem()],
        out_specs=vmem(),
        scratch_shapes=[pltpu.VMEM((width, width), BF16), pltpu.VMEM((blocks, width, nodes), BF16)],
        cost_estimate=pl.CostEstimate(
            flops=2 * blocks * nodes * width * width,
            bytes_accessed=4 * blocks * nodes * width,
            transcendentals=0,
        ),
    )(packed, shares)


def mix_apart_kernel(first, reps, where, packed, *rest):
    shares, outs, (weights, whole) = rest[:reps], rest[reps : 2 * reps], rest[2 * reps :]
    lay_weight(packed, first, weights)
    features = shares[0].shape[1]
    blocks = whole.shape[0]
    for s in range(reps):
        rows = pl.multiple_of(lax.rem(where[1] - s + reps, reps) * features, features)
        whole[:, pl.ds(rows, features), :] = shares[s][:blocks]
    for s in range(reps):
        rows = pl.multiple_of(lax.rem(where[1] + s, reps) * features, features)
        part = weights[pl.ds(rows, features), :]
        for b in range(blocks):
            outs[s][b] = jnp.dot(part, whole[b], preferred_element_type=F32).astype(BF16)


def mix_apart(where, packed, first, shares, blocks):
    reps = len(shares)
    _, features, nodes = shares[0].shape
    width = reps * features
    return pl.pallas_call(
        functools.partial(mix_apart_kernel, first, reps),
        out_shape=[jax.ShapeDtypeStruct((blocks, features, nodes), BF16)] * reps,
        in_specs=[smem()] + [vmem()] * (1 + reps),
        out_specs=[vmem()] * reps,
        scratch_shapes=[pltpu.VMEM((width, width), BF16), pltpu.VMEM((blocks, width, nodes), BF16)],
        cost_estimate=pl.CostEstimate(
            flops=2 * blocks * nodes * width * width,
            bytes_accessed=4 * blocks * nodes * width,
            transcendentals=0,
        ),
    )(where, packed, *shares)


def lay_kernel(where, done, *rest):
    shares, out = rest[:-1], rest[-1]
    reps, blocks = len(shares), shares[0].shape[0]
    start = done.shape[0]
    out[:start] = done[...]
    for s in range(reps):
        first = start + lax.rem(where[1] - s + reps, reps) * blocks
        out[pl.ds(first, blocks)] = shares[s][...]


def lay_blocks(where, done, shares, shape):
    return pl.pallas_call(
        lay_kernel,
        out_shape=jax.ShapeDtypeStruct(shape, BF16),
        in_specs=[smem()] + [vmem()] * (1 + len(shares)),
        out_specs=vmem(),
    )(where, done, *shares)


def exchange(value):
    return lax.all_to_all(value, "rep", 0, 0, tiled=True)


def shift(value, steps):
    reps = lax.axis_size("rep")
    if steps % reps == 0:
        return value
    return lax.ppermute(value, "rep", [(i, (i + steps) % reps) for i in range(reps)])


def on_device(cotangent, relu_mask, aggregated, weight, tiles, col_block, live_count):
    blocks, features, nodes = cotangent.shape
    slabs, reps = lax.axis_size("blk"), lax.axis_size("rep")
    width = weight.shape[1]
    pieces = width // nodes
    chunk = blocks // CHUNKS
    share = blocks // reps
    rep = lax.axis_index("rep")
    where = jnp.stack([lax.axis_index("blk"), rep]).astype(jnp.int32)
    cols = jnp.concatenate([col_block, live_count[:, None]], axis=1)

    grad_z = cotangent * relu_mask.astype(BF16)
    by_share = (reps, share, features, nodes)
    weight_pieces = weight.reshape(features, pieces, nodes).transpose(1, 0, 2)
    weight_pieces = jnp.broadcast_to(weight_pieces[None], (reps, pieces, features, nodes))
    packed = jnp.concatenate(
        [grad_z.reshape(by_share), aggregated.reshape(by_share), weight_pieces], axis=1
    )
    packed, grad_z = lax.optimization_barrier((packed, grad_z))
    packed = exchange(packed)

    aside, own, first, second = contributions(where, cols, grad_z, tiles, slabs)

    to_one = [(i, (i + (1 if i % 2 else -1)) % slabs) for i in range(slabs)]
    to_two = [(i, (i + (2 if i % 2 else -2)) % slabs) for i in range(slabs)]

    def add(*terms):
        return sum(term.astype(F32) for term in terms).astype(BF16)

    aside = lax.ppermute(aside, "blk", [(i, i ^ 1) for i in range(slabs)])
    near, beside = aside[:blocks], aside[blocks:]
    one = [add(first[k], near[k * chunk : (k + 1) * chunk]) for k in range(CHUNKS)]
    one_in, two_in, sums = [], [], []
    for k in range(CHUNKS):
        if k == CHUNKS - 1:
            one[k], second[k], packed = lax.optimization_barrier((one[k], second[k], packed))
        two_in.append(lax.ppermute(second[k], "blk", to_two))
        one_in.append(lax.ppermute(one[k], "blk", to_one))
    for k in range(CHUNKS):
        span = slice(k * chunk, (k + 1) * chunk)
        if k:
            one_in[k], sums[k - 1] = lax.optimization_barrier((one_in[k], sums[k - 1]))
        sums.append(add(own[span], beside[span], one_in[k], two_in[k]))

    part = chunk // reps
    mixed = mix(packed, 2 * share, exchange(sums[0].reshape(reps, part, features, nodes)))
    mixed = exchange(mixed).reshape(chunk, features, nodes)

    grad_w = weight_partial(packed, share)
    both = jnp.concatenate([sums[1].reshape(reps, part, features, nodes), grad_w], axis=1)

    def for_target(s):
        return lax.dynamic_index_in_dim(both, lax.rem(rep + s, reps), 0, keepdims=False)

    shares = [shift(for_target(s), s) for s in range(reps)]
    outs = mix_apart(where, packed, 2 * share, shares, part)
    outs = [shift(out, s) for s, out in enumerate(outs)]

    grad_w = sum(part_in[part:].astype(F32) for part_in in shares)
    step = 1
    while step < slabs:
        grad_w = grad_w + lax.ppermute(grad_w, "blk", [(i, i ^ step) for i in range(slabs)])
        step *= 2
    grad_w = grad_w.transpose(1, 0, 2).reshape(features, width)
    weight_grad = grad_w * (1.0 / math.sqrt(slabs * blocks * nodes))
    return lay_blocks(where, mixed, outs, cotangent.shape), weight_grad


def solution(mesh):
    placed = (
        P("blk", "rep", None),
        P("blk", "rep", None),
        P("blk", "rep", None),
        P("rep", None),
        P("blk", None, None, None),
        P("blk", None),
        P("blk"),
    )
    return jax.shard_map(
        on_device,
        mesh=mesh,
        in_specs=placed,
        out_specs=(P("blk", "rep", None), P("rep", None)),
        check_vma=False,
    )
```

```python
import functools
import math

import jax
import jax.numpy as jnp
from jax import lax
from jax.experimental import pallas as pl
from jax.experimental.pallas import tpu as pltpu
from jax.sharding import PartitionSpec as P

REACH = 2
STEP = 16
BF16 = jnp.bfloat16
F32 = jnp.float32


def vmem():
    return pl.BlockSpec(memory_space=pltpu.VMEM)


def smem():
    return pl.BlockSpec(memory_space=pltpu.SMEM)


def hbm():
    return pl.BlockSpec(memory_space=pl.ANY)


NEAR, LEAVE, STAY = 0, 1, 2
GROUPS = 3


def list_kernel(slabs, where, cols, lists):
    blocks, slots = cols.shape[0], cols.shape[1] - 1
    count = blocks * slots
    own = where[0]
    sign = 2 * lax.rem(own, 2) - 1

    def row_block(b, lengths):
        def slot(s, lengths):
            col = cols[b, s]
            offset = lax.rem(lax.div(col, blocks) - own + REACH + slabs, slabs) - REACH
            order = offset * sign + REACH
            group = jnp.where(order == 0, NEAR, jnp.where(order <= REACH, STAY, LEAVE))
            first = jnp.where(order <= REACH, 1, REACH + 1)
            half = jnp.where(order == 0, 0, order - first)
            place = half * blocks + lax.rem(col, blocks)
            length = jnp.where(group == 0, lengths[0], jnp.where(group == 1, lengths[1], lengths[2]))
            lists[group * count + length] = (b * slots + s) * (2 * blocks) + place
            return tuple(
                length + (group == g).astype(jnp.int32) for g, length in enumerate(lengths)
            )

        return lax.fori_loop(0, cols[b, slots], slot, lengths)

    zero = jnp.int32(0)
    lengths = lax.fori_loop(0, blocks, row_block, (zero,) * GROUPS)
    for g in range(GROUPS):
        lists[GROUPS * count + g] = lengths[g]


def list_tiles(where, cols, slabs):
    count = cols.shape[0] * (cols.shape[1] - 1)
    return pl.pallas_call(
        functools.partial(list_kernel, slabs),
        out_shape=jax.ShapeDtypeStruct((GROUPS * count + 8,), jnp.int32),
        in_specs=[smem(), smem()],
        out_specs=smem(),
    )(where, cols)


def tiles_kernel(group, slots, lists, z_ref, held, *rest):
    outs, totals = rest[:-2], rest[-2:]
    blocks = z_ref.shape[0]
    count = held.shape[0]
    window = len(outs) * blocks

    def clear(i, carry):
        for total in totals:
            total[i] = jnp.zeros(total.shape[1:], F32)
        return carry

    lax.fori_loop(0, window, clear, 0)
    length = lists[GROUPS * count + group]

    def step(i, carry):
        for u in range(STEP):
            k = i * STEP + u
            entry = lists[group * count + jnp.minimum(k, count - 1)]
            entry = jnp.where(k < length, entry, window)
            tile = lax.div(entry, 2 * blocks)
            place = jnp.where(k < length, lax.rem(entry, 2 * blocks), window)
            tile = jnp.where(k < length, tile, 0)
            total = totals[u % 2]
            total[place] += jnp.dot(
                z_ref[lax.div(tile, slots)], held[tile], preferred_element_type=F32
            )
        return carry

    lax.fori_loop(0, lax.div(length + STEP - 1, STEP), step, 0)

    for part, out in enumerate(outs):

        def store(i, carry, out=out, base=part * blocks):
            out[i] = (totals[0][base + i] + totals[1][base + i]).astype(BF16)
            return carry

        lax.fori_loop(0, blocks, store, 0)


def tile_sums(group, lists, z, held, slots):
    blocks, features, nodes = z.shape
    parts = 1 if group == NEAR else 2
    return pl.pallas_call(
        functools.partial(tiles_kernel, group, slots),
        out_shape=[jax.ShapeDtypeStruct(z.shape, BF16)] * parts,
        in_specs=[smem(), vmem(), vmem()],
        out_specs=[vmem()] * parts,
        scratch_shapes=[pltpu.VMEM((parts * blocks + 1, features, nodes), F32)] * 2,
        compiler_params=pltpu.CompilerParams(vmem_limit_bytes=28 << 20),
        cost_estimate=pl.CostEstimate(
            flops=parts * blocks * slots * features * nodes * nodes // 4,
            bytes_accessed=parts * z.size * 4,
            transcendentals=0,
        ),
    )(lists, z, pltpu.with_memory_space_constraint(held, pltpu.VMEM))


def weight_kernel(packed, aggs, out, whole_z, whole_a):
    blocks, features = whole_z.shape[0], packed.shape[2]
    for q in range(packed.shape[0]):
        rows = pl.ds(q * features, features)
        whole_z[:, rows, :] = packed[q, :blocks]
        whole_a[:, rows, :] = aggs[q]
    total = jnp.zeros((whole_a.shape[1], whole_z.shape[1]), F32)
    for b in range(blocks):
        total += lax.dot_general(
            whole_a[b], whole_z[b], (((1,), (1,)), ((), ())), preferred_element_type=F32
        )
    nodes = out.shape[3]
    for q in range(out.shape[0]):
        for h in range(out.shape[1]):
            part = total[q * features : (q + 1) * features, h * nodes : (h + 1) * nodes]
            out[q, h] = part.astype(BF16)


def weight_partial(packed, aggs):
    reps, blocks, features, nodes = aggs.shape
    width = reps * features
    return pl.pallas_call(
        weight_kernel,
        out_shape=jax.ShapeDtypeStruct((reps, width // nodes, features, nodes), BF16),
        in_specs=[vmem(), vmem()],
        out_specs=vmem(),
        scratch_shapes=[pltpu.VMEM((blocks, width, nodes), BF16)] * 2,
        cost_estimate=pl.CostEstimate(
            flops=2 * blocks * nodes * width * width,
            bytes_accessed=4 * blocks * nodes * width + 2 * width * width,
            transcendentals=0,
        ),
    )(packed, aggs)


def mix_kernel(packed, out, weights, whole):
    reps, blocks, features, nodes = out.shape
    for q in range(reps):
        rows = pl.ds(q * features, features)
        for h in range(weights.shape[1] // nodes):
            weights[rows, pl.ds(h * nodes, nodes)] = packed[q, blocks + h]
        whole[:, rows, :] = packed[q, :blocks]
    for b in range(blocks):
        mixed = jnp.dot(weights[...], whole[b], preferred_element_type=F32)
        for q in range(reps):
            out[q, b] = mixed[q * features : (q + 1) * features].astype(BF16)


def mix(packed, blocks):
    reps, _, features, nodes = packed.shape
    width = reps * features
    return pl.pallas_call(
        mix_kernel,
        out_shape=jax.ShapeDtypeStruct((reps, blocks, features, nodes), BF16),
        in_specs=[vmem()],
        out_specs=vmem(),
        scratch_shapes=[pltpu.VMEM((width, width), BF16), pltpu.VMEM((blocks, width, nodes), BF16)],
        cost_estimate=pl.CostEstimate(
            flops=2 * blocks * nodes * width * width,
            bytes_accessed=4 * blocks * nodes * width,
            transcendentals=0,
        ),
    )(packed)


def exchange(value):
    return lax.all_to_all(value, "rep", 0, 0, tiled=True)


def on_device(cotangent, relu_mask, aggregated, weight, tiles, col_block, live_count):
    blocks, features, nodes = cotangent.shape
    slots = tiles.shape[1]
    slabs, reps = lax.axis_size("blk"), lax.axis_size("rep")
    width = weight.shape[1]
    pieces = width // nodes
    share = blocks // reps
    where = lax.axis_index("blk").astype(jnp.int32)[None]
    cols = jnp.concatenate([col_block, live_count[:, None]], axis=1)

    grad_z = cotangent * relu_mask.astype(BF16)
    by_share = (reps, share, features, nodes)
    weight_pieces = weight.reshape(features, pieces, nodes).transpose(1, 0, 2)
    weight_pieces = jnp.broadcast_to(weight_pieces[None], (reps, pieces, features, nodes))
    packed = jnp.concatenate([grad_z.reshape(by_share), weight_pieces], axis=1)
    packed, cols = lax.optimization_barrier((packed, cols))
    packed = exchange(packed)
    lists = list_tiles(where, cols, slabs)
    held = tiles.reshape(blocks * slots, nodes, nodes)
    grad_h = exchange(mix(packed, share)).reshape(blocks, features, nodes)

    pair = [(i, i ^ 1) for i in range(slabs)]
    to_one = [(i, (i + (1 if i % 2 else -1)) % slabs) for i in range(slabs)]
    to_two = [(i, (i + (2 if i % 2 else -2)) % slabs) for i in range(slabs)]

    def add(*terms):
        return sum(term.astype(F32) for term in terms).astype(BF16)

    (near,) = tile_sums(NEAR, lists, grad_h, held, slots)
    near_in = lax.ppermute(near, "blk", pair)
    one, two = tile_sums(LEAVE, lists, grad_h, held, slots)
    one = add(one, near_in)
    two_in = lax.ppermute(two, "blk", to_two)
    one_in = lax.ppermute(one, "blk", to_one)
    beside, own = tile_sums(STAY, lists, grad_h, held, slots)
    beside_in = lax.ppermute(beside, "blk", pair)
    input_grad = add(own, beside_in, one_in, two_in)

    aggs, near = lax.optimization_barrier((aggregated, near))
    grad_w = weight_partial(packed, exchange(aggs.reshape(by_share)))
    grad_w = exchange(grad_w).astype(F32).sum(0)
    step = 1
    while step < slabs:
        grad_w = grad_w + lax.ppermute(grad_w, "blk", [(i, i ^ step) for i in range(slabs)])
        step *= 2
    grad_w = grad_w.transpose(1, 0, 2).reshape(features, width)
    return input_grad, grad_w * (1.0 / math.sqrt(slabs * blocks * nodes))


def solution(mesh):
    placed = (
        P("blk", "rep", None),
        P("blk", "rep", None),
        P("blk", "rep", None),
        P("rep", None),
        P("blk", None, None, None),
        P("blk", None),
        P("blk"),
    )
    return jax.shard_map(
        on_device,
        mesh=mesh,
        in_specs=placed,
        out_specs=(P("blk", "rep", None), P("rep", None)),
        check_vma=False,
    )
```

```python
import functools
import math

import jax
import jax.numpy as jnp
from jax import lax
from jax.experimental import pallas as pl
from jax.experimental.pallas import tpu as pltpu
from jax.sharding import PartitionSpec as P

REACH = 2
STEP = 16
RING = 4
BF16 = jnp.bfloat16
F32 = jnp.float32


def vmem():
    return pl.BlockSpec(memory_space=pltpu.VMEM)


def smem():
    return pl.BlockSpec(memory_space=pltpu.SMEM)


def hbm():
    return pl.BlockSpec(memory_space=pl.ANY)


NEAR, LEAVE, STAY, DEAD = 0, 1, 2, 3


def tile_codes(col_block, live_count, own, slabs):
    blocks, slots = col_block.shape
    sign = 2 * (own % 2) - 1
    offset = (col_block // blocks - own + REACH + slabs) % slabs - REACH
    order = offset * sign + REACH
    group = jnp.where(order == 0, NEAR, jnp.where(order <= REACH, STAY, LEAVE))
    half = jnp.where(order == 0, 0, (order - 1) % 2)
    slot = lax.broadcasted_iota(jnp.int32, (blocks, slots), 1)
    tile = lax.broadcasted_iota(jnp.int32, (blocks, slots), 0) * slots + slot
    group = jnp.where(slot < live_count[:, None], group, DEAD)
    return (group << 16) + tile * (2 * blocks) + half * blocks + col_block % blocks


def list_kernel(codes, lists):
    blocks, slots = codes.shape
    count = blocks * slots

    def row_block(b, lengths):
        for s in range(slots):
            code = codes[b, s]
            group = code >> 16
            length = jnp.where(group == 0, lengths[0], jnp.where(group == 1, lengths[1], lengths[2]))
            length = jnp.where(group == DEAD, 0, length)
            lists[group * count + length] = code & 0xFFFF
            lengths = tuple(
                length + jnp.where(group == g, 1, 0) for g, length in enumerate(lengths)
            )
        return lengths

    lengths = lax.fori_loop(0, blocks, row_block, (jnp.int32(0),) * DEAD)
    for g in range(DEAD):
        lists[(DEAD + 1) * count + g] = lengths[g]


def list_tiles(codes):
    return pl.pallas_call(
        list_kernel,
        out_shape=jax.ShapeDtypeStruct(((DEAD + 1) * codes.size + 8,), jnp.int32),
        in_specs=[smem()],
        out_specs=smem(),
    )(codes)


def tiles_kernel(group, slots, reps, where, lists, *rest):
    shares, tiles, rest = rest[:reps], rest[reps], rest[reps + 1 :]
    outs, (z, ring, first, second, sems) = rest[:-5], rest[-5:]
    totals = (first, second)
    count, blocks = tiles.shape[0], z.shape[0]
    window = len(outs) * blocks
    length = lists[(DEAD + 1) * count + group]
    steps = lax.div(length + STEP - 1, STEP)

    def entry(k):
        return lists[group * count + jnp.minimum(k, count - 1)]

    def fetch(i):
        slot = lax.rem(i, RING)
        for u in range(STEP):
            k = i * STEP + u
            tile = jnp.where(k < length, lax.div(entry(k), 2 * blocks), 0)
            pltpu.make_async_copy(tiles.at[tile], ring.at[slot, u], sems.at[slot]).start()

    for i in range(RING - 1):
        pl.when(i < steps)(functools.partial(fetch, jnp.int32(i)))

    share = blocks // reps
    for s in range(reps):
        source = lax.rem(where[1] - s + reps, reps)
        z[pl.ds(source * share, share)] = shares[s][...]

    def clear(i, carry):
        for total in totals:
            total[i] = jnp.zeros(total.shape[1:], F32)
        return carry

    lax.fori_loop(0, window, clear, 0)

    def step(i, carry):
        slot = lax.rem(i, RING)
        pltpu.make_async_copy(tiles.at[pl.ds(0, STEP)], ring.at[slot], sems.at[slot]).wait()
        pl.when(i + RING - 1 < steps)(functools.partial(fetch, i + RING - 1))
        for u in range(STEP):
            k = i * STEP + u
            code = entry(k)
            row = jnp.where(k < length, lax.div(code, 2 * blocks * slots), 0)
            place = jnp.where(k < length, lax.rem(code, 2 * blocks), window)
            total = totals[u % 2]
            total[place] += jnp.dot(z[row], ring[slot, u], preferred_element_type=F32)
        return carry

    lax.fori_loop(0, steps, step, 0)

    for part, out in enumerate(outs):

        def store(i, carry, out=out, base=part * blocks):
            out[i] = (first[base + i] + second[base + i]).astype(BF16)
            return carry

        lax.fori_loop(0, blocks, store, 0)


def tile_sums(group, where, lists, shares, tiles, slots):
    reps = len(shares)
    share, features, nodes = shares[0].shape
    blocks = share * reps
    parts = 1 if group == NEAR else 2
    shape = (blocks, features, nodes)
    total = pltpu.VMEM((parts * blocks + 1, features, nodes), F32)
    return pl.pallas_call(
        functools.partial(tiles_kernel, group, slots, reps),
        out_shape=[jax.ShapeDtypeStruct(shape, BF16)] * parts,
        in_specs=[smem(), smem()] + [vmem()] * reps + [hbm()],
        out_specs=[vmem()] * parts,
        scratch_shapes=[
            pltpu.VMEM(shape, BF16),
            pltpu.VMEM((RING, STEP, nodes, nodes), BF16),
            total,
            total,
            pltpu.SemaphoreType.DMA((RING,)),
        ],
        compiler_params=pltpu.CompilerParams(vmem_limit_bytes=40 << 20),
        cost_estimate=pl.CostEstimate(
            flops=parts * blocks * slots * features * nodes * nodes // 4,
            bytes_accessed=parts * tiles.size // 4,
            transcendentals=0,
        ),
    )(where, lists, *shares, tiles)


def lay_features(where, shares, whole):
    reps, blocks = len(shares), whole.shape[0]
    features = shares[0].shape[1]
    for s in range(reps):
        first = pl.multiple_of(lax.rem(where[1] - s + reps, reps) * features, features)
        whole[:, pl.ds(first, features), :] = shares[s][:blocks]


def mix_kernel(reps, where, *rest):
    shares, outs, (weights, whole) = rest[:reps], rest[reps : 2 * reps], rest[2 * reps :]
    blocks, features, nodes = outs[0].shape
    lay_features(where, shares, whole)
    for s in range(reps):
        for h in range(weights.shape[1] // nodes):
            rows, columns = pl.ds(s * features, features), pl.ds(h * nodes, nodes)
            weights[rows, columns] = shares[(reps - s) % reps][blocks + h]
    for b in range(blocks):
        mixed = jnp.dot(weights[...], whole[b], preferred_element_type=F32)
        for s in range(reps):
            outs[s][b] = mixed[s * features : (s + 1) * features].astype(BF16)


def mix(where, shares, blocks):
    reps = len(shares)
    _, features, nodes = shares[0].shape
    width = reps * features
    return pl.pallas_call(
        functools.partial(mix_kernel, reps),
        out_shape=[jax.ShapeDtypeStruct((blocks, features, nodes), BF16)] * reps,
        in_specs=[smem()] + [vmem()] * reps,
        out_specs=[vmem()] * reps,
        scratch_shapes=[pltpu.VMEM((width, width), BF16), pltpu.VMEM((blocks, width, nodes), BF16)],
        cost_estimate=pl.CostEstimate(
            flops=2 * blocks * nodes * width * width,
            bytes_accessed=4 * blocks * nodes * width,
            transcendentals=0,
        ),
    )(where, *shares)


def weight_kernel(reps, where, *rest):
    shares, aggs, outs = rest[:reps], rest[reps : 2 * reps], rest[2 * reps : 3 * reps]
    whole, whole_a = rest[3 * reps :]
    lay_features(where, shares, whole)
    blocks, features, nodes = aggs[0].shape
    for s in range(reps):
        whole_a[:, pl.ds(s * features, features), :] = aggs[s][...]
    total = jnp.zeros((whole_a.shape[1], whole.shape[1]), F32)
    for b in range(blocks):
        total += lax.dot_general(
            whole_a[b], whole[b], (((1,), (1,)), ((), ())), preferred_element_type=F32
        )
    for s in range(reps):
        for h in range(outs[s].shape[0]):
            part = total[s * features : (s + 1) * features, h * nodes : (h + 1) * nodes]
            outs[s][h] = part.astype(BF16)


def weight_partial(where, shares, aggs):
    reps = len(aggs)
    blocks, features, nodes = aggs[0].shape
    width = reps * features
    return pl.pallas_call(
        functools.partial(weight_kernel, reps),
        out_shape=[jax.ShapeDtypeStruct((width // nodes, features, nodes), BF16)] * reps,
        in_specs=[smem()] + [vmem()] * (2 * reps),
        out_specs=[vmem()] * reps,
        scratch_shapes=[pltpu.VMEM((blocks, width, nodes), BF16)] * 2,
        cost_estimate=pl.CostEstimate(
            flops=2 * blocks * nodes * width * width,
            bytes_accessed=4 * blocks * nodes * width + 2 * width * width,
            transcendentals=0,
        ),
    )(where, *shares, *aggs)


def add_kernel(*refs):
    terms, out = refs[:-1], refs[-1]

    def one(i, carry):
        total = terms[0][i].astype(F32)
        for term in terms[1:]:
            total += term[i].astype(F32)
        out[i] = total.astype(BF16)
        return carry

    lax.fori_loop(0, out.shape[0], one, 0)


def add(*terms):
    return pl.pallas_call(
        add_kernel,
        out_shape=jax.ShapeDtypeStruct(terms[0].shape, BF16),
        in_specs=[vmem()] * len(terms),
        out_specs=vmem(),
        cost_estimate=pl.CostEstimate(
            flops=len(terms) * terms[0].size,
            bytes_accessed=2 * (len(terms) + 1) * terms[0].size,
            transcendentals=0,
        ),
    )(*terms)


def shift(value, steps):
    reps = lax.axis_size("rep")
    if steps % reps == 0:
        return value
    return lax.ppermute(value, "rep", [(i, (i + steps) % reps) for i in range(reps)])


def node_share(value, steps):
    reps = lax.axis_size("rep")
    blocks = value.shape[0] // reps
    first = lax.rem(lax.axis_index("rep") + steps, reps) * blocks
    return lax.dynamic_slice_in_dim(value, first, blocks, 0)


def on_device(cotangent, relu_mask, aggregated, weight, tiles, col_block, live_count):
    blocks, features, nodes = cotangent.shape
    slots = tiles.shape[1]
    slabs, reps = lax.axis_size("blk"), lax.axis_size("rep")
    width = weight.shape[1]
    share = blocks // reps
    where = jnp.stack([lax.axis_index("blk"), lax.axis_index("rep")]).astype(jnp.int32)

    grad_z = cotangent * relu_mask.astype(BF16)
    weight_pieces = weight.reshape(features, width // nodes, nodes).transpose(1, 0, 2)
    shares = [
        shift(jnp.concatenate([node_share(grad_z, s), weight_pieces], axis=0), s)
        for s in range(reps)
    ]
    lists = list_tiles(tile_codes(col_block, live_count, lax.axis_index("blk"), slabs))
    grad_h = [shift(part, s) for s, part in enumerate(mix(where, shares, share))]

    pair = [(i, i ^ 1) for i in range(slabs)]
    to_one = [(i, (i + (1 if i % 2 else -1)) % slabs) for i in range(slabs)]
    to_two = [(i, (i + (2 if i % 2 else -2)) % slabs) for i in range(slabs)]

    held = tiles.reshape(blocks * slots, nodes, nodes)
    (near,) = tile_sums(NEAR, where, lists, grad_h, held, slots)
    near_in = lax.ppermute(near, "blk", pair)
    one, two = tile_sums(LEAVE, where, lists, grad_h, held, slots)
    two_in = lax.ppermute(two, "blk", to_two)
    one = add(one, near_in)
    one_in = lax.ppermute(one, "blk", to_one)
    stay_lists, _ = lax.optimization_barrier((lists, one))
    beside, own = tile_sums(STAY, where, stay_lists, grad_h, held, slots)
    beside_in = lax.ppermute(beside, "blk", pair)
    input_grad = add(own, beside_in, one_in, two_in)

    aggregated, _ = lax.optimization_barrier((aggregated, near))
    aggs = [shift(node_share(aggregated, s), s) for s in range(reps)]
    aggs, _ = lax.optimization_barrier((aggs, beside))
    grad_w = weight_partial(where, shares, aggs)
    grad_w = sum(shift(part, -s).astype(F32) for s, part in enumerate(grad_w))
    step = 1
    while step < slabs:
        grad_w = grad_w + lax.ppermute(grad_w, "blk", [(i, i ^ step) for i in range(slabs)])
        step *= 2
    grad_w = grad_w.transpose(1, 0, 2).reshape(features, width)
    return input_grad, grad_w * (1.0 / math.sqrt(slabs * blocks * nodes))


def solution(mesh):
    placed = (
        P("blk", "rep", None),
        P("blk", "rep", None),
        P("blk", "rep", None),
        P("rep", None),
        P("blk", None, None, None),
        P("blk", None),
        P("blk"),
    )
    return jax.shard_map(
        on_device,
        mesh=mesh,
        in_specs=placed,
        out_specs=(P("blk", "rep", None), P("rep", None)),
        check_vma=False,
    )
```

```python
import functools
import math

import jax
import jax.numpy as jnp
from jax import lax
from jax.experimental import pallas as pl
from jax.experimental.pallas import tpu as pltpu
from jax.sharding import PartitionSpec as P

REACH = 2
GROUP = 4
STEP = 4
RING = 10
BF16 = jnp.bfloat16
F32 = jnp.float32
MIB = 1 << 20


def vmem():
    return pl.BlockSpec(memory_space=pltpu.VMEM)


def smem():
    return pl.BlockSpec(memory_space=pltpu.SMEM)


def hbm():
    return pl.BlockSpec(memory_space=pl.ANY)


def in_hbm(value):
    return pltpu.with_memory_space_constraint(value, pltpu.HBM)


def wrap(value, size):
    if size & (size - 1):
        return lax.rem(value + size, size)
    return value & (size - 1)


def tiles_kernel(slabs, where, cols, live, cot, mask, tiles, *rest):
    outs, (cot_in, mask_in, z, ring, first, second, rows, left, sems, z_sems) = rest[:5], rest[5:]
    totals = (first, second)
    blocks, slots = cols.shape
    per_row = slots // GROUP
    window = (2 * REACH + 1) * blocks
    copies = [
        pltpu.make_async_copy(cot, cot_in, z_sems.at[0]),
        pltpu.make_async_copy(mask, mask_in, z_sems.at[1]),
    ]
    for copy in copies:
        copy.start()

    def list_row(b, count):
        for g in range(per_row):
            rows[count + g] = b * per_row + g
            left[count + g] = live[b] - g * GROUP
        return count + lax.shift_right_logical(live[b] + GROUP - 1, GROUP.bit_length() - 1)

    count = lax.fori_loop(0, blocks, list_row, jnp.int32(0))
    for u in range(STEP):
        rows[count + u] = 0
        left[count + u] = 0
    steps = lax.div(count + STEP - 1, STEP)

    def fetch(i):
        slot = lax.rem(i, RING)
        for u in range(STEP):
            start = rows[i * STEP + u] * GROUP
            pltpu.make_async_copy(
                tiles.at[pl.ds(start, GROUP)], ring.at[slot, pl.ds(u * GROUP, GROUP)], sems.at[slot]
            ).start()

    for i in range(RING - 1):
        pl.when(i < steps)(functools.partial(fetch, jnp.int32(i)))

    def clear(i, carry):
        for total in totals:
            total[i] = jnp.zeros(total.shape[1:], F32)
        return carry

    lax.fori_loop(0, window, clear, 0)
    for copy in copies:
        copy.wait()

    def mask_row(b, carry):
        z[b] = cot_in[b] * mask_in[b].astype(BF16)
        return carry

    lax.fori_loop(0, blocks, mask_row, 0)
    shift = REACH * blocks - where[0] * blocks

    def step(i, carry):
        slot = lax.rem(i, RING)
        pltpu.make_async_copy(
            tiles.at[pl.ds(0, STEP * GROUP)], ring.at[slot], sems.at[slot]
        ).wait()
        pl.when(i + RING - 1 < steps)(functools.partial(fetch, i + RING - 1))
        for u in range(STEP):
            row, remain = rows[i * STEP + u], left[i * STEP + u]
            b, g = lax.div(row, per_row), lax.rem(row, per_row)
            z_row = z[b]
            for j in range(GROUP):
                place = wrap(cols[b, g * GROUP + j] + shift, slabs * blocks)
                place = jnp.where(j < remain, place, window)
                totals[j % 2][place] += jnp.dot(
                    z_row, ring[slot, u * GROUP + j], preferred_element_type=F32
                )
        return carry

    lax.fori_loop(0, steps, step, 0)
    sign = 2 * lax.rem(where[0], 2) - 1
    for order, out in enumerate(outs):
        base = ((order - REACH) * sign + REACH) * blocks

        def store(i, carry, out=out, base=base):
            out[i] = (first[base + i] + second[base + i]).astype(BF16)
            return carry

        lax.fori_loop(0, blocks, store, 0)


def contributions(where, cols, live, cot, mask, tiles, slabs):
    blocks, slots, nodes = tiles.shape[:3]
    features = cot.shape[1]
    window = (2 * REACH + 1) * blocks
    lists = blocks * (slots // GROUP) + slots // GROUP + STEP
    total = pltpu.VMEM((window + 1, features, nodes), F32)
    return pl.pallas_call(
        functools.partial(tiles_kernel, slabs),
        out_shape=[jax.ShapeDtypeStruct(cot.shape, BF16)] * 5,
        in_specs=[smem(), smem(), smem(), hbm(), hbm(), hbm()],
        out_specs=[vmem()] * 5,
        scratch_shapes=[
            pltpu.VMEM(cot.shape, BF16),
            pltpu.VMEM(mask.shape, jnp.int32),
            pltpu.VMEM(cot.shape, BF16),
            pltpu.VMEM((RING, STEP * GROUP, nodes, nodes), BF16),
            total,
            total,
            pltpu.SMEM((lists,), jnp.int32),
            pltpu.SMEM((lists,), jnp.int32),
            pltpu.SemaphoreType.DMA((RING,)),
            pltpu.SemaphoreType.DMA((2,)),
        ],
        compiler_params=pltpu.CompilerParams(vmem_limit_bytes=26 * MIB),
        cost_estimate=pl.CostEstimate(
            flops=2 * blocks * slots * features * nodes * nodes,
            bytes_accessed=tiles.size * 2,
            transcendentals=0,
        ),
    )(
        where,
        cols,
        live,
        in_hbm(cot),
        in_hbm(mask),
        in_hbm(tiles.reshape(blocks * slots, nodes, nodes)),
    )


def lay_features(where, shares, whole):
    reps, blocks = len(shares), whole.shape[0]
    features = shares[0].shape[1]
    for s in range(reps):
        first = pl.multiple_of(wrap(where[1] - s, reps) * features, features)
        whole[:, pl.ds(first, features), :] = shares[s][:blocks]


def mix_kernel(reps, first, where, *rest):
    shares, packed, outs = rest[:reps], rest[reps : 2 * reps], rest[2 * reps : 3 * reps]
    weights, whole = rest[3 * reps :]
    blocks, features, nodes = outs[0].shape
    lay_features(where, shares, whole)
    for s in range(reps):
        for h in range(weights.shape[1] // nodes):
            rows, columns = pl.ds(s * features, features), pl.ds(h * nodes, nodes)
            weights[rows, columns] = packed[(reps - s) % reps][first + h]
    for b in range(blocks):
        mixed = jnp.dot(weights[...], whole[b], preferred_element_type=F32)
        for s in range(reps):
            outs[s][b] = mixed[s * features : (s + 1) * features].astype(BF16)


def mix(where, shares, packed, first):
    reps = len(shares)
    blocks, features, nodes = shares[0].shape
    width = reps * features
    return pl.pallas_call(
        functools.partial(mix_kernel, reps, first),
        out_shape=[jax.ShapeDtypeStruct((blocks, features, nodes), BF16)] * reps,
        in_specs=[smem()] + [vmem()] * (2 * reps),
        out_specs=[vmem()] * reps,
        scratch_shapes=[pltpu.VMEM((width, width), BF16), pltpu.VMEM((blocks, width, nodes), BF16)],
        compiler_params=pltpu.CompilerParams(vmem_limit_bytes=4 * MIB),
        cost_estimate=pl.CostEstimate(
            flops=2 * blocks * nodes * width * width,
            bytes_accessed=4 * blocks * nodes * width,
            transcendentals=0,
        ),
    )(where, *shares, *packed)


def weight_kernel(reps, blocks, where, *rest):
    packed, outs, (whole_z, whole_a) = rest[:reps], rest[reps : 2 * reps], rest[2 * reps :]
    features, nodes = outs[0].shape[1:]
    lay_features(where, packed, whole_z)
    for s in range(reps):
        whole_a[:, pl.ds(s * features, features), :] = packed[s][blocks : 2 * blocks]
    total = jnp.zeros((whole_a.shape[1], whole_z.shape[1]), F32)
    for b in range(blocks):
        total += lax.dot_general(
            whole_a[b], whole_z[b], (((1,), (1,)), ((), ())), preferred_element_type=F32
        )
    for s in range(reps):
        for h in range(outs[s].shape[0]):
            part = total[s * features : (s + 1) * features, h * nodes : (h + 1) * nodes]
            outs[s][h] = part.astype(BF16)


def weight_partial(where, packed, blocks):
    reps = len(packed)
    _, features, nodes = packed[0].shape
    width = reps * features
    return pl.pallas_call(
        functools.partial(weight_kernel, reps, blocks),
        out_shape=[jax.ShapeDtypeStruct((width // nodes, features, nodes), BF16)] * reps,
        in_specs=[smem()] + [vmem()] * reps,
        out_specs=[vmem()] * reps,
        scratch_shapes=[pltpu.VMEM((blocks, width, nodes), BF16)] * 2,
        compiler_params=pltpu.CompilerParams(vmem_limit_bytes=4 * MIB),
        cost_estimate=pl.CostEstimate(
            flops=2 * blocks * nodes * width * width,
            bytes_accessed=4 * blocks * nodes * width + 2 * width * width,
            transcendentals=0,
        ),
    )(where, *packed)


def add_kernel(one, other, out):
    def row(i, carry):
        out[i] = (one[i].astype(F32) + other[i].astype(F32)).astype(BF16)
        return carry

    lax.fori_loop(0, out.shape[0], row, 0)


def add(one, other):
    return pl.pallas_call(
        add_kernel,
        out_shape=jax.ShapeDtypeStruct(one.shape, BF16),
        in_specs=[vmem()] * 2,
        out_specs=vmem(),
        compiler_params=pltpu.CompilerParams(vmem_limit_bytes=2 * MIB),
        cost_estimate=pl.CostEstimate(
            flops=one.size, bytes_accessed=6 * one.size, transcendentals=0
        ),
    )(one, other)


def total_kernel(reps, where, *rest):
    terms, outs = rest[:-reps], rest[-reps:]
    share = outs[0].shape[0]
    for s, out in enumerate(outs):
        first = wrap(where[1] + s, reps) * share
        for i in range(share):
            total = terms[0][first + i].astype(F32)
            for term in terms[1:]:
                total += term[first + i].astype(F32)
            out[i] = total.astype(BF16)


def total_shares(where, terms, reps):
    blocks, features, nodes = terms[0].shape
    return pl.pallas_call(
        functools.partial(total_kernel, reps),
        out_shape=[jax.ShapeDtypeStruct((blocks // reps, features, nodes), BF16)] * reps,
        in_specs=[smem()] + [vmem()] * len(terms),
        out_specs=[vmem()] * reps,
        compiler_params=pltpu.CompilerParams(vmem_limit_bytes=2 * MIB),
        cost_estimate=pl.CostEstimate(
            flops=4 * terms[0].size, bytes_accessed=10 * terms[0].size, transcendentals=0
        ),
    )(where, *terms)


def lay_kernel(reps, where, *rest):
    shares, out, sems = rest[:reps], rest[reps], rest[reps + 1]
    blocks = shares[0].shape[0]
    copies = []
    for s in range(reps):
        first = wrap(where[1] - s, reps) * blocks
        copies.append(pltpu.make_async_copy(shares[s], out.at[pl.ds(first, blocks)], sems.at[s]))
        copies[s].start()
    for copy in copies:
        copy.wait()


def lay_blocks(where, shares, shape):
    reps = len(shares)
    return pl.pallas_call(
        functools.partial(lay_kernel, reps),
        out_shape=jax.ShapeDtypeStruct(shape, BF16),
        in_specs=[smem()] + [vmem()] * reps,
        out_specs=hbm(),
        scratch_shapes=[pltpu.SemaphoreType.DMA((reps,))],
        compiler_params=pltpu.CompilerParams(vmem_limit_bytes=2 * MIB),
        cost_estimate=pl.CostEstimate(flops=0, bytes_accessed=32 * MIB, transcendentals=0),
    )(where, *shares)


def shift(value, steps):
    reps = lax.axis_size("rep")
    if steps % reps == 0:
        return value
    return lax.ppermute(value, "rep", [(i, (i + steps) % reps) for i in range(reps)])


def node_share(value, steps):
    reps = lax.axis_size("rep")
    blocks = value.shape[0] // reps
    first = lax.rem(lax.axis_index("rep") + steps, reps) * blocks
    return lax.dynamic_slice_in_dim(value, first, blocks, 0)


def on_device(cotangent, relu_mask, aggregated, weight, tiles, col_block, live_count):
    blocks, features, nodes = cotangent.shape
    slabs, reps = lax.axis_size("blk"), lax.axis_size("rep")
    width = weight.shape[1]
    share = blocks // reps
    where = jnp.stack([lax.axis_index("blk"), lax.axis_index("rep")]).astype(jnp.int32)

    pair = [(i, i ^ 1) for i in range(slabs)]
    to_one = [(i, (i + (1 if i % 2 else -1)) % slabs) for i in range(slabs)]
    to_two = [(i, (i + (2 if i % 2 else -2)) % slabs) for i in range(slabs)]
    near, beside, own, one, two = contributions(
        where, col_block, live_count, cotangent, relu_mask, tiles, slabs
    )
    near_in = lax.ppermute(near, "blk", pair)
    two_in = lax.ppermute(two, "blk", to_two)
    one = add(one, near_in)
    one_in = lax.ppermute(one, "blk", to_one)
    beside_in = lax.ppermute(beside, "blk", pair)

    cotangent, relu_mask, aggregated, weight, _ = lax.optimization_barrier(
        (cotangent, relu_mask, aggregated, weight, one)
    )
    grad_z = cotangent * relu_mask.astype(BF16)
    weight_pieces = weight.reshape(features, width // nodes, nodes).transpose(1, 0, 2)
    packed = [
        shift(
            jnp.concatenate([node_share(grad_z, s), node_share(aggregated, s), weight_pieces]), s
        )
        for s in range(reps)
    ]

    shares = total_shares(where, [own, beside_in, one_in, two_in], reps)
    shares = [shift(value, s) for s, value in enumerate(shares)]
    held, _ = lax.optimization_barrier((packed, shares))
    outs = [shift(value, s) for s, value in enumerate(mix(where, shares, packed, 2 * share))]
    input_grad = lay_blocks(where, outs, cotangent.shape)

    grad_w = weight_partial(where, held, share)
    grad_w = sum(shift(part, -s).astype(F32) for s, part in enumerate(grad_w))
    grad_w = grad_w + lax.ppermute(grad_w, "blk", pair)
    grad_w = grad_w + sum(
        lax.ppermute(grad_w, "blk", [(i, i ^ step) for i in range(slabs)])
        for step in range(2, slabs, 2)
    )
    grad_w = grad_w.transpose(1, 0, 2).reshape(features, width)
    return input_grad, grad_w * (1.0 / math.sqrt(slabs * blocks * nodes))


def solution(mesh):
    placed = (
        P("blk", "rep", None),
        P("blk", "rep", None),
        P("blk", "rep", None),
        P("rep", None),
        P("blk", None, None, None),
        P("blk", None),
        P("blk"),
    )
    return jax.shard_map(
        on_device,
        mesh=mesh,
        in_specs=placed,
        out_specs=(P("blk", "rep", None), P("rep", None)),
        check_vma=False,
    )
```

```python
import functools
import math

import jax
import jax.numpy as jnp
from jax import lax
from jax.experimental import pallas as pl
from jax.experimental.pallas import tpu as pltpu
from jax.sharding import PartitionSpec as P

REACH = 2
GROUP = 4
STEP = 4
RING = 10
BF16 = jnp.bfloat16
F32 = jnp.float32
MIB = 1 << 20


def vmem():
    return pl.BlockSpec(memory_space=pltpu.VMEM)


def smem():
    return pl.BlockSpec(memory_space=pltpu.SMEM)


def hbm():
    return pl.BlockSpec(memory_space=pl.ANY)


def in_hbm(value):
    return pltpu.with_memory_space_constraint(value, pltpu.HBM)


def wrap(value, size):
    if size & (size - 1):
        return lax.rem(value + size, size)
    return value & (size - 1)


def tiles_kernel(slabs, reps, where, cols, live, weight, cot, mask, tiles, *rest):
    outs, packed, rest = rest[:5], rest[5 : 5 + reps], rest[5 + reps :]
    cot_in, mask_in, z, ring, first, second, rows, left, sems, z_sems = rest
    totals = (first, second)
    blocks, slots = cols.shape
    per_row = slots // GROUP
    window = (2 * REACH + 1) * blocks
    copies = [
        pltpu.make_async_copy(cot, cot_in, z_sems.at[0]),
        pltpu.make_async_copy(mask, mask_in, z_sems.at[1]),
    ]
    for copy in copies:
        copy.start()

    def list_row(b, count):
        for g in range(per_row):
            rows[count + g] = b * per_row + g
            left[count + g] = live[b] - g * GROUP
        return count + lax.shift_right_logical(live[b] + GROUP - 1, GROUP.bit_length() - 1)

    count = lax.fori_loop(0, blocks, list_row, jnp.int32(0))
    for u in range(STEP):
        rows[count + u] = 0
        left[count + u] = 0
    steps = lax.div(count + STEP - 1, STEP)

    def fetch(i):
        slot = lax.rem(i, RING)
        for u in range(STEP):
            start = rows[i * STEP + u] * GROUP
            pltpu.make_async_copy(
                tiles.at[pl.ds(start, GROUP)], ring.at[slot, pl.ds(u * GROUP, GROUP)], sems.at[slot]
            ).start()

    for i in range(RING - 1):
        pl.when(i < steps)(functools.partial(fetch, jnp.int32(i)))

    def clear(i, carry):
        for total in totals:
            total[pl.ds(i * GROUP, GROUP)] = jnp.zeros((GROUP,) + total.shape[1:], F32)
        return carry

    lax.fori_loop(0, window // GROUP, clear, 0)
    for copy in copies:
        copy.wait()

    def mask_row(b, carry):
        z[b] = cot_in[b] * mask_in[b].astype(BF16)
        return carry

    lax.fori_loop(0, blocks, mask_row, 0)
    nodes = z.shape[2]
    share = blocks // reps
    for s in range(reps):
        packed[s][:share] = z[pl.ds(wrap(where[1] + s, reps) * share, share)]
        for h in range(weight.shape[1] // nodes):
            packed[s][share + h] = weight[:, h * nodes : (h + 1) * nodes]
    shift = REACH * blocks - where[0] * blocks

    def step(i, carry):
        slot = lax.rem(i, RING)
        pltpu.make_async_copy(
            tiles.at[pl.ds(0, STEP * GROUP)], ring.at[slot], sems.at[slot]
        ).wait()
        pl.when(i + RING - 1 < steps)(functools.partial(fetch, i + RING - 1))
        for u in range(STEP):
            row, remain = rows[i * STEP + u], left[i * STEP + u]
            b, g = lax.div(row, per_row), lax.rem(row, per_row)
            z_row = z[b]
            for j in range(GROUP):
                place = wrap(cols[b, g * GROUP + j] + shift, slabs * blocks)
                place = jnp.where(j < remain, place, window)
                totals[j % 2][place] += jnp.dot(
                    z_row, ring[slot, u * GROUP + j], preferred_element_type=F32
                )
        return carry

    lax.fori_loop(0, steps, step, 0)
    sign = 2 * lax.rem(where[0], 2) - 1
    for order, out in enumerate(outs):
        base = ((order - REACH) * sign + REACH) * blocks

        def store(i, carry, out=out, base=base):
            for k in range(GROUP):
                at = i * GROUP + k
                out[at] = (first[base + at] + second[base + at]).astype(BF16)
            return carry

        lax.fori_loop(0, blocks // GROUP, store, 0)


def contributions(where, cols, live, weight, cot, mask, tiles, slabs, reps):
    blocks, slots, nodes = tiles.shape[:3]
    features = cot.shape[1]
    window = (2 * REACH + 1) * blocks
    lists = blocks * (slots // GROUP) + slots // GROUP + STEP
    total = pltpu.VMEM((window + 1, features, nodes), F32)
    packs = blocks // reps + weight.shape[1] // nodes
    return pl.pallas_call(
        functools.partial(tiles_kernel, slabs, reps),
        out_shape=[jax.ShapeDtypeStruct(cot.shape, BF16)] * 5
        + [jax.ShapeDtypeStruct((packs, features, nodes), BF16)] * reps,
        in_specs=[smem(), smem(), smem(), vmem(), hbm(), hbm(), hbm()],
        out_specs=[vmem()] * (5 + reps),
        scratch_shapes=[
            pltpu.VMEM(cot.shape, BF16),
            pltpu.VMEM(mask.shape, jnp.int32),
            pltpu.VMEM(cot.shape, BF16),
            pltpu.VMEM((RING, STEP * GROUP, nodes, nodes), BF16),
            total,
            total,
            pltpu.SMEM((lists,), jnp.int32),
            pltpu.SMEM((lists,), jnp.int32),
            pltpu.SemaphoreType.DMA((RING,)),
            pltpu.SemaphoreType.DMA((2,)),
        ],
        compiler_params=pltpu.CompilerParams(vmem_limit_bytes=26 * MIB),
        cost_estimate=pl.CostEstimate(
            flops=2 * blocks * slots * features * nodes * nodes,
            bytes_accessed=tiles.size * 2,
            transcendentals=0,
        ),
    )(
        where,
        in_hbm(cols),
        in_hbm(live),
        weight,
        in_hbm(cot),
        in_hbm(mask),
        in_hbm(tiles.reshape(blocks * slots, nodes, nodes)),
    )


def lay_features(where, shares, whole):
    reps, blocks = len(shares), whole.shape[0]
    features = shares[0].shape[1]
    for s in range(reps):
        first = pl.multiple_of(wrap(where[1] - s, reps) * features, features)
        whole[:, pl.ds(first, features), :] = shares[s][:blocks]


def mix_kernel(reps, first, where, *rest):
    shares, packed, outs = rest[:reps], rest[reps : 2 * reps], rest[2 * reps : 3 * reps]
    weights, whole = rest[3 * reps :]
    blocks, features, nodes = outs[0].shape
    lay_features(where, shares, whole)
    for s in range(reps):
        for h in range(weights.shape[1] // nodes):
            rows, columns = pl.ds(s * features, features), pl.ds(h * nodes, nodes)
            weights[rows, columns] = packed[(reps - s) % reps][first + h]
    for b in range(blocks):
        mixed = jnp.dot(weights[...], whole[b], preferred_element_type=F32)
        for s in range(reps):
            outs[s][b] = mixed[s * features : (s + 1) * features].astype(BF16)


def mix(where, shares, packed, first):
    reps = len(shares)
    blocks, features, nodes = shares[0].shape
    width = reps * features
    return pl.pallas_call(
        functools.partial(mix_kernel, reps, first),
        out_shape=[jax.ShapeDtypeStruct((blocks, features, nodes), BF16)] * reps,
        in_specs=[smem()] + [vmem()] * (2 * reps),
        out_specs=[vmem()] * reps,
        scratch_shapes=[pltpu.VMEM((width, width), BF16), pltpu.VMEM((blocks, width, nodes), BF16)],
        compiler_params=pltpu.CompilerParams(vmem_limit_bytes=4 * MIB),
        cost_estimate=pl.CostEstimate(
            flops=2 * blocks * nodes * width * width,
            bytes_accessed=4 * blocks * nodes * width,
            transcendentals=0,
        ),
    )(where, *shares, *packed)


def weight_kernel(reps, where, *rest):
    packed, aggs, outs = rest[:reps], rest[reps : 2 * reps], rest[2 * reps : 3 * reps]
    whole_z, whole_a = rest[3 * reps :]
    blocks, features, nodes = aggs[0].shape
    lay_features(where, packed, whole_z)
    for s in range(reps):
        whole_a[:, pl.ds(s * features, features), :] = aggs[s][...]
    total = jnp.zeros((whole_a.shape[1], whole_z.shape[1]), F32)
    for b in range(blocks):
        total += lax.dot_general(
            whole_a[b], whole_z[b], (((1,), (1,)), ((), ())), preferred_element_type=F32
        )
    for s in range(reps):
        for h in range(outs[s].shape[0]):
            part = total[s * features : (s + 1) * features, h * nodes : (h + 1) * nodes]
            outs[s][h] = part.astype(BF16)


def weight_partial(where, packed, aggs):
    reps = len(packed)
    blocks, features, nodes = aggs[0].shape
    width = reps * features
    return pl.pallas_call(
        functools.partial(weight_kernel, reps),
        out_shape=[jax.ShapeDtypeStruct((width // nodes, features, nodes), BF16)] * reps,
        in_specs=[smem()] + [vmem()] * (2 * reps),
        out_specs=[vmem()] * reps,
        scratch_shapes=[pltpu.VMEM((blocks, width, nodes), BF16)] * 2,
        compiler_params=pltpu.CompilerParams(vmem_limit_bytes=4 * MIB),
        cost_estimate=pl.CostEstimate(
            flops=2 * blocks * nodes * width * width,
            bytes_accessed=4 * blocks * nodes * width + 2 * width * width,
            transcendentals=0,
        ),
    )(where, *packed, *aggs)


def add_kernel(one, other, out):
    def row(i, carry):
        out[i] = (one[i].astype(F32) + other[i].astype(F32)).astype(BF16)
        return carry

    lax.fori_loop(0, out.shape[0], row, 0)


def add(one, other):
    return pl.pallas_call(
        add_kernel,
        out_shape=jax.ShapeDtypeStruct(one.shape, BF16),
        in_specs=[vmem()] * 2,
        out_specs=vmem(),
        compiler_params=pltpu.CompilerParams(vmem_limit_bytes=2 * MIB),
        cost_estimate=pl.CostEstimate(
            flops=one.size, bytes_accessed=6 * one.size, transcendentals=0
        ),
    )(one, other)


def total_kernel(reps, where, *rest):
    terms, outs = rest[:-reps], rest[-reps:]
    share = outs[0].shape[0]
    for s, out in enumerate(outs):
        first = wrap(where[1] + s, reps) * share
        for i in range(share):
            total = terms[0][first + i].astype(F32)
            for term in terms[1:]:
                total += term[first + i].astype(F32)
            out[i] = total.astype(BF16)


def total_shares(where, terms, reps):
    blocks, features, nodes = terms[0].shape
    return pl.pallas_call(
        functools.partial(total_kernel, reps),
        out_shape=[jax.ShapeDtypeStruct((blocks // reps, features, nodes), BF16)] * reps,
        in_specs=[smem()] + [vmem()] * len(terms),
        out_specs=[vmem()] * reps,
        compiler_params=pltpu.CompilerParams(vmem_limit_bytes=2 * MIB),
        cost_estimate=pl.CostEstimate(
            flops=4 * terms[0].size, bytes_accessed=10 * terms[0].size, transcendentals=0
        ),
    )(where, *terms)


def lay_kernel(reps, where, *rest):
    shares, out, sems = rest[:reps], rest[reps], rest[reps + 1]
    blocks = shares[0].shape[0]
    copies = []
    for s in range(reps):
        first = wrap(where[1] - s, reps) * blocks
        copies.append(pltpu.make_async_copy(shares[s], out.at[pl.ds(first, blocks)], sems.at[s]))
        copies[s].start()
    for copy in copies:
        copy.wait()


def lay_blocks(where, shares, shape):
    reps = len(shares)
    return pl.pallas_call(
        functools.partial(lay_kernel, reps),
        out_shape=jax.ShapeDtypeStruct(shape, BF16),
        in_specs=[smem()] + [vmem()] * reps,
        out_specs=hbm(),
        scratch_shapes=[pltpu.SemaphoreType.DMA((reps,))],
        compiler_params=pltpu.CompilerParams(vmem_limit_bytes=2 * MIB),
        cost_estimate=pl.CostEstimate(flops=0, bytes_accessed=32 * MIB, transcendentals=0),
    )(where, *shares)


def shift(value, steps):
    reps = lax.axis_size("rep")
    if steps % reps == 0:
        return value
    return lax.ppermute(value, "rep", [(i, (i + steps) % reps) for i in range(reps)])


def node_share(value, steps):
    reps = lax.axis_size("rep")
    blocks = value.shape[0] // reps
    first = lax.rem(lax.axis_index("rep") + steps, reps) * blocks
    return lax.dynamic_slice_in_dim(value, first, blocks, 0)


def on_device(cotangent, relu_mask, aggregated, weight, tiles, col_block, live_count):
    blocks, features, nodes = cotangent.shape
    slabs, reps = lax.axis_size("blk"), lax.axis_size("rep")
    width = weight.shape[1]
    share = blocks // reps
    where = jnp.stack([lax.axis_index("blk"), lax.axis_index("rep")]).astype(jnp.int32)

    pair = [(i, i ^ 1) for i in range(slabs)]
    to_one = [(i, (i + (1 if i % 2 else -1)) % slabs) for i in range(slabs)]
    to_two = [(i, (i + (2 if i % 2 else -2)) % slabs) for i in range(slabs)]
    aggs = [shift(node_share(aggregated, s), s) for s in range(reps)]
    near, beside, own, one, two, *packed = contributions(
        where, col_block, live_count, weight, cotangent, relu_mask, tiles, slabs, reps
    )
    near, aggs = lax.optimization_barrier((near, aggs))
    near_in = lax.ppermute(near, "blk", pair)
    two_in = lax.ppermute(two, "blk", to_two)
    one = add(one, near_in)
    one_in = lax.ppermute(one, "blk", to_one)
    beside_in = lax.ppermute(beside, "blk", pair)

    packed, _ = lax.optimization_barrier((packed, one))
    packed = [shift(value, s) for s, value in enumerate(packed)]
    grad_w = weight_partial(where, packed, aggs)
    grad_w = sum(shift(part, -s).astype(F32) for s, part in enumerate(grad_w))

    own, grad_w = lax.optimization_barrier((own, grad_w))
    shares = total_shares(where, [own, beside_in, one_in, two_in], reps)
    shares = [shift(value, s) for s, value in enumerate(shares)]
    outs = [shift(value, s) for s, value in enumerate(mix(where, shares, packed, share))]
    input_grad = lay_blocks(where, outs, cotangent.shape)

    grad_w = grad_w + lax.ppermute(grad_w, "blk", pair)
    grad_w = grad_w + sum(
        lax.ppermute(grad_w, "blk", [(i, i ^ step) for i in range(slabs)])
        for step in range(2, slabs, 2)
    )
    grad_w = grad_w.transpose(1, 0, 2).reshape(features, width)
    return input_grad, grad_w * (1.0 / math.sqrt(slabs * blocks * nodes))


def solution(mesh):
    placed = (
        P("blk", "rep", None),
        P("blk", "rep", None),
        P("blk", "rep", None),
        P("rep", None),
        P("blk", None, None, None),
        P("blk", None),
        P("blk"),
    )
    return jax.shard_map(
        on_device,
        mesh=mesh,
        in_specs=placed,
        out_specs=(P("blk", "rep", None), P("rep", None)),
        check_vma=False,
    )
```

```python
import functools
import math

import jax
import jax.numpy as jnp
from jax import lax
from jax.experimental import pallas as pl
from jax.experimental.pallas import tpu as pltpu
from jax.sharding import PartitionSpec as P

REACH = 2
GROUP = 4
STEP = 4
BF16 = jnp.bfloat16
F32 = jnp.float32
MIB = 1 << 20


def vmem():
    return pl.BlockSpec(memory_space=pltpu.VMEM)


def smem():
    return pl.BlockSpec(memory_space=pltpu.SMEM)


def hbm():
    return pl.BlockSpec(memory_space=pl.ANY)


def in_hbm(value):
    return pltpu.with_memory_space_constraint(value, pltpu.HBM)


def wrap(value, size):
    if size & (size - 1):
        return lax.rem(value + size, size)
    return value & (size - 1)


def tiles_kernel(slabs, reps, where, cols, live, weight, cot, mask, tiles, *rest):
    outs, packed, rest = rest[:4], rest[4 : 4 + reps], rest[4 + reps :]
    outs = [outs[0].at[pl.ds(0, cols.shape[1])], outs[0].at[pl.ds(cols.shape[1], cols.shape[1])], *outs[1:]]
    cot_in, mask_in, weight_in, z, held, first, second, rows, left, sems, z_sems = rest
    totals = (first, second)
    slots, blocks = cols.shape
    per_row = slots // GROUP
    window = (2 * REACH + 1) * blocks
    copies = [
        pltpu.make_async_copy(cot, cot_in, z_sems.at[0]),
        pltpu.make_async_copy(mask, mask_in, z_sems.at[1]),
        pltpu.make_async_copy(weight, weight_in, z_sems.at[2]),
    ]
    for copy in copies:
        copy.start()

    def groups_of(b):
        return lax.shift_right_logical(live[b] + GROUP - 1, GROUP.bit_length() - 1)

    def fetched(b, act):
        groups = groups_of(b)
        for g in range(1, per_row + 1):

            @pl.when(groups == g)
            def _(span=pl.ds(b * slots, g * GROUP)):
                act(pltpu.make_async_copy(tiles.at[span], held.at[span], sems.at[b]))

    def list_row(b, count):
        fetched(b, lambda copy: copy.start())
        for g in range(per_row):
            rows[count + g] = b * per_row + g
            left[count + g] = live[b] - g * GROUP
        return count + groups_of(b)

    count = lax.fori_loop(0, blocks, list_row, jnp.int32(0))
    for u in range(STEP):
        rows[count + u] = 0
        left[count + u] = 0
    steps = lax.div(count + STEP - 1, STEP)

    def wait_row(b, carry):
        fetched(b, lambda copy: copy.wait())
        return carry

    def clear(i, carry):
        for total in totals:
            total[pl.ds(i * GROUP, GROUP)] = jnp.zeros((GROUP,) + total.shape[1:], F32)
        return carry

    lax.fori_loop(0, window // GROUP, clear, 0)
    for copy in copies:
        copy.wait()

    def mask_row(b, carry):
        z[b] = cot_in[b] * mask_in[b].astype(BF16)
        return carry

    lax.fori_loop(0, blocks, mask_row, 0)
    nodes = z.shape[2]
    share = blocks // reps
    for s in range(reps):
        packed[s][:share] = z[pl.ds(wrap(where[1] + s, reps) * share, share)]
        for h in range(weight.shape[1] // nodes):
            packed[s][share + h] = weight_in[:, h * nodes : (h + 1) * nodes]
    shift = REACH * blocks - where[0] * blocks

    def step(i, ready):
        entries = [rows[i * STEP + u] for u in range(STEP)]
        need = lax.div(functools.reduce(jnp.maximum, entries), per_row) + 1
        lax.fori_loop(ready, need, wait_row, 0)
        for u in range(STEP):
            row, remain = entries[u], left[i * STEP + u]
            b, g = lax.div(row, per_row), lax.rem(row, per_row)
            z_row = z[b]
            for j in range(GROUP):
                place = wrap(cols[g * GROUP + j, b] + shift, slabs * blocks)
                place = jnp.where(j < remain, place, window)
                totals[j % 2][place] += jnp.dot(
                    z_row, held[row * GROUP + j], preferred_element_type=F32
                )
        return jnp.maximum(ready, need)

    ready = lax.fori_loop(0, steps, step, jnp.int32(0))
    lax.fori_loop(ready, blocks, wait_row, 0)
    sign = 2 * lax.rem(where[0], 2) - 1
    for order, out in enumerate(outs):
        base = ((order - REACH) * sign + REACH) * blocks

        def store(i, carry, out=out, base=base):
            for k in range(GROUP):
                at = i * GROUP + k
                out[at] = (first[base + at] + second[base + at]).astype(BF16)
            return carry

        lax.fori_loop(0, blocks // GROUP, store, 0)


def contributions(where, cols, live, weight, cot, mask, tiles, slabs, reps):
    blocks, slots, nodes = tiles.shape[:3]
    features = cot.shape[1]
    window = (2 * REACH + 1) * blocks
    lists = blocks * (slots // GROUP) + slots // GROUP + STEP
    total = pltpu.VMEM((window + 1, features, nodes), F32)
    packs = blocks // reps + weight.shape[1] // nodes
    counts = [2 * blocks, blocks, blocks, blocks]
    return pl.pallas_call(
        functools.partial(tiles_kernel, slabs, reps),
        out_shape=[jax.ShapeDtypeStruct((count, features, nodes), BF16) for count in counts]
        + [jax.ShapeDtypeStruct((packs, features, nodes), BF16)] * reps,
        in_specs=[smem()] * 3 + [hbm()] * 4,
        out_specs=[vmem()] * (len(counts) + reps),
        scratch_shapes=[
            pltpu.VMEM(cot.shape, BF16),
            pltpu.VMEM(mask.shape, jnp.int32),
            pltpu.VMEM(weight.shape, BF16),
            pltpu.VMEM(cot.shape, BF16),
            pltpu.VMEM((blocks * slots, nodes, nodes), BF16),
            total,
            total,
            pltpu.SMEM((lists,), jnp.int32),
            pltpu.SMEM((lists,), jnp.int32),
            pltpu.SemaphoreType.DMA((blocks,)),
            pltpu.SemaphoreType.DMA((3,)),
        ],
        compiler_params=pltpu.CompilerParams(vmem_limit_bytes=36 * MIB),
        cost_estimate=pl.CostEstimate(
            flops=2 * blocks * slots * features * nodes * nodes,
            bytes_accessed=tiles.size * 2,
            transcendentals=0,
        ),
    )(
        where,
        in_hbm(cols.T),
        in_hbm(live),
        in_hbm(weight),
        in_hbm(cot),
        in_hbm(mask),
        in_hbm(tiles.reshape(blocks * slots, nodes, nodes)),
    )


def lay_features(where, shares, whole):
    reps, blocks = len(shares), whole.shape[0]
    features = shares[0].shape[1]
    for s in range(reps):
        first = pl.multiple_of(wrap(where[1] - s, reps) * features, features)
        whole[:, pl.ds(first, features), :] = shares[s][:blocks]


def mix_kernel(reps, first, where, *rest):
    shares, packed, outs = rest[:reps], rest[reps : 2 * reps], rest[2 * reps : 3 * reps]
    weights, whole = rest[3 * reps :]
    blocks, features, nodes = outs[0].shape
    lay_features(where, shares, whole)
    for s in range(reps):
        for h in range(weights.shape[1] // nodes):
            rows, columns = pl.ds(s * features, features), pl.ds(h * nodes, nodes)
            weights[rows, columns] = packed[(reps - s) % reps][first + h]
    for b in range(blocks):
        mixed = jnp.dot(weights[...], whole[b], preferred_element_type=F32)
        for s in range(reps):
            outs[s][b] = mixed[s * features : (s + 1) * features].astype(BF16)


def mix(where, shares, packed, first):
    reps = len(shares)
    blocks, features, nodes = shares[0].shape
    width = reps * features
    return pl.pallas_call(
        functools.partial(mix_kernel, reps, first),
        out_shape=[jax.ShapeDtypeStruct((blocks, features, nodes), BF16)] * reps,
        in_specs=[smem()] + [vmem()] * (2 * reps),
        out_specs=[vmem()] * reps,
        scratch_shapes=[pltpu.VMEM((width, width), BF16), pltpu.VMEM((blocks, width, nodes), BF16)],
        compiler_params=pltpu.CompilerParams(vmem_limit_bytes=4 * MIB),
        cost_estimate=pl.CostEstimate(
            flops=2 * blocks * nodes * width * width,
            bytes_accessed=4 * blocks * nodes * width,
            transcendentals=0,
        ),
    )(where, *shares, *packed)


def weight_kernel(reps, where, *rest):
    packed, aggs, outs = rest[:reps], rest[reps : 2 * reps], rest[2 * reps : 3 * reps]
    whole_z, whole_a = rest[3 * reps :]
    blocks, features, nodes = aggs[0].shape
    lay_features(where, packed, whole_z)
    for s in range(reps):
        whole_a[:, pl.ds(s * features, features), :] = aggs[s][...]
    total = jnp.zeros((whole_a.shape[1], whole_z.shape[1]), F32)
    for b in range(blocks):
        total += lax.dot_general(
            whole_a[b], whole_z[b], (((1,), (1,)), ((), ())), preferred_element_type=F32
        )
    for s in range(reps):
        for h in range(outs[s].shape[0]):
            part = total[s * features : (s + 1) * features, h * nodes : (h + 1) * nodes]
            outs[s][h] = part.astype(BF16)


def weight_partial(where, packed, aggs):
    reps = len(packed)
    blocks, features, nodes = aggs[0].shape
    width = reps * features
    return pl.pallas_call(
        functools.partial(weight_kernel, reps),
        out_shape=[jax.ShapeDtypeStruct((width // nodes, features, nodes), BF16)] * reps,
        in_specs=[smem()] + [vmem()] * (2 * reps),
        out_specs=[vmem()] * reps,
        scratch_shapes=[pltpu.VMEM((blocks, width, nodes), BF16)] * 2,
        compiler_params=pltpu.CompilerParams(vmem_limit_bytes=4 * MIB),
        cost_estimate=pl.CostEstimate(
            flops=2 * blocks * nodes * width * width,
            bytes_accessed=4 * blocks * nodes * width + 2 * width * width,
            transcendentals=0,
        ),
    )(where, *packed, *aggs)


def add_kernel(one, other, out):
    def row(i, carry):
        out[i] = (one[i].astype(F32) + other[i].astype(F32)).astype(BF16)
        return carry

    lax.fori_loop(0, out.shape[0], row, 0)


def add(one, other):
    return pl.pallas_call(
        add_kernel,
        out_shape=jax.ShapeDtypeStruct(one.shape, BF16),
        in_specs=[vmem()] * 2,
        out_specs=vmem(),
        compiler_params=pltpu.CompilerParams(vmem_limit_bytes=2 * MIB),
        cost_estimate=pl.CostEstimate(
            flops=one.size, bytes_accessed=6 * one.size, transcendentals=0
        ),
    )(one, other)


def total_kernel(reps, where, aside, *rest):
    terms, outs = rest[:-reps], rest[-reps:]
    terms = (aside.at[pl.ds(terms[0].shape[0], terms[0].shape[0])], *terms)
    share = outs[0].shape[0]
    for s, out in enumerate(outs):
        first = wrap(where[1] + s, reps) * share
        for i in range(share):
            total = terms[0][first + i].astype(F32)
            for term in terms[1:]:
                total += term[first + i].astype(F32)
            out[i] = total.astype(BF16)


def total_shares(where, aside, terms, reps):
    blocks, features, nodes = terms[0].shape
    return pl.pallas_call(
        functools.partial(total_kernel, reps),
        out_shape=[jax.ShapeDtypeStruct((blocks // reps, features, nodes), BF16)] * reps,
        in_specs=[smem()] + [vmem()] * (1 + len(terms)),
        out_specs=[vmem()] * reps,
        compiler_params=pltpu.CompilerParams(vmem_limit_bytes=2 * MIB),
        cost_estimate=pl.CostEstimate(
            flops=4 * terms[0].size, bytes_accessed=10 * terms[0].size, transcendentals=0
        ),
    )(where, aside, *terms)


def lay_kernel(reps, where, *rest):
    shares, out, sems = rest[:reps], rest[reps], rest[reps + 1]
    blocks = shares[0].shape[0]
    copies = []
    for s in range(reps):
        first = wrap(where[1] - s, reps) * blocks
        copies.append(pltpu.make_async_copy(shares[s], out.at[pl.ds(first, blocks)], sems.at[s]))
        copies[s].start()
    for copy in copies:
        copy.wait()


def lay_blocks(where, shares, shape):
    reps = len(shares)
    return pl.pallas_call(
        functools.partial(lay_kernel, reps),
        out_shape=jax.ShapeDtypeStruct(shape, BF16),
        in_specs=[smem()] + [vmem()] * reps,
        out_specs=hbm(),
        scratch_shapes=[pltpu.SemaphoreType.DMA((reps,))],
        compiler_params=pltpu.CompilerParams(vmem_limit_bytes=2 * MIB),
        cost_estimate=pl.CostEstimate(flops=0, bytes_accessed=32 * MIB, transcendentals=0),
    )(where, *shares)


def shift(value, steps):
    reps = lax.axis_size("rep")
    if steps % reps == 0:
        return value
    return lax.ppermute(value, "rep", [(i, (i + steps) % reps) for i in range(reps)])


def node_share(value, steps):
    reps = lax.axis_size("rep")
    blocks = value.shape[0] // reps
    first = lax.rem(lax.axis_index("rep") + steps, reps) * blocks
    return lax.dynamic_slice_in_dim(value, first, blocks, 0)


def on_device(cotangent, relu_mask, aggregated, weight, tiles, col_block, live_count):
    blocks, features, nodes = cotangent.shape
    slabs, reps = lax.axis_size("blk"), lax.axis_size("rep")
    width = weight.shape[1]
    share = blocks // reps
    where = jnp.stack([lax.axis_index("blk"), lax.axis_index("rep")]).astype(jnp.int32)

    pair = [(i, i ^ 1) for i in range(slabs)]
    to_one = [(i, (i + (1 if i % 2 else -1)) % slabs) for i in range(slabs)]
    to_two = [(i, (i + (2 if i % 2 else -2)) % slabs) for i in range(slabs)]
    aggs = [shift(node_share(aggregated, s), s) for s in range(reps)]
    aside, own, one, two, *packed = contributions(
        where, col_block, live_count, weight, cotangent, relu_mask, tiles, slabs, reps
    )
    aside, aggs = lax.optimization_barrier((aside, aggs))
    aside = lax.ppermute(aside, "blk", pair)
    two_in = lax.ppermute(two, "blk", to_two)
    one = add(one, aside)
    one_in = lax.ppermute(one, "blk", to_one)

    packed, _ = lax.optimization_barrier((packed, one))
    packed = [shift(value, s) for s, value in enumerate(packed)]
    grad_w = weight_partial(where, packed, aggs)

    own, grad_w = lax.optimization_barrier((own, grad_w))
    shares = total_shares(where, aside, [own, one_in, two_in], reps)
    shares = [shift(value, s) for s, value in enumerate(shares)]
    outs = [shift(value, s) for s, value in enumerate(mix(where, shares, packed, share))]
    input_grad = lay_blocks(where, outs, cotangent.shape)

    grad_w = sum(shift(part, -s).astype(F32) for s, part in enumerate(grad_w))
    grad_w = grad_w + lax.ppermute(grad_w, "blk", pair)
    grad_w = grad_w + sum(
        lax.ppermute(grad_w, "blk", [(i, i ^ step) for i in range(slabs)])
        for step in range(2, slabs, 2)
    )
    grad_w = grad_w.transpose(1, 0, 2).reshape(features, width)
    return input_grad, grad_w * (1.0 / math.sqrt(slabs * blocks * nodes))


def solution(mesh):
    placed = (
        P("blk", "rep", None),
        P("blk", "rep", None),
        P("blk", "rep", None),
        P("rep", None),
        P("blk", None, None, None),
        P("blk", None),
        P("blk"),
    )
    return jax.shard_map(
        on_device,
        mesh=mesh,
        in_specs=placed,
        out_specs=(P("blk", "rep", None), P("rep", None)),
        check_vma=False,
    )
```

```python
import functools
import math

import jax
import jax.numpy as jnp
from jax import lax
from jax.experimental import pallas as pl
from jax.experimental.pallas import tpu as pltpu
from jax.sharding import PartitionSpec as P

REACH = 2
GROUP = 4
STEP = 4
CHUNKS = 2
BF16 = jnp.bfloat16
F32 = jnp.float32
MIB = 1 << 20


def vmem():
    return pl.BlockSpec(memory_space=pltpu.VMEM)


def smem():
    return pl.BlockSpec(memory_space=pltpu.SMEM)


def hbm():
    return pl.BlockSpec(memory_space=pl.ANY)


def in_hbm(value):
    return pltpu.with_memory_space_constraint(value, pltpu.HBM)


def wrap(value, size):
    if size & (size - 1):
        return lax.rem(value + size, size)
    return value & (size - 1)


def tiles_kernel(slabs, reps, where, cols, live, weight, cot, mask, tiles, *rest):
    count = 2 + REACH * CHUNKS
    (aside, *outs), packed, rest = rest[:count], rest[count : count + reps], rest[count + reps :]
    cot_in, mask_in, weight_in, z, held, first, second, rows, left, sems, z_sems = rest
    totals = (first, second)
    slots, blocks = cols.shape
    per_row = slots // GROUP
    window = (2 * REACH + 1) * blocks
    copies = [
        pltpu.make_async_copy(cot, cot_in, z_sems.at[0]),
        pltpu.make_async_copy(mask, mask_in, z_sems.at[1]),
        pltpu.make_async_copy(weight, weight_in, z_sems.at[2]),
    ]
    for copy in copies:
        copy.start()

    def groups_of(b):
        return lax.shift_right_logical(live[b] + GROUP - 1, GROUP.bit_length() - 1)

    def fetched(b, act):
        groups = groups_of(b)
        for g in range(1, per_row + 1):

            @pl.when(groups == g)
            def _(span=pl.ds(b * slots, g * GROUP)):
                act(pltpu.make_async_copy(tiles.at[span], held.at[span], sems.at[b]))

    def list_row(b, count):
        fetched(b, lambda copy: copy.start())
        for g in range(per_row):
            rows[count + g] = b * per_row + g
            left[count + g] = live[b] - g * GROUP
        return count + groups_of(b)

    count = lax.fori_loop(0, blocks, list_row, jnp.int32(0))
    for u in range(STEP):
        rows[count + u] = 0
        left[count + u] = 0
    steps = lax.div(count + STEP - 1, STEP)

    def wait_row(b, carry):
        fetched(b, lambda copy: copy.wait())
        return carry

    def clear(i, carry):
        for total in totals:
            total[pl.ds(i * GROUP, GROUP)] = jnp.zeros((GROUP,) + total.shape[1:], F32)
        return carry

    lax.fori_loop(0, window // GROUP, clear, 0)
    for copy in copies:
        copy.wait()

    def mask_row(b, carry):
        z[b] = cot_in[b] * mask_in[b].astype(BF16)
        return carry

    lax.fori_loop(0, blocks, mask_row, 0)
    nodes = z.shape[2]
    share = blocks // reps
    for s in range(reps):
        packed[s][:share] = z[pl.ds(wrap(where[1] + s, reps) * share, share)]
        for h in range(weight.shape[1] // nodes):
            packed[s][share + h] = weight_in[:, h * nodes : (h + 1) * nodes]
    shift = REACH * blocks - where[0] * blocks

    def step(i, ready):
        entries = [rows[i * STEP + u] for u in range(STEP)]
        need = lax.div(functools.reduce(jnp.maximum, entries), per_row) + 1
        lax.fori_loop(ready, need, wait_row, 0)
        for u in range(STEP):
            row, remain = entries[u], left[i * STEP + u]
            b, g = lax.div(row, per_row), lax.rem(row, per_row)
            z_row = z[b]
            for j in range(0, GROUP, 2):
                both = [held[row * GROUP + j], held[row * GROUP + j + 1]]
                terms = jnp.dot(
                    z_row, jnp.concatenate(both, axis=1), preferred_element_type=F32
                )
                for k, total in enumerate(totals):
                    place = wrap(cols[g * GROUP + j + k, b] + shift, slabs * blocks)
                    place = jnp.where(j + k < remain, place, window)
                    total[place] += terms[:, k * nodes : (k + 1) * nodes]
        return jnp.maximum(ready, need)

    ready = lax.fori_loop(0, steps, step, jnp.int32(0))
    lax.fori_loop(ready, blocks, wait_row, 0)
    sign = 2 * lax.rem(where[0], 2) - 1

    def store(out, order, start=0):
        base = ((order - REACH) * sign + REACH) * blocks + start

        def some(i, carry):
            for k in range(GROUP):
                at = i * GROUP + k
                out[at] = (first[base + at] + second[base + at]).astype(BF16)
            return carry

        lax.fori_loop(0, out.shape[0] // GROUP, some, 0)

    for order in range(REACH):
        store(aside.at[pl.ds(order * blocks, blocks)], order)
    store(outs[0], REACH)
    for i, out in enumerate(outs[1:]):
        order, k = divmod(i, CHUNKS)
        store(out, REACH + 1 + order, k * out.shape[0])


def contributions(where, cols, live, weight, cot, mask, tiles, slabs, reps):
    blocks, slots, nodes = tiles.shape[:3]
    features = cot.shape[1]
    window = (2 * REACH + 1) * blocks
    lists = blocks * (slots // GROUP) + slots // GROUP + STEP
    total = pltpu.VMEM((window + 1, features, nodes), F32)
    packs = blocks // reps + weight.shape[1] // nodes
    counts = [REACH * blocks, blocks] + [blocks // CHUNKS] * (REACH * CHUNKS)
    return pl.pallas_call(
        functools.partial(tiles_kernel, slabs, reps),
        out_shape=[jax.ShapeDtypeStruct((count, features, nodes), BF16) for count in counts]
        + [jax.ShapeDtypeStruct((packs, features, nodes), BF16)] * reps,
        in_specs=[smem()] * 3 + [hbm()] * 4,
        out_specs=[vmem()] * (len(counts) + reps),
        scratch_shapes=[
            pltpu.VMEM(cot.shape, BF16),
            pltpu.VMEM(mask.shape, jnp.int32),
            pltpu.VMEM(weight.shape, BF16),
            pltpu.VMEM(cot.shape, BF16),
            pltpu.VMEM((blocks * slots, nodes, nodes), BF16),
            total,
            total,
            pltpu.SMEM((lists,), jnp.int32),
            pltpu.SMEM((lists,), jnp.int32),
            pltpu.SemaphoreType.DMA((blocks,)),
            pltpu.SemaphoreType.DMA((3,)),
        ],
        compiler_params=pltpu.CompilerParams(vmem_limit_bytes=36 * MIB),
        cost_estimate=pl.CostEstimate(
            flops=2 * blocks * slots * features * nodes * nodes,
            bytes_accessed=tiles.size * 2,
            transcendentals=0,
        ),
    )(
        where,
        in_hbm(cols.T),
        in_hbm(live),
        in_hbm(weight),
        in_hbm(cot),
        in_hbm(mask),
        in_hbm(tiles.reshape(blocks * slots, nodes, nodes)),
    )


def lay_features(where, shares, whole):
    reps, blocks = len(shares), whole.shape[0]
    features = shares[0].shape[1]
    for s in range(reps):
        first = pl.multiple_of(wrap(where[1] - s, reps) * features, features)
        whole[:, pl.ds(first, features), :] = shares[s][:blocks]


def mix_kernel(reps, first, where, *rest):
    shares, packed, outs = rest[:reps], rest[reps : 2 * reps], rest[2 * reps : 3 * reps]
    weights, whole = rest[3 * reps :]
    blocks, features, nodes = outs[0].shape
    lay_features(where, shares, whole)
    for s in range(reps):
        for h in range(weights.shape[1] // nodes):
            rows, columns = pl.ds(s * features, features), pl.ds(h * nodes, nodes)
            weights[rows, columns] = packed[(reps - s) % reps][first + h]
    for b in range(blocks):
        mixed = jnp.dot(weights[...], whole[b], preferred_element_type=F32)
        for s in range(reps):
            outs[s][b] = mixed[s * features : (s + 1) * features].astype(BF16)


def mix(where, shares, packed, first):
    reps = len(shares)
    blocks, features, nodes = shares[0].shape
    width = reps * features
    return pl.pallas_call(
        functools.partial(mix_kernel, reps, first),
        out_shape=[jax.ShapeDtypeStruct((blocks, features, nodes), BF16)] * reps,
        in_specs=[smem()] + [vmem()] * (2 * reps),
        out_specs=[vmem()] * reps,
        scratch_shapes=[pltpu.VMEM((width, width), BF16), pltpu.VMEM((blocks, width, nodes), BF16)],
        compiler_params=pltpu.CompilerParams(vmem_limit_bytes=4 * MIB),
        cost_estimate=pl.CostEstimate(
            flops=2 * blocks * nodes * width * width,
            bytes_accessed=4 * blocks * nodes * width,
            transcendentals=0,
        ),
    )(where, *shares, *packed)


def weight_kernel(reps, where, *rest):
    packed, aggs, outs = rest[:reps], rest[reps : 2 * reps], rest[2 * reps : 3 * reps]
    whole_z, whole_a = rest[3 * reps :]
    blocks, features, nodes = aggs[0].shape
    lay_features(where, packed, whole_z)
    for s in range(reps):
        whole_a[:, pl.ds(s * features, features), :] = aggs[s][...]
    total = jnp.zeros((whole_a.shape[1], whole_z.shape[1]), F32)
    for b in range(blocks):
        total += lax.dot_general(
            whole_a[b], whole_z[b], (((1,), (1,)), ((), ())), preferred_element_type=F32
        )
    for s in range(reps):
        for h in range(outs[s].shape[0]):
            part = total[s * features : (s + 1) * features, h * nodes : (h + 1) * nodes]
            outs[s][h] = part.astype(BF16)


def weight_partial(where, packed, aggs):
    reps = len(packed)
    blocks, features, nodes = aggs[0].shape
    width = reps * features
    return pl.pallas_call(
        functools.partial(weight_kernel, reps),
        out_shape=[jax.ShapeDtypeStruct((width // nodes, features, nodes), BF16)] * reps,
        in_specs=[smem()] + [vmem()] * (2 * reps),
        out_specs=[vmem()] * reps,
        scratch_shapes=[pltpu.VMEM((blocks, width, nodes), BF16)] * 2,
        compiler_params=pltpu.CompilerParams(vmem_limit_bytes=4 * MIB),
        cost_estimate=pl.CostEstimate(
            flops=2 * blocks * nodes * width * width,
            bytes_accessed=4 * blocks * nodes * width + 2 * width * width,
            transcendentals=0,
        ),
    )(where, *packed, *aggs)


def add_kernel(other, *refs):
    for part, out in enumerate(refs[CHUNKS:]):
        one, base = refs[part], part * out.shape[0]

        def row(i, carry, one=one, out=out, base=base):
            out[i] = (one[i].astype(F32) + other[base + i].astype(F32)).astype(BF16)
            return carry

        lax.fori_loop(0, out.shape[0], row, 0)


def add(one, aside):
    return pl.pallas_call(
        add_kernel,
        out_shape=[jax.ShapeDtypeStruct(one[0].shape, BF16)] * CHUNKS,
        in_specs=[vmem()] * (1 + CHUNKS),
        out_specs=[vmem()] * CHUNKS,
        compiler_params=pltpu.CompilerParams(vmem_limit_bytes=2 * MIB),
        cost_estimate=pl.CostEstimate(
            flops=aside.size // 2, bytes_accessed=3 * aside.size, transcendentals=0
        ),
    )(aside, *one)


def total_kernel(reps, chunk, where, aside, own, one, two, *outs):
    share = outs[0].shape[0]
    blocks = own.shape[0]
    for s, out in enumerate(outs):
        first = wrap(where[1] + s, reps) * share
        for i in range(share):
            at = chunk * one.shape[0] + first + i
            total = own[at].astype(F32) + aside[blocks + at].astype(F32)
            total += one[first + i].astype(F32) + two[first + i].astype(F32)
            out[i] = total.astype(BF16)


def total_shares(chunk, where, aside, own, one, two, reps):
    blocks, features, nodes = one.shape
    return pl.pallas_call(
        functools.partial(total_kernel, reps, chunk),
        out_shape=[jax.ShapeDtypeStruct((blocks // reps, features, nodes), BF16)] * reps,
        in_specs=[smem()] + [vmem()] * 4,
        out_specs=[vmem()] * reps,
        compiler_params=pltpu.CompilerParams(vmem_limit_bytes=2 * MIB),
        cost_estimate=pl.CostEstimate(
            flops=4 * one.size, bytes_accessed=10 * one.size, transcendentals=0
        ),
    )(where, aside, own, one, two)


def lay_kernel(reps, where, *rest):
    shares, out, sems = rest[:-2], rest[-2], rest[-1]
    blocks = shares[0].shape[0]
    copies = []
    for i, share in enumerate(shares):
        chunk, s = divmod(i, reps)
        first = (chunk * reps + wrap(where[1] - s, reps)) * blocks
        copies.append(pltpu.make_async_copy(share, out.at[pl.ds(first, blocks)], sems.at[i]))
        copies[i].start()
    for copy in copies:
        copy.wait()


def lay_blocks(where, shares, shape):
    reps = len(shares[0])
    shares = [share for chunk in shares for share in chunk]
    return pl.pallas_call(
        functools.partial(lay_kernel, reps),
        out_shape=jax.ShapeDtypeStruct(shape, BF16),
        in_specs=[smem()] + [vmem()] * len(shares),
        out_specs=hbm(),
        scratch_shapes=[pltpu.SemaphoreType.DMA((len(shares),))],
        compiler_params=pltpu.CompilerParams(vmem_limit_bytes=2 * MIB),
        cost_estimate=pl.CostEstimate(flops=0, bytes_accessed=32 * MIB, transcendentals=0),
    )(where, *shares)


def shift(value, steps):
    reps = lax.axis_size("rep")
    if steps % reps == 0:
        return value
    return lax.ppermute(value, "rep", [(i, (i + steps) % reps) for i in range(reps)])


def node_share(value, steps):
    reps = lax.axis_size("rep")
    blocks = value.shape[0] // reps
    first = lax.rem(lax.axis_index("rep") + steps, reps) * blocks
    return lax.dynamic_slice_in_dim(value, first, blocks, 0)


def on_device(cotangent, relu_mask, aggregated, weight, tiles, col_block, live_count):
    blocks, features, nodes = cotangent.shape
    slabs, reps = lax.axis_size("blk"), lax.axis_size("rep")
    width = weight.shape[1]
    share = blocks // reps
    where = jnp.stack([lax.axis_index("blk"), lax.axis_index("rep")]).astype(jnp.int32)

    pair = [(i, i ^ 1) for i in range(slabs)]
    to_one = [(i, (i + (1 if i % 2 else -1)) % slabs) for i in range(slabs)]
    to_two = [(i, (i + (2 if i % 2 else -2)) % slabs) for i in range(slabs)]
    aggs = [shift(node_share(aggregated, s), s) for s in range(reps)]
    aside, own, *rest = contributions(
        where, col_block, live_count, weight, cotangent, relu_mask, tiles, slabs, reps
    )
    one, two, packed = rest[:CHUNKS], rest[CHUNKS : 2 * CHUNKS], rest[2 * CHUNKS :]
    aside, aggs = lax.optimization_barrier((aside, aggs))
    aside = lax.ppermute(aside, "blk", pair)
    one = add(one, aside)
    one_in, two_in = [], []
    for k in range(CHUNKS):
        two_in.append(lax.ppermute(two[k], "blk", to_two))
        one_in.append(lax.ppermute(one[k], "blk", to_one))

    packed, _ = lax.optimization_barrier((packed, one))
    packed = [shift(value, s) for s, value in enumerate(packed)]
    grad_w = weight_partial(where, packed, aggs)

    def exchange(values):
        return [shift(value, s) for s, value in enumerate(values)]

    outs = []
    for k in range(CHUNKS):
        if k:
            own, shares, grad_w = lax.optimization_barrier((own, shares, grad_w))
        sums = total_shares(k, where, aside, own, one_in[k], two_in[k], reps)
        if k:
            outs.append(exchange(mix(where, shares, packed, share)))
        shares = exchange(sums)
    shares, _ = lax.optimization_barrier((shares, outs))
    outs.append(exchange(mix(where, shares, packed, share)))
    input_grad = lay_blocks(where, outs, cotangent.shape)

    grad_w = sum(shift(part, -s).astype(F32) for s, part in enumerate(grad_w))
    grad_w = grad_w + lax.ppermute(grad_w, "blk", pair)
    grad_w = grad_w + sum(
        lax.ppermute(grad_w, "blk", [(i, i ^ step) for i in range(slabs)])
        for step in range(2, slabs, 2)
    )
    grad_w = grad_w.transpose(1, 0, 2).reshape(features, width)
    return input_grad, grad_w * (1.0 / math.sqrt(slabs * blocks * nodes))


def solution(mesh):
    placed = (
        P("blk", "rep", None),
        P("blk", "rep", None),
        P("blk", "rep", None),
        P("rep", None),
        P("blk", None, None, None),
        P("blk", None),
        P("blk"),
    )
    return jax.shard_map(
        on_device,
        mesh=mesh,
        in_specs=placed,
        out_specs=(P("blk", "rep", None), P("rep", None)),
        check_vma=False,
    )
```

```python
import functools
import math

import jax
import jax.numpy as jnp
from jax import lax
from jax.experimental import pallas as pl
from jax.experimental.pallas import tpu as pltpu
from jax.sharding import PartitionSpec as P

REACH = 2
GROUP = 4
STEP = 8
BF16 = jnp.bfloat16
F32 = jnp.float32
MIB = 1 << 20


def vmem():
    return pl.BlockSpec(memory_space=pltpu.VMEM)


def smem():
    return pl.BlockSpec(memory_space=pltpu.SMEM)


def hbm():
    return pl.BlockSpec(memory_space=pl.ANY)


def in_hbm(value):
    return pltpu.with_memory_space_constraint(value, pltpu.HBM)


def wrap(value, size):
    if size & (size - 1):
        return lax.rem(value + size, size)
    return value & (size - 1)


def tiles_kernel(slabs, reps, where, cols, live, cot, mask, tiles, *rest):
    outs, packed, rest = rest[:4], rest[4 : 4 + reps], rest[4 + reps :]
    outs = [outs[0].at[pl.ds(0, cols.shape[1])], outs[0].at[pl.ds(cols.shape[1], cols.shape[1])], *outs[1:]]
    cot_in, mask_in, z, held, total, rows, left, sems, z_sems = rest
    slots, blocks = cols.shape
    per_row = slots // GROUP
    window = (2 * REACH + 1) * blocks
    copies = [
        pltpu.make_async_copy(cot, cot_in, z_sems.at[0]),
        pltpu.make_async_copy(mask, mask_in, z_sems.at[1]),
    ]
    for copy in copies:
        copy.start()

    def groups_of(b):
        return lax.shift_right_logical(live[b] + GROUP - 1, GROUP.bit_length() - 1)

    def fetched(b, act):
        groups = groups_of(b)
        for g in range(1, per_row + 1):

            @pl.when(groups == g)
            def _(span=pl.ds(b * slots, g * GROUP)):
                act(pltpu.make_async_copy(tiles.at[span], held.at[span], sems.at[b]))

    def list_row(b, count):
        fetched(b, lambda copy: copy.start())
        for g in range(per_row):
            rows[count + g] = b * per_row + g
            left[count + g] = live[b] - g * GROUP
        return count + groups_of(b)

    count = lax.fori_loop(0, blocks, list_row, jnp.int32(0))
    for u in range(STEP):
        rows[count + u] = 0
        left[count + u] = 0
    steps = lax.div(count + STEP - 1, STEP)

    def wait_row(b, carry):
        fetched(b, lambda copy: copy.wait())
        return carry

    def clear(i, carry):
        total[pl.ds(i * GROUP, GROUP)] = jnp.zeros((GROUP,) + total.shape[1:], F32)
        return carry

    lax.fori_loop(0, window // GROUP, clear, 0)
    for copy in copies:
        copy.wait()

    def mask_row(b, carry):
        z[b] = cot_in[b] * mask_in[b].astype(BF16)
        return carry

    lax.fori_loop(0, blocks, mask_row, 0)
    share = blocks // reps
    for s in range(reps):
        packed[s][...] = z[pl.ds(wrap(where[1] + s, reps) * share, share)]
    shift = REACH * blocks - where[0] * blocks

    def step(i, ready):
        entries = [rows[i * STEP + u] for u in range(STEP)]
        need = lax.div(functools.reduce(jnp.maximum, entries), per_row) + 1
        lax.fori_loop(ready, need, wait_row, 0)
        for u in range(STEP):
            row, remain = entries[u], left[i * STEP + u]
            b, g = lax.div(row, per_row), lax.rem(row, per_row)
            z_row = z[b]
            for j in range(GROUP):
                place = wrap(cols[g * GROUP + j, b] + shift, slabs * blocks)
                place = jnp.where(j < remain, place, window)
                total[place] += jnp.dot(
                    z_row, held[row * GROUP + j], preferred_element_type=F32
                )
        return jnp.maximum(ready, need)

    ready = lax.fori_loop(0, steps, step, jnp.int32(0))
    lax.fori_loop(ready, blocks, wait_row, 0)
    sign = 2 * lax.rem(where[0], 2) - 1
    for order, out in enumerate(outs):
        base = ((order - REACH) * sign + REACH) * blocks

        def store(i, carry, out=out, base=base):
            for k in range(GROUP):
                at = i * GROUP + k
                out[at] = total[base + at].astype(BF16)
            return carry

        lax.fori_loop(0, blocks // GROUP, store, 0)


def contributions(where, cols, live, cot, mask, tiles, slabs, reps):
    blocks, slots, nodes = tiles.shape[:3]
    features = cot.shape[1]
    window = (2 * REACH + 1) * blocks
    lists = blocks * (slots // GROUP) + slots // GROUP + STEP
    counts = [2 * blocks, blocks, blocks, blocks]
    return pl.pallas_call(
        functools.partial(tiles_kernel, slabs, reps),
        out_shape=[jax.ShapeDtypeStruct((count, features, nodes), BF16) for count in counts]
        + [jax.ShapeDtypeStruct((blocks // reps, features, nodes), BF16)] * reps,
        in_specs=[smem()] * 3 + [hbm()] * 3,
        out_specs=[vmem()] * (len(counts) + reps),
        scratch_shapes=[
            pltpu.VMEM(cot.shape, BF16),
            pltpu.VMEM(mask.shape, jnp.int32),
            pltpu.VMEM(cot.shape, BF16),
            pltpu.VMEM((blocks * slots, nodes, nodes), BF16),
            pltpu.VMEM((window + 1, features, nodes), F32),
            pltpu.SMEM((lists,), jnp.int32),
            pltpu.SMEM((lists,), jnp.int32),
            pltpu.SemaphoreType.DMA((blocks,)),
            pltpu.SemaphoreType.DMA((2,)),
        ],
        compiler_params=pltpu.CompilerParams(vmem_limit_bytes=30 * MIB),
        cost_estimate=pl.CostEstimate(
            flops=2 * blocks * slots * features * nodes * nodes,
            bytes_accessed=tiles.size * 2,
            transcendentals=0,
        ),
    )(
        where,
        in_hbm(cols.T),
        in_hbm(live),
        in_hbm(cot),
        in_hbm(mask),
        in_hbm(tiles.reshape(blocks * slots, nodes, nodes)),
    )


def lay_features(where, shares, whole):
    reps, blocks = len(shares), whole.shape[0]
    features = shares[0].shape[1]
    for s in range(reps):
        first = pl.multiple_of(wrap(where[1] - s, reps) * features, features)
        whole[:, pl.ds(first, features), :] = shares[s][:blocks]


def mix_kernel(reps, first, where, *rest):
    shares, aggs, outs = rest[:reps], rest[reps : 2 * reps], rest[2 * reps : 3 * reps]
    weights, whole = rest[3 * reps :]
    blocks, features, nodes = outs[0].shape
    lay_features(where, shares, whole)
    for s in range(reps):
        for h in range(weights.shape[1] // nodes):
            rows, columns = pl.ds(s * features, features), pl.ds(h * nodes, nodes)
            weights[rows, columns] = aggs[(reps - s) % reps][first + h]
    for b in range(blocks):
        mixed = jnp.dot(weights[...], whole[b], preferred_element_type=F32)
        for s in range(reps):
            outs[s][b] = mixed[s * features : (s + 1) * features].astype(BF16)


def mix(where, shares, aggs):
    reps = len(shares)
    blocks, features, nodes = shares[0].shape
    width = reps * features
    return pl.pallas_call(
        functools.partial(mix_kernel, reps, blocks),
        out_shape=[jax.ShapeDtypeStruct((blocks, features, nodes), BF16)] * reps,
        in_specs=[smem()] + [vmem()] * (2 * reps),
        out_specs=[vmem()] * reps,
        scratch_shapes=[pltpu.VMEM((width, width), BF16), pltpu.VMEM((blocks, width, nodes), BF16)],
        compiler_params=pltpu.CompilerParams(vmem_limit_bytes=4 * MIB),
        cost_estimate=pl.CostEstimate(
            flops=2 * blocks * nodes * width * width,
            bytes_accessed=4 * blocks * nodes * width,
            transcendentals=0,
        ),
    )(where, *shares, *aggs)


def weight_kernel(reps, where, *rest):
    packed, aggs, outs = rest[:reps], rest[reps : 2 * reps], rest[2 * reps : 3 * reps]
    whole_z, whole_a = rest[3 * reps :]
    blocks, features, nodes = packed[0].shape
    lay_features(where, packed, whole_z)
    for s in range(reps):
        whole_a[:, pl.ds(s * features, features), :] = aggs[s][:blocks]
    total = jnp.zeros((whole_a.shape[1], whole_z.shape[1]), F32)
    for b in range(blocks):
        total += lax.dot_general(
            whole_a[b], whole_z[b], (((1,), (1,)), ((), ())), preferred_element_type=F32
        )
    for s in range(reps):
        for h in range(outs[s].shape[0]):
            part = total[s * features : (s + 1) * features, h * nodes : (h + 1) * nodes]
            outs[s][h] = part.astype(BF16)


def weight_partial(where, packed, aggs):
    reps = len(packed)
    blocks, features, nodes = packed[0].shape
    width = reps * features
    return pl.pallas_call(
        functools.partial(weight_kernel, reps),
        out_shape=[jax.ShapeDtypeStruct((width // nodes, features, nodes), BF16)] * reps,
        in_specs=[smem()] + [vmem()] * (2 * reps),
        out_specs=[vmem()] * reps,
        scratch_shapes=[pltpu.VMEM((blocks, width, nodes), BF16)] * 2,
        compiler_params=pltpu.CompilerParams(vmem_limit_bytes=4 * MIB),
        cost_estimate=pl.CostEstimate(
            flops=2 * blocks * nodes * width * width,
            bytes_accessed=4 * blocks * nodes * width + 2 * width * width,
            transcendentals=0,
        ),
    )(where, *packed, *aggs)


def add_kernel(one, other, out):
    def row(i, carry):
        out[i] = (one[i].astype(F32) + other[i].astype(F32)).astype(BF16)
        return carry

    lax.fori_loop(0, out.shape[0], row, 0)


def add(one, other):
    return pl.pallas_call(
        add_kernel,
        out_shape=jax.ShapeDtypeStruct(one.shape, BF16),
        in_specs=[vmem()] * 2,
        out_specs=vmem(),
        compiler_params=pltpu.CompilerParams(vmem_limit_bytes=2 * MIB),
        cost_estimate=pl.CostEstimate(
            flops=one.size, bytes_accessed=6 * one.size, transcendentals=0
        ),
    )(one, other)


def total_kernel(reps, where, aside, *rest):
    terms, outs = rest[:-reps], rest[-reps:]
    terms = (aside.at[pl.ds(terms[0].shape[0], terms[0].shape[0])], *terms)
    share = outs[0].shape[0]
    for s, out in enumerate(outs):
        first = wrap(where[1] + s, reps) * share
        for i in range(share):
            total = terms[0][first + i].astype(F32)
            for term in terms[1:]:
                total += term[first + i].astype(F32)
            out[i] = total.astype(BF16)


def total_shares(where, aside, terms, reps):
    blocks, features, nodes = terms[0].shape
    return pl.pallas_call(
        functools.partial(total_kernel, reps),
        out_shape=[jax.ShapeDtypeStruct((blocks // reps, features, nodes), BF16)] * reps,
        in_specs=[smem()] + [vmem()] * (1 + len(terms)),
        out_specs=[vmem()] * reps,
        compiler_params=pltpu.CompilerParams(vmem_limit_bytes=2 * MIB),
        cost_estimate=pl.CostEstimate(
            flops=4 * terms[0].size, bytes_accessed=10 * terms[0].size, transcendentals=0
        ),
    )(where, aside, *terms)


def pack_kernel(reps, where, agg, weight, *rest):
    outs, sems = rest[:reps], rest[reps]
    features, nodes = agg.shape[1:]
    share = agg.shape[0] // reps
    pieces = weight.shape[1] // nodes
    copies = []
    for s, out in enumerate(outs):
        first = wrap(where[1] + s, reps) * share
        copies.append((agg.at[pl.ds(first, share)], out.at[pl.ds(0, share)]))
        for h in range(pieces):
            copies.append((weight.at[:, pl.ds(h * nodes, nodes)], out.at[share + h]))
    copies = [pltpu.make_async_copy(*ends, sems.at[i]) for i, ends in enumerate(copies)]
    for copy in copies:
        copy.start()
    for copy in copies:
        copy.wait()


def pack(where, agg, weight, reps):
    blocks, features, nodes = agg.shape
    share, pieces = blocks // reps, weight.shape[1] // nodes
    return pl.pallas_call(
        functools.partial(pack_kernel, reps),
        out_shape=[jax.ShapeDtypeStruct((share + pieces, features, nodes), BF16)] * reps,
        in_specs=[smem(), hbm(), hbm()],
        out_specs=[vmem()] * reps,
        scratch_shapes=[pltpu.SemaphoreType.DMA((reps * (1 + pieces),))],
        compiler_params=pltpu.CompilerParams(vmem_limit_bytes=2 * MIB),
    )(where, in_hbm(agg), in_hbm(weight))


def lay_kernel(reps, where, *rest):
    shares, out, sems = rest[:reps], rest[reps], rest[reps + 1]
    blocks = shares[0].shape[0]
    copies = []
    for s in range(reps):
        first = wrap(where[1] - s, reps) * blocks
        copies.append(pltpu.make_async_copy(shares[s], out.at[pl.ds(first, blocks)], sems.at[s]))
        copies[s].start()
    for copy in copies:
        copy.wait()


def lay_blocks(where, shares, shape):
    reps = len(shares)
    return pl.pallas_call(
        functools.partial(lay_kernel, reps),
        out_shape=jax.ShapeDtypeStruct(shape, BF16),
        in_specs=[smem()] + [vmem()] * reps,
        out_specs=hbm(),
        scratch_shapes=[pltpu.SemaphoreType.DMA((reps,))],
        compiler_params=pltpu.CompilerParams(vmem_limit_bytes=2 * MIB),
        cost_estimate=pl.CostEstimate(flops=0, bytes_accessed=32 * MIB, transcendentals=0),
    )(where, *shares)


def shift(value, steps):
    reps = lax.axis_size("rep")
    if steps % reps == 0:
        return value
    return lax.ppermute(value, "rep", [(i, (i + steps) % reps) for i in range(reps)])


def on_device(cotangent, relu_mask, aggregated, weight, tiles, col_block, live_count):
    blocks, features, nodes = cotangent.shape
    slabs, reps = lax.axis_size("blk"), lax.axis_size("rep")
    width = weight.shape[1]
    where = jnp.stack([lax.axis_index("blk"), lax.axis_index("rep")]).astype(jnp.int32)

    pair = [(i, i ^ 1) for i in range(slabs)]
    to_one = [(i, (i + (1 if i % 2 else -1)) % slabs) for i in range(slabs)]
    to_two = [(i, (i + (2 if i % 2 else -2)) % slabs) for i in range(slabs)]
    aggs = [shift(value, s) for s, value in enumerate(pack(where, aggregated, weight, reps))]
    aside, own, one, two, *packed = contributions(
        where, col_block, live_count, cotangent, relu_mask, tiles, slabs, reps
    )
    aside, aggs = lax.optimization_barrier((aside, aggs))
    aside = lax.ppermute(aside, "blk", pair)
    two_in = lax.ppermute(two, "blk", to_two)
    one = add(one, aside)
    one_in = lax.ppermute(one, "blk", to_one)

    packed, _ = lax.optimization_barrier((packed, one))
    packed = [shift(value, s) for s, value in enumerate(packed)]
    grad_w = weight_partial(where, packed, aggs)

    own, grad_w = lax.optimization_barrier((own, grad_w))
    shares = total_shares(where, aside, [own, one_in, two_in], reps)
    shares = [shift(value, s) for s, value in enumerate(shares)]
    outs = [shift(value, s) for s, value in enumerate(mix(where, shares, aggs))]
    input_grad = lay_blocks(where, outs, cotangent.shape)

    grad_w = sum(shift(part, -s).astype(F32) for s, part in enumerate(grad_w))
    grad_w = grad_w + lax.ppermute(grad_w, "blk", pair)
    grad_w = grad_w + sum(
        lax.ppermute(grad_w, "blk", [(i, i ^ step) for i in range(slabs)])
        for step in range(2, slabs, 2)
    )
    grad_w = grad_w.transpose(1, 0, 2).reshape(features, width)
    return input_grad, grad_w * (1.0 / math.sqrt(slabs * blocks * nodes))


def solution(mesh):
    placed = (
        P("blk", "rep", None),
        P("blk", "rep", None),
        P("blk", "rep", None),
        P("rep", None),
        P("blk", None, None, None),
        P("blk", None),
        P("blk"),
    )
    return jax.shard_map(
        on_device,
        mesh=mesh,
        in_specs=placed,
        out_specs=(P("blk", "rep", None), P("rep", None)),
        check_vma=False,
    )
```

```python
import functools
import math

import jax
import jax.numpy as jnp
from jax import lax
from jax.experimental import pallas as pl
from jax.experimental.pallas import tpu as pltpu
from jax.sharding import PartitionSpec as P

REACH = 2
GROUP = 4
STEP = 16
AHEAD = 6
BF16 = jnp.bfloat16
F32 = jnp.float32
MIB = 1 << 20


def vmem():
    return pl.BlockSpec(memory_space=pltpu.VMEM)


def smem():
    return pl.BlockSpec(memory_space=pltpu.SMEM)


def hbm():
    return pl.BlockSpec(memory_space=pl.ANY)


def in_hbm(value):
    return pltpu.with_memory_space_constraint(value, pltpu.HBM)


def wrap(value, size):
    if size & (size - 1):
        return lax.rem(value + size, size)
    return value & (size - 1)


def low_bits(blocks):
    return ((2 * REACH - 1) * blocks).bit_length()


def add_tiles(listed, count, blocks, slots, tiles, z, total, held, sems):
    bits = low_bits(blocks)
    steps = lax.div(count + STEP - 1, STEP)

    def fetch(i):
        for u in range(STEP):
            tile = lax.shift_right_logical(listed[i * STEP + u], bits)
            pltpu.make_async_copy(tiles.at[tile], held.at[i, u], sems.at[i]).start()

    for i in range(AHEAD):
        pl.when(i < steps)(functools.partial(fetch, i))

    def clear(i, carry):
        total[pl.ds(i * GROUP, GROUP)] = jnp.zeros((GROUP,) + total.shape[1:], F32)
        return carry

    lax.fori_loop(0, total.shape[0] // GROUP, clear, 0)

    def step(i, carry):
        pl.when(i + AHEAD < steps)(functools.partial(fetch, i + AHEAD))
        pltpu.make_async_copy(tiles.at[pl.ds(0, STEP)], held.at[i], sems.at[i]).wait()
        for u in range(STEP):
            entry = listed[i * STEP + u]
            row = lax.div(lax.shift_right_logical(entry, bits), slots)
            place = entry & ((1 << bits) - 1)
            total[place] += jnp.dot(z[row], held[i, u], preferred_element_type=F32)
        return carry

    lax.fori_loop(0, steps, step, 0)


def store_sums(out, total, base):
    def some(i, carry):
        for k in range(GROUP):
            at = i * GROUP + k
            out[at] = total[base + at].astype(BF16)
        return carry

    lax.fori_loop(0, out.shape[0] // GROUP, some, 0)


def ends_kernel(slabs, reps, where, cols, live, cot, mask, tiles, weight, *rest):
    (near, two, listed, z), packed, rest = rest[:4], rest[4 : 4 + reps], rest[4 + reps :]
    cot_in, mask_in, weight_in, total, held, mine, sems, z_sems = rest
    slots, blocks = cols.shape
    window = (2 * REACH + 1) * blocks
    bits = low_bits(blocks)
    copies = [
        pltpu.make_async_copy(cot, cot_in, z_sems.at[0]),
        pltpu.make_async_copy(mask, mask_in, z_sems.at[1]),
        pltpu.make_async_copy(weight, weight_in, z_sems.at[2]),
    ]
    for copy in copies:
        copy.start()
    shift = REACH * blocks - where[0] * blocks

    def list_row(b, counts):
        ends, middle = counts
        for s in range(slots):
            place = wrap(cols[s, b] + shift, slabs * blocks)
            first, last = place < blocks, place >= window - blocks
            alive = s < live[b]
            entry = (b * slots + s) << bits
            mine[ends] = entry + jnp.where(last, place - (window - 2 * blocks), place)
            listed[middle] = entry + place - blocks
            is_end = first | last
            ends += jnp.where(alive & is_end, 1, 0)
            middle += jnp.where(alive & jnp.logical_not(is_end), 1, 0)
        return ends, middle

    ends, middle = lax.fori_loop(0, blocks, list_row, (jnp.int32(0), jnp.int32(0)))
    for u in range(STEP):
        mine[ends + u] = 2 * blocks
        listed[middle + u] = window - 2 * blocks
    listed[blocks * slots + STEP] = middle
    for copy in copies:
        copy.wait()

    def mask_row(b, carry):
        z[b] = cot_in[b] * mask_in[b].astype(BF16)
        return carry

    lax.fori_loop(0, blocks, mask_row, 0)
    add_tiles(mine, ends, blocks, slots, tiles, z, total, held, sems)
    odd = lax.rem(where[0], 2)
    store_sums(near, total, (1 - odd) * blocks)
    store_sums(two, total, odd * blocks)
    nodes = z.shape[2]
    share = blocks // reps
    for s in range(reps):
        packed[s][:share] = z[pl.ds(wrap(where[1] + s, reps) * share, share)]
        for h in range(weight_in.shape[1] // nodes):
            packed[s][share + h] = weight_in[:, h * nodes : (h + 1) * nodes]


def held_tiles(count, nodes):
    steps = count // STEP + 1
    return pltpu.VMEM((steps, STEP, nodes, nodes), BF16), pltpu.SemaphoreType.DMA((steps,))


def end_sums(where, cols, live, cot, mask, tiles, weight, slabs, reps):
    slots, blocks = cols.shape
    _, features, nodes = cot.shape
    count = blocks * slots
    lists = count + STEP + 8
    packs = blocks // reps + weight.shape[1] // nodes
    held, sems = held_tiles(count, nodes)
    whole = jax.ShapeDtypeStruct(cot.shape, BF16)
    share = jax.ShapeDtypeStruct((packs, features, nodes), BF16)
    return pl.pallas_call(
        functools.partial(ends_kernel, slabs, reps),
        out_shape=[whole, whole, jax.ShapeDtypeStruct((lists,), jnp.int32), whole] + [share] * reps,
        in_specs=[smem()] * 3 + [hbm()] * 4,
        out_specs=[vmem(), vmem(), smem(), vmem()] + [vmem()] * reps,
        scratch_shapes=[
            pltpu.VMEM(cot.shape, BF16),
            pltpu.VMEM(mask.shape, jnp.int32),
            pltpu.VMEM(weight.shape, BF16),
            pltpu.VMEM((2 * blocks + GROUP, features, nodes), F32),
            held,
            pltpu.SMEM((lists,), jnp.int32),
            sems,
            pltpu.SemaphoreType.DMA((3,)),
        ],
        compiler_params=pltpu.CompilerParams(vmem_limit_bytes=28 * MIB),
        cost_estimate=pl.CostEstimate(
            flops=blocks * slots * features * nodes * nodes,
            bytes_accessed=tiles.size,
            transcendentals=0,
        ),
    )(where, in_hbm(cols), in_hbm(live), in_hbm(cot), in_hbm(mask), in_hbm(tiles), in_hbm(weight))


def middle_kernel(slots, where, listed, z, tiles, beside, own, one, total, held, sems):
    blocks = z.shape[0]
    count = listed[blocks * slots + STEP]
    add_tiles(listed, count, blocks, slots, tiles, z, total, held, sems)
    odd = lax.rem(where[0], 2)
    store_sums(one, total, 2 * odd * blocks)
    store_sums(beside, total, (2 - 2 * odd) * blocks)
    store_sums(own, total, blocks)


def middle_sums(where, listed, z, tiles, slots):
    blocks, features, nodes = z.shape
    held, sems = held_tiles(blocks * slots, nodes)
    return pl.pallas_call(
        functools.partial(middle_kernel, slots),
        out_shape=[jax.ShapeDtypeStruct(z.shape, BF16)] * 3,
        in_specs=[smem(), smem(), vmem(), hbm()],
        out_specs=[vmem()] * 3,
        scratch_shapes=[
            pltpu.VMEM(((2 * REACH - 1) * blocks + GROUP, features, nodes), F32),
            held,
            sems,
        ],
        compiler_params=pltpu.CompilerParams(vmem_limit_bytes=28 * MIB),
        cost_estimate=pl.CostEstimate(
            flops=blocks * slots * features * nodes * nodes,
            bytes_accessed=tiles.size,
            transcendentals=0,
        ),
    )(where, listed, z, in_hbm(tiles))


def lay_features(where, shares, whole):
    reps, blocks = len(shares), whole.shape[0]
    features = shares[0].shape[1]
    for s in range(reps):
        first = pl.multiple_of(wrap(where[1] - s, reps) * features, features)
        whole[:, pl.ds(first, features), :] = shares[s][:blocks]


def mix_kernel(reps, first, where, *rest):
    shares, packed, outs = rest[:reps], rest[reps : 2 * reps], rest[2 * reps : 3 * reps]
    weights, whole = rest[3 * reps :]
    blocks, features, nodes = outs[0].shape
    lay_features(where, shares, whole)
    for s in range(reps):
        for h in range(weights.shape[1] // nodes):
            rows, columns = pl.ds(s * features, features), pl.ds(h * nodes, nodes)
            weights[rows, columns] = packed[(reps - s) % reps][first + h]
    for b in range(blocks):
        mixed = jnp.dot(weights[...], whole[b], preferred_element_type=F32)
        for s in range(reps):
            outs[s][b] = mixed[s * features : (s + 1) * features].astype(BF16)


def mix(where, shares, packed, first):
    reps = len(shares)
    blocks, features, nodes = shares[0].shape
    width = reps * features
    return pl.pallas_call(
        functools.partial(mix_kernel, reps, first),
        out_shape=[jax.ShapeDtypeStruct((blocks, features, nodes), BF16)] * reps,
        in_specs=[smem()] + [vmem()] * (2 * reps),
        out_specs=[vmem()] * reps,
        scratch_shapes=[pltpu.VMEM((width, width), BF16), pltpu.VMEM((blocks, width, nodes), BF16)],
        compiler_params=pltpu.CompilerParams(vmem_limit_bytes=4 * MIB),
        cost_estimate=pl.CostEstimate(
            flops=2 * blocks * nodes * width * width,
            bytes_accessed=4 * blocks * nodes * width,
            transcendentals=0,
        ),
    )(where, *shares, *packed)


def weight_kernel(reps, where, *rest):
    packed, aggs, outs = rest[:reps], rest[reps : 2 * reps], rest[2 * reps : 3 * reps]
    whole_z, whole_a = rest[3 * reps :]
    blocks, features, nodes = aggs[0].shape
    lay_features(where, packed, whole_z)
    for s in range(reps):
        whole_a[:, pl.ds(s * features, features), :] = aggs[s][...]
    total = jnp.zeros((whole_a.shape[1], whole_z.shape[1]), F32)
    for b in range(blocks):
        total += lax.dot_general(
            whole_a[b], whole_z[b], (((1,), (1,)), ((), ())), preferred_element_type=F32
        )
    for s in range(reps):
        for h in range(outs[s].shape[0]):
            part = total[s * features : (s + 1) * features, h * nodes : (h + 1) * nodes]
            outs[s][h] = part.astype(BF16)


def weight_partial(where, packed, aggs):
    reps = len(packed)
    blocks, features, nodes = aggs[0].shape
    width = reps * features
    return pl.pallas_call(
        functools.partial(weight_kernel, reps),
        out_shape=[jax.ShapeDtypeStruct((width // nodes, features, nodes), BF16)] * reps,
        in_specs=[smem()] + [vmem()] * (2 * reps),
        out_specs=[vmem()] * reps,
        scratch_shapes=[pltpu.VMEM((blocks, width, nodes), BF16)] * 2,
        compiler_params=pltpu.CompilerParams(vmem_limit_bytes=4 * MIB),
        cost_estimate=pl.CostEstimate(
            flops=2 * blocks * nodes * width * width,
            bytes_accessed=4 * blocks * nodes * width + 2 * width * width,
            transcendentals=0,
        ),
    )(where, *packed, *aggs)


def add_kernel(one, other, out):
    def row(i, carry):
        out[i] = (one[i].astype(F32) + other[i].astype(F32)).astype(BF16)
        return carry

    lax.fori_loop(0, out.shape[0], row, 0)


def add(one, other):
    return pl.pallas_call(
        add_kernel,
        out_shape=jax.ShapeDtypeStruct(one.shape, BF16),
        in_specs=[vmem()] * 2,
        out_specs=vmem(),
        compiler_params=pltpu.CompilerParams(vmem_limit_bytes=2 * MIB),
        cost_estimate=pl.CostEstimate(
            flops=one.size, bytes_accessed=6 * one.size, transcendentals=0
        ),
    )(one, other)


def total_kernel(reps, where, *rest):
    terms, outs = rest[:-reps], rest[-reps:]
    share = outs[0].shape[0]
    for s, out in enumerate(outs):
        first = wrap(where[1] + s, reps) * share
        for i in range(share):
            total = terms[0][first + i].astype(F32)
            for term in terms[1:]:
                total += term[first + i].astype(F32)
            out[i] = total.astype(BF16)


def total_shares(where, terms, reps):
    blocks, features, nodes = terms[0].shape
    return pl.pallas_call(
        functools.partial(total_kernel, reps),
        out_shape=[jax.ShapeDtypeStruct((blocks // reps, features, nodes), BF16)] * reps,
        in_specs=[smem()] + [vmem()] * len(terms),
        out_specs=[vmem()] * reps,
        compiler_params=pltpu.CompilerParams(vmem_limit_bytes=2 * MIB),
        cost_estimate=pl.CostEstimate(
            flops=4 * terms[0].size, bytes_accessed=10 * terms[0].size, transcendentals=0
        ),
    )(where, *terms)


def lay_kernel(reps, where, *rest):
    shares, out, sems = rest[:reps], rest[reps], rest[reps + 1]
    blocks = shares[0].shape[0]
    copies = []
    for s in range(reps):
        first = wrap(where[1] - s, reps) * blocks
        copies.append(pltpu.make_async_copy(shares[s], out.at[pl.ds(first, blocks)], sems.at[s]))
        copies[s].start()
    for copy in copies:
        copy.wait()


def lay_blocks(where, shares, shape):
    reps = len(shares)
    return pl.pallas_call(
        functools.partial(lay_kernel, reps),
        out_shape=jax.ShapeDtypeStruct(shape, BF16),
        in_specs=[smem()] + [vmem()] * reps,
        out_specs=hbm(),
        scratch_shapes=[pltpu.SemaphoreType.DMA((reps,))],
        compiler_params=pltpu.CompilerParams(vmem_limit_bytes=2 * MIB),
        cost_estimate=pl.CostEstimate(flops=0, bytes_accessed=32 * MIB, transcendentals=0),
    )(where, *shares)


def shift(value, steps):
    reps = lax.axis_size("rep")
    if steps % reps == 0:
        return value
    return lax.ppermute(value, "rep", [(i, (i + steps) % reps) for i in range(reps)])


def node_share(value, steps):
    reps = lax.axis_size("rep")
    blocks = value.shape[0] // reps
    first = lax.rem(lax.axis_index("rep") + steps, reps) * blocks
    return lax.dynamic_slice_in_dim(value, first, blocks, 0)


def on_device(cotangent, relu_mask, aggregated, weight, tiles, col_block, live_count):
    blocks, features, nodes = cotangent.shape
    slabs, reps = lax.axis_size("blk"), lax.axis_size("rep")
    width = weight.shape[1]
    share = blocks // reps
    where = jnp.stack([lax.axis_index("blk"), lax.axis_index("rep")]).astype(jnp.int32)

    pair = [(i, i ^ 1) for i in range(slabs)]
    to_one = [(i, (i + (1 if i % 2 else -1)) % slabs) for i in range(slabs)]
    to_two = [(i, (i + (2 if i % 2 else -2)) % slabs) for i in range(slabs)]
    slots = tiles.shape[1]
    tiles = tiles.reshape(blocks * slots, nodes, nodes)
    near, two, listed, grad_z, *packed = end_sums(
        where, col_block.T, live_count, cotangent, relu_mask, tiles, weight, slabs, reps
    )
    near_in = lax.ppermute(near, "blk", pair)
    two_in = lax.ppermute(two, "blk", to_two)
    aggregated, _ = lax.optimization_barrier((aggregated, near))
    aggs = [shift(node_share(aggregated, s), s) for s in range(reps)]

    beside, own, one = middle_sums(where, listed, grad_z, tiles, slots)
    one, aggs = lax.optimization_barrier((one, aggs))
    one = add(one, near_in)
    one_in = lax.ppermute(one, "blk", to_one)
    beside_in = lax.ppermute(beside, "blk", pair)
    packed, _ = lax.optimization_barrier((packed, (one, two_in)))
    packed = [shift(value, s) for s, value in enumerate(packed)]

    shares = total_shares(where, [own, beside_in, one_in, two_in], reps)
    shares = [shift(value, s) for s, value in enumerate(shares)]
    outs = [shift(value, s) for s, value in enumerate(mix(where, shares, packed, share))]
    input_grad = lay_blocks(where, outs, cotangent.shape)

    grad_w = weight_partial(where, packed, aggs)
    grad_w = sum(shift(part, -s).astype(F32) for s, part in enumerate(grad_w))
    grad_w = grad_w + lax.ppermute(grad_w, "blk", pair)
    parts = [
        lax.ppermute(grad_w, "blk", [(i, i ^ step) for i in range(slabs)])
        for step in range(2, slabs, 2)
    ]
    parts, _ = lax.optimization_barrier((parts, input_grad))
    grad_w = grad_w + sum(parts)
    grad_w = grad_w.transpose(1, 0, 2).reshape(features, width)
    return input_grad, grad_w * (1.0 / math.sqrt(slabs * blocks * nodes))


def solution(mesh):
    placed = (
        P("blk", "rep", None),
        P("blk", "rep", None),
        P("blk", "rep", None),
        P("rep", None),
        P("blk", None, None, None),
        P("blk", None),
        P("blk"),
    )
    return jax.shard_map(
        on_device,
        mesh=mesh,
        in_specs=placed,
        out_specs=(P("blk", "rep", None), P("rep", None)),
        check_vma=False,
    )
```

```python
import functools
import math

import jax
import jax.numpy as jnp
from jax import lax
from jax.experimental import pallas as pl
from jax.experimental.pallas import tpu as pltpu
from jax.sharding import PartitionSpec as P

REACH = 2
GROUP = 4
STEP = 8
BF16 = jnp.bfloat16
F32 = jnp.float32
MIB = 1 << 20


def vmem():
    return pl.BlockSpec(memory_space=pltpu.VMEM)


def smem():
    return pl.BlockSpec(memory_space=pltpu.SMEM)


def hbm():
    return pl.BlockSpec(memory_space=pl.ANY)


def in_hbm(value):
    return pltpu.with_memory_space_constraint(value, pltpu.HBM)


def wrap(value, size):
    if size & (size - 1):
        return lax.rem(value + size, size)
    return value & (size - 1)


def tiles_kernel(slabs, reps, where, cols, live, cot, mask, tiles, *rest):
    outs, packed, rest = rest[:4], rest[4 : 4 + reps], rest[4 + reps :]
    outs = [outs[0].at[pl.ds(0, cols.shape[1])], outs[0].at[pl.ds(cols.shape[1], cols.shape[1])], *outs[1:]]
    cot_in, mask_in, z, held, total, rows, left, sems, z_sems = rest
    slots, blocks = cols.shape
    per_row = slots // GROUP
    window = (2 * REACH + 1) * blocks
    copies = [
        pltpu.make_async_copy(cot, cot_in, z_sems.at[0]),
        pltpu.make_async_copy(mask, mask_in, z_sems.at[1]),
    ]
    for copy in copies:
        copy.start()

    def groups_of(b):
        return lax.shift_right_logical(live[b] + GROUP - 1, GROUP.bit_length() - 1)

    def fetched(b, act):
        groups = groups_of(b)
        for g in range(1, per_row + 1):

            @pl.when(groups == g)
            def _(span=pl.ds(b * slots, g * GROUP)):
                act(pltpu.make_async_copy(tiles.at[span], held.at[span], sems.at[b]))

    def list_row(b, count):
        fetched(b, lambda copy: copy.start())
        for g in range(per_row):
            rows[count + g] = b * per_row + g
            left[count + g] = live[b] - g * GROUP
        return count + groups_of(b)

    count = lax.fori_loop(0, blocks, list_row, jnp.int32(0))
    for u in range(STEP):
        rows[count + u] = 0
        left[count + u] = 0
    steps = lax.div(count + STEP - 1, STEP)

    def wait_row(b, carry):
        fetched(b, lambda copy: copy.wait())
        return carry

    def clear(i, carry):
        total[pl.ds(i * GROUP, GROUP)] = jnp.zeros((GROUP,) + total.shape[1:], F32)
        return carry

    lax.fori_loop(0, window // GROUP, clear, 0)
    for copy in copies:
        copy.wait()

    def mask_row(b, carry):
        z[b] = cot_in[b] * mask_in[b].astype(BF16)
        return carry

    lax.fori_loop(0, blocks, mask_row, 0)
    share = blocks // reps
    for s in range(reps):
        packed[s][...] = z[pl.ds(wrap(where[1] + s, reps) * share, share)]
    shift = REACH * blocks - where[0] * blocks

    def step(i, ready):
        entries = [rows[i * STEP + u] for u in range(STEP)]
        need = lax.div(functools.reduce(jnp.maximum, entries), per_row) + 1
        lax.fori_loop(ready, need, wait_row, 0)
        for u in range(STEP):
            row, remain = entries[u], left[i * STEP + u]
            b, g = lax.div(row, per_row), lax.rem(row, per_row)
            z_row = z[b]
            for j in range(GROUP):
                place = wrap(cols[g * GROUP + j, b] + shift, slabs * blocks)
                place = jnp.where(j < remain, place, window)
                total[place] += jnp.dot(
                    z_row, held[row * GROUP + j], preferred_element_type=F32
                )
        return jnp.maximum(ready, need)

    ready = lax.fori_loop(0, steps, step, jnp.int32(0))
    lax.fori_loop(ready, blocks, wait_row, 0)
    sign = 2 * lax.rem(where[0], 2) - 1
    for order, out in enumerate(outs):
        base = ((order - REACH) * sign + REACH) * blocks

        def store(i, carry, out=out, base=base):
            for k in range(GROUP):
                at = i * GROUP + k
                out[at] = total[base + at].astype(BF16)
            return carry

        lax.fori_loop(0, blocks // GROUP, store, 0)


def contributions(where, cols, live, cot, mask, tiles, slabs, reps):
    blocks, slots, nodes = tiles.shape[:3]
    features = cot.shape[1]
    window = (2 * REACH + 1) * blocks
    lists = blocks * (slots // GROUP) + slots // GROUP + STEP
    counts = [2 * blocks, blocks, blocks, blocks]
    return pl.pallas_call(
        functools.partial(tiles_kernel, slabs, reps),
        out_shape=[jax.ShapeDtypeStruct((count, features, nodes), BF16) for count in counts]
        + [jax.ShapeDtypeStruct((blocks // reps, features, nodes), BF16)] * reps,
        in_specs=[smem()] * 3 + [hbm()] * 3,
        out_specs=[vmem()] * (len(counts) + reps),
        scratch_shapes=[
            pltpu.VMEM(cot.shape, BF16),
            pltpu.VMEM(mask.shape, jnp.int32),
            pltpu.VMEM(cot.shape, BF16),
            pltpu.VMEM((blocks * slots, nodes, nodes), BF16),
            pltpu.VMEM((window + 1, features, nodes), F32),
            pltpu.SMEM((lists,), jnp.int32),
            pltpu.SMEM((lists,), jnp.int32),
            pltpu.SemaphoreType.DMA((blocks,)),
            pltpu.SemaphoreType.DMA((2,)),
        ],
        compiler_params=pltpu.CompilerParams(vmem_limit_bytes=30 * MIB),
        cost_estimate=pl.CostEstimate(
            flops=2 * blocks * slots * features * nodes * nodes,
            bytes_accessed=tiles.size * 2,
            transcendentals=0,
        ),
    )(
        where,
        in_hbm(cols.T),
        in_hbm(live),
        in_hbm(cot),
        in_hbm(mask),
        in_hbm(tiles.reshape(blocks * slots, nodes, nodes)),
    )


def lay_features(where, shares, whole):
    reps, blocks = len(shares), whole.shape[0]
    features = shares[0].shape[1]
    for s in range(reps):
        first = pl.multiple_of(wrap(where[1] - s, reps) * features, features)
        whole[:, pl.ds(first, features), :] = shares[s][:blocks]


def mix_kernel(reps, where, *rest):
    shares, pieces, outs = rest[:reps], rest[reps : 2 * reps], rest[2 * reps : 3 * reps]
    weights, whole = rest[3 * reps :]
    blocks, features, nodes = outs[0].shape
    halves = weights.shape[1] // nodes
    lay_features(where, shares, whole)
    for s in range(reps):
        for h in range(halves):
            rows, columns = pl.ds(s * features, features), pl.ds(h * nodes, nodes)
            weights[rows, columns] = pieces[s][halves + h]
    for b in range(blocks):
        mixed = jnp.dot(weights[...], whole[b], preferred_element_type=F32)
        for s in range(reps):
            outs[s][b] = mixed[s * features : (s + 1) * features].astype(BF16)


def mix(where, shares, pieces):
    reps = len(shares)
    blocks, features, nodes = shares[0].shape
    width = reps * features
    return pl.pallas_call(
        functools.partial(mix_kernel, reps),
        out_shape=[jax.ShapeDtypeStruct((blocks, features, nodes), BF16)] * reps,
        in_specs=[smem()] + [vmem()] * (2 * reps),
        out_specs=[vmem()] * reps,
        scratch_shapes=[pltpu.VMEM((width, width), BF16), pltpu.VMEM((blocks, width, nodes), BF16)],
        compiler_params=pltpu.CompilerParams(vmem_limit_bytes=4 * MIB),
        cost_estimate=pl.CostEstimate(
            flops=2 * blocks * nodes * width * width,
            bytes_accessed=4 * blocks * nodes * width,
            transcendentals=0,
        ),
    )(where, *shares, *pieces)


def weight_kernel(reps, where, aggs, weight, *rest):
    shares, outs, (whole_z, whole_a) = rest[:reps], rest[reps : 2 * reps], rest[2 * reps :]
    blocks, features, nodes = shares[0].shape
    halves = weight.shape[1] // nodes
    lay_features(where, shares, whole_z)
    for s in range(reps):
        whole_a[:, pl.ds(s * features, features), :] = aggs[wrap(where[1] - s, reps)]
    total = jnp.zeros((whole_a.shape[1], whole_z.shape[1]), F32)
    for b in range(blocks):
        total += lax.dot_general(
            whole_a[b], whole_z[b], (((1,), (1,)), ((), ())), preferred_element_type=F32
        )
    for s in range(reps):
        for h in range(halves):
            columns = slice(h * nodes, (h + 1) * nodes)
            outs[s][h] = total[s * features : (s + 1) * features, columns].astype(BF16)
            outs[s][halves + h] = weight[:, columns]


def weight_partial(where, aggs, weight, shares):
    reps = len(shares)
    blocks, features, nodes = shares[0].shape
    width = reps * features
    pieces = jax.ShapeDtypeStruct((2 * (width // nodes), features, nodes), BF16)
    return pl.pallas_call(
        functools.partial(weight_kernel, reps),
        out_shape=[pieces] * reps,
        in_specs=[smem()] + [vmem()] * (2 + reps),
        out_specs=[vmem()] * reps,
        scratch_shapes=[pltpu.VMEM((blocks, width, nodes), BF16)] * 2,
        compiler_params=pltpu.CompilerParams(vmem_limit_bytes=4 * MIB),
        cost_estimate=pl.CostEstimate(
            flops=2 * blocks * nodes * width * width,
            bytes_accessed=4 * blocks * nodes * width + 2 * width * width,
            transcendentals=0,
        ),
    )(where, aggs, weight, *shares)


def add_kernel(one, other, out):
    def row(i, carry):
        out[i] = (one[i].astype(F32) + other[i].astype(F32)).astype(BF16)
        return carry

    lax.fori_loop(0, out.shape[0], row, 0)


def add(one, other):
    return pl.pallas_call(
        add_kernel,
        out_shape=jax.ShapeDtypeStruct(one.shape, BF16),
        in_specs=[vmem()] * 2,
        out_specs=vmem(),
        compiler_params=pltpu.CompilerParams(vmem_limit_bytes=2 * MIB),
        cost_estimate=pl.CostEstimate(
            flops=one.size, bytes_accessed=6 * one.size, transcendentals=0
        ),
    )(one, other)


def total_kernel(reps, where, aside, *rest):
    terms, outs = rest[:-reps], rest[-reps:]
    terms = (aside.at[pl.ds(terms[0].shape[0], terms[0].shape[0])], *terms)
    share = outs[0].shape[0]
    for s, out in enumerate(outs):
        first = wrap(where[1] + s, reps) * share
        for i in range(share):
            total = terms[0][first + i].astype(F32)
            for term in terms[1:]:
                total += term[first + i].astype(F32)
            out[i] = total.astype(BF16)


def total_shares(where, aside, terms, reps):
    blocks, features, nodes = terms[0].shape
    return pl.pallas_call(
        functools.partial(total_kernel, reps),
        out_shape=[jax.ShapeDtypeStruct((blocks // reps, features, nodes), BF16)] * reps,
        in_specs=[smem()] + [vmem()] * (1 + len(terms)),
        out_specs=[vmem()] * reps,
        compiler_params=pltpu.CompilerParams(vmem_limit_bytes=2 * MIB),
        cost_estimate=pl.CostEstimate(
            flops=4 * terms[0].size, bytes_accessed=10 * terms[0].size, transcendentals=0
        ),
    )(where, aside, *terms)


def lay_kernel(reps, where, *rest):
    shares, out, sems = rest[:reps], rest[reps], rest[reps + 1]
    blocks = shares[0].shape[0]
    copies = []
    for s in range(reps):
        first = wrap(where[1] - s, reps) * blocks
        copies.append(pltpu.make_async_copy(shares[s], out.at[pl.ds(first, blocks)], sems.at[s]))
        copies[s].start()
    for copy in copies:
        copy.wait()


def lay_blocks(where, shares, shape):
    reps = len(shares)
    return pl.pallas_call(
        functools.partial(lay_kernel, reps),
        out_shape=jax.ShapeDtypeStruct(shape, BF16),
        in_specs=[smem()] + [vmem()] * reps,
        out_specs=hbm(),
        scratch_shapes=[pltpu.SemaphoreType.DMA((reps,))],
        compiler_params=pltpu.CompilerParams(vmem_limit_bytes=2 * MIB),
        cost_estimate=pl.CostEstimate(flops=0, bytes_accessed=32 * MIB, transcendentals=0),
    )(where, *shares)


def shift(value, steps):
    reps = lax.axis_size("rep")
    if steps % reps == 0:
        return value
    return lax.ppermute(value, "rep", [(i, (i + steps) % reps) for i in range(reps)])


def on_device(cotangent, relu_mask, aggregated, weight, tiles, col_block, live_count):
    blocks, features, nodes = cotangent.shape
    slabs, reps = lax.axis_size("blk"), lax.axis_size("rep")
    width = weight.shape[1]
    where = jnp.stack([lax.axis_index("blk"), lax.axis_index("rep")]).astype(jnp.int32)

    pair = [(i, i ^ 1) for i in range(slabs)]
    to_one = [(i, (i + (1 if i % 2 else -1)) % slabs) for i in range(slabs)]
    to_two = [(i, (i + (2 if i % 2 else -2)) % slabs) for i in range(slabs)]
    aggs = lax.all_to_all(
        aggregated.reshape(reps, blocks // reps, features, nodes), "rep", 0, 0, tiled=True
    )
    aside, own, one, two, *packed = contributions(
        where, col_block, live_count, cotangent, relu_mask, tiles, slabs, reps
    )
    aside, aggs = lax.optimization_barrier((aside, aggs))
    aside = lax.ppermute(aside, "blk", pair)
    two_in = lax.ppermute(two, "blk", to_two)
    one = add(one, aside)
    one_in = lax.ppermute(one, "blk", to_one)

    packed, _ = lax.optimization_barrier((packed, one))
    packed = [shift(value, s) for s, value in enumerate(packed)]
    pieces = weight_partial(where, aggs, weight, packed)

    own, pieces = lax.optimization_barrier((own, pieces))
    pieces = [shift(value, -s) for s, value in enumerate(pieces)]
    shares = total_shares(where, aside, [own, one_in, two_in], reps)
    shares = [shift(value, s) for s, value in enumerate(shares)]
    outs = [shift(value, s) for s, value in enumerate(mix(where, shares, pieces))]
    input_grad = lay_blocks(where, outs, cotangent.shape)

    grad_w = sum(value[: width // nodes].astype(F32) for value in pieces)
    grad_w = grad_w + lax.ppermute(grad_w, "blk", pair)
    grad_w = grad_w + sum(
        lax.ppermute(grad_w, "blk", [(i, i ^ step) for i in range(slabs)])
        for step in range(2, slabs, 2)
    )
    grad_w = grad_w.transpose(1, 0, 2).reshape(features, width)
    return input_grad, grad_w * (1.0 / math.sqrt(slabs * blocks * nodes))


def solution(mesh):
    placed = (
        P("blk", "rep", None),
        P("blk", "rep", None),
        P("blk", "rep", None),
        P("rep", None),
        P("blk", None, None, None),
        P("blk", None),
        P("blk"),
    )
    return jax.shard_map(
        on_device,
        mesh=mesh,
        in_specs=placed,
        out_specs=(P("blk", "rep", None), P("rep", None)),
        check_vma=False,
    )
```

```python
import functools
import math

import jax
import jax.numpy as jnp
from jax import lax
from jax.experimental import pallas as pl
from jax.experimental.pallas import tpu as pltpu
from jax.sharding import PartitionSpec as P

REACH = 2
GROUP = 4
STEP = 8
BF16 = jnp.bfloat16
F32 = jnp.float32
MIB = 1 << 20


def vmem():
    return pl.BlockSpec(memory_space=pltpu.VMEM)


def smem():
    return pl.BlockSpec(memory_space=pltpu.SMEM)


def hbm():
    return pl.BlockSpec(memory_space=pl.ANY)


def in_hbm(value):
    return pltpu.with_memory_space_constraint(value, pltpu.HBM)


def wrap(value, size):
    if size & (size - 1):
        return lax.rem(value + size, size)
    return value & (size - 1)


def tiles_kernel(slabs, reps, where, cols, live, cot, mask, agg, weight, tiles, *rest):
    outs, packed, rest = rest[:4], rest[4 : 4 + reps], rest[4 + reps :]
    outs = [outs[0].at[pl.ds(0, cols.shape[1])], outs[0].at[pl.ds(cols.shape[1], cols.shape[1])], *outs[1:]]
    cot_in, mask_in, z, held, total, rows, left, sems, z_sems, agg_sems = rest
    share = cols.shape[1] // reps
    slots, blocks = cols.shape
    per_row = slots // GROUP
    window = (2 * REACH + 1) * blocks
    copies = [
        pltpu.make_async_copy(cot, cot_in, z_sems.at[0]),
        pltpu.make_async_copy(mask, mask_in, z_sems.at[1]),
    ]
    for copy in copies:
        copy.start()

    def groups_of(b):
        return lax.shift_right_logical(live[b] + GROUP - 1, GROUP.bit_length() - 1)

    def fetched(b, act):
        groups = groups_of(b)
        for g in range(1, per_row + 1):

            @pl.when(groups == g)
            def _(span=pl.ds(b * slots, g * GROUP)):
                act(pltpu.make_async_copy(tiles.at[span], held.at[span], sems.at[b]))

    def list_row(b, count):
        fetched(b, lambda copy: copy.start())
        for g in range(per_row):
            rows[count + g] = b * per_row + g
            left[count + g] = live[b] - g * GROUP
        return count + groups_of(b)

    count = lax.fori_loop(0, blocks, list_row, jnp.int32(0))
    for u in range(STEP):
        rows[count + u] = 0
        left[count + u] = 0
    steps = lax.div(count + STEP - 1, STEP)

    def wait_row(b, carry):
        fetched(b, lambda copy: copy.wait())
        return carry

    def clear(i, carry):
        total[pl.ds(i * GROUP, GROUP)] = jnp.zeros((GROUP,) + total.shape[1:], F32)
        return carry

    lax.fori_loop(0, window // GROUP, clear, 0)
    for copy in copies:
        copy.wait()

    def mask_row(b, carry):
        z[b] = cot_in[b] * mask_in[b].astype(BF16)
        return carry

    lax.fori_loop(0, blocks, mask_row, 0)
    agg_copies = []
    for s in range(reps):
        span = pl.ds(wrap(where[1] + s, reps) * share, share)
        packed[s][:share] = z[span]
        end = packed[s].at[pl.ds(share, share)]
        ends = [(agg.at[span], end)]
        for h in range(weight.shape[1] // z.shape[2]):
            columns = pl.ds(h * z.shape[2], z.shape[2])
            ends.append((weight.at[:, columns], packed[s].at[2 * share + h]))
        for source, target in ends:
            copy = pltpu.make_async_copy(source, target, agg_sems.at[len(agg_copies)])
            copy.start()
            agg_copies.append(copy)
    shift = REACH * blocks - where[0] * blocks

    def step(i, ready):
        entries = [rows[i * STEP + u] for u in range(STEP)]
        need = lax.div(functools.reduce(jnp.maximum, entries), per_row) + 1
        lax.fori_loop(ready, need, wait_row, 0)
        for u in range(STEP):
            row, remain = entries[u], left[i * STEP + u]
            b, g = lax.div(row, per_row), lax.rem(row, per_row)
            z_row = z[b]
            for j in range(GROUP):
                place = wrap(cols[g * GROUP + j, b] + shift, slabs * blocks)
                place = jnp.where(j < remain, place, window)
                total[place] += jnp.dot(
                    z_row, held[row * GROUP + j], preferred_element_type=F32
                )
        return jnp.maximum(ready, need)

    ready = lax.fori_loop(0, steps, step, jnp.int32(0))
    lax.fori_loop(ready, blocks, wait_row, 0)
    for copy in agg_copies:
        copy.wait()
    sign = 2 * lax.rem(where[0], 2) - 1
    for order, out in enumerate(outs):
        base = ((order - REACH) * sign + REACH) * blocks

        def store(i, carry, out=out, base=base):
            for k in range(GROUP):
                at = i * GROUP + k
                out[at] = total[base + at].astype(BF16)
            return carry

        lax.fori_loop(0, blocks // GROUP, store, 0)


def contributions(where, cols, live, cot, mask, agg, weight, tiles, slabs, reps):
    blocks, slots, nodes = tiles.shape[:3]
    features = cot.shape[1]
    window = (2 * REACH + 1) * blocks
    lists = blocks * (slots // GROUP) + slots // GROUP + STEP
    counts = [2 * blocks, blocks, blocks, blocks]
    halves = weight.shape[1] // nodes
    packs = 2 * blocks // reps + halves
    return pl.pallas_call(
        functools.partial(tiles_kernel, slabs, reps),
        out_shape=[jax.ShapeDtypeStruct((count, features, nodes), BF16) for count in counts]
        + [jax.ShapeDtypeStruct((packs, features, nodes), BF16)] * reps,
        in_specs=[smem()] * 3 + [hbm()] * 5,
        out_specs=[vmem()] * (len(counts) + reps),
        scratch_shapes=[
            pltpu.VMEM(cot.shape, BF16),
            pltpu.VMEM(mask.shape, jnp.int32),
            pltpu.VMEM(cot.shape, BF16),
            pltpu.VMEM((blocks * slots, nodes, nodes), BF16),
            pltpu.VMEM((window + 1, features, nodes), F32),
            pltpu.SMEM((lists,), jnp.int32),
            pltpu.SMEM((lists,), jnp.int32),
            pltpu.SemaphoreType.DMA((blocks,)),
            pltpu.SemaphoreType.DMA((2,)),
            pltpu.SemaphoreType.DMA((reps * (1 + halves),)),
        ],
        compiler_params=pltpu.CompilerParams(vmem_limit_bytes=30 * MIB),
        cost_estimate=pl.CostEstimate(
            flops=2 * blocks * slots * features * nodes * nodes,
            bytes_accessed=tiles.size * 2,
            transcendentals=0,
        ),
    )(
        where,
        in_hbm(cols.T),
        in_hbm(live),
        in_hbm(cot),
        in_hbm(mask),
        in_hbm(agg),
        in_hbm(weight),
        in_hbm(tiles.reshape(blocks * slots, nodes, nodes)),
    )


def lay_features(where, shares, whole):
    reps, blocks = len(shares), whole.shape[0]
    features = shares[0].shape[1]
    for s in range(reps):
        first = pl.multiple_of(wrap(where[1] - s, reps) * features, features)
        whole[:, pl.ds(first, features), :] = shares[s][:blocks]


def mix_kernel(reps, where, *rest):
    shares, packed, outs = rest[:reps], rest[reps : 2 * reps], rest[2 * reps : 3 * reps]
    weights, whole = rest[3 * reps :]
    blocks, features, nodes = outs[0].shape
    lay_features(where, shares, whole)
    for s in range(reps):
        for h in range(weights.shape[1] // nodes):
            rows, columns = pl.ds(s * features, features), pl.ds(h * nodes, nodes)
            weights[rows, columns] = packed[(reps - s) % reps][2 * blocks + h]
    for b in range(blocks):
        mixed = jnp.dot(weights[...], whole[b], preferred_element_type=F32)
        for s in range(reps):
            outs[s][b] = mixed[s * features : (s + 1) * features].astype(BF16)


def mix(where, shares, packed):
    reps = len(shares)
    blocks, features, nodes = shares[0].shape
    width = reps * features
    return pl.pallas_call(
        functools.partial(mix_kernel, reps),
        out_shape=[jax.ShapeDtypeStruct((blocks, features, nodes), BF16)] * reps,
        in_specs=[smem()] + [vmem()] * (2 * reps),
        out_specs=[vmem()] * reps,
        scratch_shapes=[pltpu.VMEM((width, width), BF16), pltpu.VMEM((blocks, width, nodes), BF16)],
        compiler_params=pltpu.CompilerParams(vmem_limit_bytes=4 * MIB),
        cost_estimate=pl.CostEstimate(
            flops=2 * blocks * nodes * width * width,
            bytes_accessed=4 * blocks * nodes * width,
            transcendentals=0,
        ),
    )(where, *shares, *packed)


def weight_kernel(reps, where, *rest):
    packed, outs, (whole_z, whole_a) = rest[:reps], rest[reps : 2 * reps], rest[2 * reps :]
    blocks, _, nodes = whole_z.shape
    features = packed[0].shape[1]
    lay_features(where, packed, whole_z)
    for s in range(reps):
        whole_a[:, pl.ds(s * features, features), :] = packed[s][blocks : 2 * blocks]
    total = jnp.zeros((whole_a.shape[1], whole_z.shape[1]), F32)
    for b in range(blocks):
        total += lax.dot_general(
            whole_a[b], whole_z[b], (((1,), (1,)), ((), ())), preferred_element_type=F32
        )
    for s in range(reps):
        for h in range(outs[s].shape[0]):
            part = total[s * features : (s + 1) * features, h * nodes : (h + 1) * nodes]
            outs[s][h] = part.astype(BF16)


def weight_partial(where, packed, blocks):
    reps = len(packed)
    _, features, nodes = packed[0].shape
    width = reps * features
    return pl.pallas_call(
        functools.partial(weight_kernel, reps),
        out_shape=[jax.ShapeDtypeStruct((width // nodes, features, nodes), BF16)] * reps,
        in_specs=[smem()] + [vmem()] * reps,
        out_specs=[vmem()] * reps,
        scratch_shapes=[pltpu.VMEM((blocks, width, nodes), BF16)] * 2,
        compiler_params=pltpu.CompilerParams(vmem_limit_bytes=4 * MIB),
        cost_estimate=pl.CostEstimate(
            flops=2 * blocks * nodes * width * width,
            bytes_accessed=4 * blocks * nodes * width + 2 * width * width,
            transcendentals=0,
        ),
    )(where, *packed)


def add_kernel(one, other, out):
    def row(i, carry):
        out[i] = (one[i].astype(F32) + other[i].astype(F32)).astype(BF16)
        return carry

    lax.fori_loop(0, out.shape[0], row, 0)


def add(one, other):
    return pl.pallas_call(
        add_kernel,
        out_shape=jax.ShapeDtypeStruct(one.shape, BF16),
        in_specs=[vmem()] * 2,
        out_specs=vmem(),
        compiler_params=pltpu.CompilerParams(vmem_limit_bytes=2 * MIB),
        cost_estimate=pl.CostEstimate(
            flops=one.size, bytes_accessed=6 * one.size, transcendentals=0
        ),
    )(one, other)


def total_kernel(reps, where, aside, *rest):
    terms, outs = rest[:-reps], rest[-reps:]
    terms = (aside.at[pl.ds(terms[0].shape[0], terms[0].shape[0])], *terms)
    share = outs[0].shape[0]
    for s, out in enumerate(outs):
        first = wrap(where[1] + s, reps) * share
        for i in range(share):
            total = terms[0][first + i].astype(F32)
            for term in terms[1:]:
                total += term[first + i].astype(F32)
            out[i] = total.astype(BF16)


def total_shares(where, aside, terms, reps):
    blocks, features, nodes = terms[0].shape
    return pl.pallas_call(
        functools.partial(total_kernel, reps),
        out_shape=[jax.ShapeDtypeStruct((blocks // reps, features, nodes), BF16)] * reps,
        in_specs=[smem()] + [vmem()] * (1 + len(terms)),
        out_specs=[vmem()] * reps,
        compiler_params=pltpu.CompilerParams(vmem_limit_bytes=2 * MIB),
        cost_estimate=pl.CostEstimate(
            flops=4 * terms[0].size, bytes_accessed=10 * terms[0].size, transcendentals=0
        ),
    )(where, aside, *terms)


def lay_kernel(reps, where, *rest):
    shares, out, sems = rest[:reps], rest[reps], rest[reps + 1]
    blocks = shares[0].shape[0]
    copies = []
    for s in range(reps):
        first = wrap(where[1] - s, reps) * blocks
        copies.append(pltpu.make_async_copy(shares[s], out.at[pl.ds(first, blocks)], sems.at[s]))
        copies[s].start()
    for copy in copies:
        copy.wait()


def lay_blocks(where, shares, shape):
    reps = len(shares)
    return pl.pallas_call(
        functools.partial(lay_kernel, reps),
        out_shape=jax.ShapeDtypeStruct(shape, BF16),
        in_specs=[smem()] + [vmem()] * reps,
        out_specs=hbm(),
        scratch_shapes=[pltpu.SemaphoreType.DMA((reps,))],
        compiler_params=pltpu.CompilerParams(vmem_limit_bytes=2 * MIB),
        cost_estimate=pl.CostEstimate(flops=0, bytes_accessed=32 * MIB, transcendentals=0),
    )(where, *shares)


def shift(value, steps):
    reps = lax.axis_size("rep")
    if steps % reps == 0:
        return value
    return lax.ppermute(value, "rep", [(i, (i + steps) % reps) for i in range(reps)])


def on_device(cotangent, relu_mask, aggregated, weight, tiles, col_block, live_count):
    blocks, features, nodes = cotangent.shape
    slabs, reps = lax.axis_size("blk"), lax.axis_size("rep")
    width = weight.shape[1]
    where = jnp.stack([lax.axis_index("blk"), lax.axis_index("rep")]).astype(jnp.int32)

    pair = [(i, i ^ 1) for i in range(slabs)]
    to_one = [(i, (i + (1 if i % 2 else -1)) % slabs) for i in range(slabs)]
    to_two = [(i, (i + (2 if i % 2 else -2)) % slabs) for i in range(slabs)]
    aside, own, one, two, *packed = contributions(
        where, col_block, live_count, cotangent, relu_mask, aggregated, weight, tiles, slabs, reps
    )
    aside = lax.ppermute(aside, "blk", pair)
    two_in = lax.ppermute(two, "blk", to_two)
    one = add(one, aside)
    one_in = lax.ppermute(one, "blk", to_one)

    packed, _ = lax.optimization_barrier((packed, one))
    packed = [shift(value, s) for s, value in enumerate(packed)]
    shares = total_shares(where, aside, [own, one_in, two_in], reps)
    held, _ = lax.optimization_barrier((packed, shares))
    pieces = weight_partial(where, held, blocks // reps)
    pieces = [shift(value, -s) for s, value in enumerate(pieces)]
    shares = [shift(value, s) for s, value in enumerate(shares)]
    outs = [shift(value, s) for s, value in enumerate(mix(where, shares, packed))]
    input_grad = lay_blocks(where, outs, cotangent.shape)

    grad_w = sum(value.astype(F32) for value in pieces)
    grad_w = grad_w + lax.ppermute(grad_w, "blk", pair)
    parts = [
        lax.ppermute(grad_w, "blk", [(i, i ^ step) for i in range(slabs)])
        for step in range(2, slabs, 2)
    ]
    parts, _ = lax.optimization_barrier((parts, input_grad))
    grad_w = grad_w + sum(parts)
    grad_w = grad_w.transpose(1, 0, 2).reshape(features, width)
    return input_grad, grad_w * (1.0 / math.sqrt(slabs * blocks * nodes))


def solution(mesh):
    placed = (
        P("blk", "rep", None),
        P("blk", "rep", None),
        P("blk", "rep", None),
        P("rep", None),
        P("blk", None, None, None),
        P("blk", None),
        P("blk"),
    )
    return jax.shard_map(
        on_device,
        mesh=mesh,
        in_specs=placed,
        out_specs=(P("blk", "rep", None), P("rep", None)),
        check_vma=False,
    )
```

```python
import functools
import math

import jax
import jax.numpy as jnp
from jax import lax
from jax.experimental import pallas as pl
from jax.experimental.pallas import tpu as pltpu
from jax.sharding import PartitionSpec as P

REACH = 2
GROUP = 4
STEP = 8
BF16 = jnp.bfloat16
F32 = jnp.float32
MIB = 1 << 20


def vmem():
    return pl.BlockSpec(memory_space=pltpu.VMEM)


def smem():
    return pl.BlockSpec(memory_space=pltpu.SMEM)


def hbm():
    return pl.BlockSpec(memory_space=pl.ANY)


def in_hbm(value):
    return pltpu.with_memory_space_constraint(value, pltpu.HBM)


def wrap(value, size):
    if size & (size - 1):
        return lax.rem(value + size, size)
    return value & (size - 1)


def tiles_kernel(slabs, reps, where, cols, live, cot, mask, agg, weight, tiles, *rest):
    outs, packed, rest = rest[:4], rest[4 : 4 + reps], rest[4 + reps :]
    outs = [outs[0].at[pl.ds(0, cols.shape[1])], outs[0].at[pl.ds(cols.shape[1], cols.shape[1])], *outs[1:]]
    cot_in, mask_in, z, held, total, rows, left, sems, z_sems, agg_sems = rest
    share = cols.shape[1] // reps
    slots, blocks = cols.shape
    per_row = slots // GROUP
    window = (2 * REACH + 1) * blocks
    copies = [
        pltpu.make_async_copy(cot, cot_in, z_sems.at[0]),
        pltpu.make_async_copy(mask, mask_in, z_sems.at[1]),
    ]
    for copy in copies:
        copy.start()

    def groups_of(b):
        return lax.shift_right_logical(live[b] + GROUP - 1, GROUP.bit_length() - 1)

    def fetched(b, act):
        groups = groups_of(b)
        for g in range(1, per_row + 1):

            @pl.when(groups == g)
            def _(span=pl.ds(b * slots, g * GROUP)):
                act(pltpu.make_async_copy(tiles.at[span], held.at[span], sems.at[b]))

    def list_row(b, count):
        fetched(b, lambda copy: copy.start())
        for g in range(per_row):
            rows[count + g] = b * per_row + g
            left[count + g] = live[b] - g * GROUP
        return count + groups_of(b)

    count = lax.fori_loop(0, blocks, list_row, jnp.int32(0))
    for u in range(STEP):
        rows[count + u] = 0
        left[count + u] = 0
    steps = lax.div(count + STEP - 1, STEP)

    def wait_row(b, carry):
        fetched(b, lambda copy: copy.wait())
        return carry

    def clear(i, carry):
        total[pl.ds(i * GROUP, GROUP)] = jnp.zeros((GROUP,) + total.shape[1:], F32)
        return carry

    lax.fori_loop(0, window // GROUP, clear, 0)
    for copy in copies:
        copy.wait()

    def mask_row(b, carry):
        z[b] = cot_in[b] * mask_in[b].astype(BF16)
        return carry

    lax.fori_loop(0, blocks, mask_row, 0)
    agg_copies = []
    for s in range(reps):
        span = pl.ds(wrap(where[1] + s, reps) * share, share)
        packed[s][:share] = z[span]
        end = packed[s].at[pl.ds(share, share)]
        ends = [(agg.at[span], end)]
        for h in range(weight.shape[1] // z.shape[2]):
            columns = pl.ds(h * z.shape[2], z.shape[2])
            ends.append((weight.at[:, columns], packed[s].at[2 * share + h]))
        for source, target in ends:
            copy = pltpu.make_async_copy(source, target, agg_sems.at[len(agg_copies)])
            copy.start()
            agg_copies.append(copy)
    shift = REACH * blocks - where[0] * blocks

    def step(i, ready):
        entries = [rows[i * STEP + u] for u in range(STEP)]
        need = lax.div(functools.reduce(jnp.maximum, entries), per_row) + 1
        lax.fori_loop(ready, need, wait_row, 0)
        for u in range(STEP):
            row, remain = entries[u], left[i * STEP + u]
            b, g = lax.div(row, per_row), lax.rem(row, per_row)
            z_row = z[b]
            for j in range(GROUP):
                place = wrap(cols[g * GROUP + j, b] + shift, slabs * blocks)
                place = jnp.where(j < remain, place, window)
                total[place] += jnp.dot(
                    z_row, held[row * GROUP + j], preferred_element_type=F32
                )
        return jnp.maximum(ready, need)

    ready = lax.fori_loop(0, steps, step, jnp.int32(0))
    lax.fori_loop(ready, blocks, wait_row, 0)
    for copy in agg_copies:
        copy.wait()
    sign = 2 * lax.rem(where[0], 2) - 1
    for order, out in enumerate(outs):
        base = ((order - REACH) * sign + REACH) * blocks

        def store(i, carry, out=out, base=base):
            for k in range(GROUP):
                at = i * GROUP + k
                out[at] = total[base + at].astype(BF16)
            return carry

        lax.fori_loop(0, blocks // GROUP, store, 0)


def contributions(where, cols, live, cot, mask, agg, weight, tiles, slabs, reps):
    blocks, slots, nodes = tiles.shape[:3]
    features = cot.shape[1]
    window = (2 * REACH + 1) * blocks
    lists = blocks * (slots // GROUP) + slots // GROUP + STEP
    counts = [2 * blocks, blocks, blocks, blocks]
    halves = weight.shape[1] // nodes
    packs = 2 * blocks // reps + halves
    return pl.pallas_call(
        functools.partial(tiles_kernel, slabs, reps),
        out_shape=[jax.ShapeDtypeStruct((count, features, nodes), BF16) for count in counts]
        + [jax.ShapeDtypeStruct((packs, features, nodes), BF16)] * reps,
        in_specs=[smem()] * 3 + [hbm()] * 5,
        out_specs=[vmem()] * (len(counts) + reps),
        scratch_shapes=[
            pltpu.VMEM(cot.shape, BF16),
            pltpu.VMEM(mask.shape, jnp.int32),
            pltpu.VMEM(cot.shape, BF16),
            pltpu.VMEM((blocks * slots, nodes, nodes), BF16),
            pltpu.VMEM((window + 1, features, nodes), F32),
            pltpu.SMEM((lists,), jnp.int32),
            pltpu.SMEM((lists,), jnp.int32),
            pltpu.SemaphoreType.DMA((blocks,)),
            pltpu.SemaphoreType.DMA((2,)),
            pltpu.SemaphoreType.DMA((reps * (1 + halves),)),
        ],
        compiler_params=pltpu.CompilerParams(vmem_limit_bytes=30 * MIB),
        cost_estimate=pl.CostEstimate(
            flops=2 * blocks * slots * features * nodes * nodes,
            bytes_accessed=tiles.size * 2,
            transcendentals=0,
        ),
    )(
        where,
        in_hbm(cols.T),
        in_hbm(live),
        in_hbm(cot),
        in_hbm(mask),
        in_hbm(agg),
        in_hbm(weight),
        in_hbm(tiles.reshape(blocks * slots, nodes, nodes)),
    )


def lay_features(where, shares, whole):
    reps, blocks = len(shares), whole.shape[0]
    features = shares[0].shape[1]
    for s in range(reps):
        first = pl.multiple_of(wrap(where[1] - s, reps) * features, features)
        whole[:, pl.ds(first, features), :] = shares[s][:blocks]


def mix_kernel(reps, where, *rest):
    shares, packed, outs = rest[:reps], rest[reps : 2 * reps], rest[2 * reps : 3 * reps]
    weights, whole = rest[3 * reps :]
    blocks, features, nodes = outs[0].shape
    lay_features(where, shares, whole)
    for s in range(reps):
        for h in range(weights.shape[1] // nodes):
            rows, columns = pl.ds(s * features, features), pl.ds(h * nodes, nodes)
            weights[rows, columns] = packed[(reps - s) % reps][2 * blocks + h]
    for b in range(blocks):
        mixed = jnp.dot(weights[...], whole[b], preferred_element_type=F32)
        for s in range(reps):
            outs[s][b] = mixed[s * features : (s + 1) * features].astype(BF16)


def mix(where, shares, packed):
    reps = len(shares)
    blocks, features, nodes = shares[0].shape
    width = reps * features
    return pl.pallas_call(
        functools.partial(mix_kernel, reps),
        out_shape=[jax.ShapeDtypeStruct((blocks, features, nodes), BF16)] * reps,
        in_specs=[smem()] + [vmem()] * (2 * reps),
        out_specs=[vmem()] * reps,
        scratch_shapes=[pltpu.VMEM((width, width), BF16), pltpu.VMEM((blocks, width, nodes), BF16)],
        compiler_params=pltpu.CompilerParams(vmem_limit_bytes=4 * MIB),
        cost_estimate=pl.CostEstimate(
            flops=2 * blocks * nodes * width * width,
            bytes_accessed=4 * blocks * nodes * width,
            transcendentals=0,
        ),
    )(where, *shares, *packed)


def weight_kernel(reps, where, *rest):
    packed, outs, (whole_z, whole_a) = rest[:reps], rest[reps : 2 * reps], rest[2 * reps :]
    blocks, _, nodes = whole_z.shape
    features = packed[0].shape[1]
    lay_features(where, packed, whole_z)
    for s in range(reps):
        whole_a[:, pl.ds(s * features, features), :] = packed[s][blocks : 2 * blocks]
    total = jnp.zeros((whole_a.shape[1], whole_z.shape[1]), F32)
    for b in range(blocks):
        total += lax.dot_general(
            whole_a[b], whole_z[b], (((1,), (1,)), ((), ())), preferred_element_type=F32
        )
    for s in range(reps):
        for h in range(outs[s].shape[0]):
            part = total[s * features : (s + 1) * features, h * nodes : (h + 1) * nodes]
            outs[s][h] = part.astype(BF16)


def weight_partial(where, packed, blocks):
    reps = len(packed)
    _, features, nodes = packed[0].shape
    width = reps * features
    return pl.pallas_call(
        functools.partial(weight_kernel, reps),
        out_shape=[jax.ShapeDtypeStruct((width // nodes, features, nodes), BF16)] * reps,
        in_specs=[smem()] + [vmem()] * reps,
        out_specs=[vmem()] * reps,
        scratch_shapes=[pltpu.VMEM((blocks, width, nodes), BF16)] * 2,
        compiler_params=pltpu.CompilerParams(vmem_limit_bytes=4 * MIB),
        cost_estimate=pl.CostEstimate(
            flops=2 * blocks * nodes * width * width,
            bytes_accessed=4 * blocks * nodes * width + 2 * width * width,
            transcendentals=0,
        ),
    )(where, *packed)


def add_kernel(one, other, out):
    def row(i, carry):
        out[i] = (one[i].astype(F32) + other[i].astype(F32)).astype(BF16)
        return carry

    lax.fori_loop(0, out.shape[0], row, 0)


def add(one, other):
    return pl.pallas_call(
        add_kernel,
        out_shape=jax.ShapeDtypeStruct(one.shape, BF16),
        in_specs=[vmem()] * 2,
        out_specs=vmem(),
        compiler_params=pltpu.CompilerParams(vmem_limit_bytes=2 * MIB),
        cost_estimate=pl.CostEstimate(
            flops=one.size, bytes_accessed=6 * one.size, transcendentals=0
        ),
    )(one, other)


def total_kernel(reps, where, aside, *rest):
    terms, outs = rest[:-reps], rest[-reps:]
    terms = (aside.at[pl.ds(terms[0].shape[0], terms[0].shape[0])], *terms)
    share = outs[0].shape[0]
    for s, out in enumerate(outs):
        first = wrap(where[1] + s, reps) * share
        for i in range(share):
            total = terms[0][first + i].astype(F32)
            for term in terms[1:]:
                total += term[first + i].astype(F32)
            out[i] = total.astype(BF16)


def total_shares(where, aside, terms, reps):
    blocks, features, nodes = terms[0].shape
    return pl.pallas_call(
        functools.partial(total_kernel, reps),
        out_shape=[jax.ShapeDtypeStruct((blocks // reps, features, nodes), BF16)] * reps,
        in_specs=[smem()] + [vmem()] * (1 + len(terms)),
        out_specs=[vmem()] * reps,
        compiler_params=pltpu.CompilerParams(vmem_limit_bytes=2 * MIB),
        cost_estimate=pl.CostEstimate(
            flops=4 * terms[0].size, bytes_accessed=10 * terms[0].size, transcendentals=0
        ),
    )(where, aside, *terms)


def lay_kernel(reps, where, *rest):
    shares, out, sems = rest[:reps], rest[reps], rest[reps + 1]
    blocks = shares[0].shape[0]
    copies = []
    for s in range(reps):
        first = wrap(where[1] - s, reps) * blocks
        copies.append(pltpu.make_async_copy(shares[s], out.at[pl.ds(first, blocks)], sems.at[s]))
        copies[s].start()
    for copy in copies:
        copy.wait()


def lay_blocks(where, shares, shape):
    reps = len(shares)
    return pl.pallas_call(
        functools.partial(lay_kernel, reps),
        out_shape=jax.ShapeDtypeStruct(shape, BF16),
        in_specs=[smem()] + [vmem()] * reps,
        out_specs=hbm(),
        scratch_shapes=[pltpu.SemaphoreType.DMA((reps,))],
        compiler_params=pltpu.CompilerParams(vmem_limit_bytes=2 * MIB),
        cost_estimate=pl.CostEstimate(flops=0, bytes_accessed=32 * MIB, transcendentals=0),
    )(where, *shares)


def shift(value, steps):
    reps = lax.axis_size("rep")
    if steps % reps == 0:
        return value
    return lax.ppermute(value, "rep", [(i, (i + steps) % reps) for i in range(reps)])


def on_device(cotangent, relu_mask, aggregated, weight, tiles, col_block, live_count):
    blocks, features, nodes = cotangent.shape
    slabs, reps = lax.axis_size("blk"), lax.axis_size("rep")
    width = weight.shape[1]
    where = jnp.stack([lax.axis_index("blk"), lax.axis_index("rep")]).astype(jnp.int32)

    pair = [(i, i ^ 1) for i in range(slabs)]
    to_one = [(i, (i + (1 if i % 2 else -1)) % slabs) for i in range(slabs)]
    to_two = [(i, (i + (2 if i % 2 else -2)) % slabs) for i in range(slabs)]
    aside, own, one, two, *packed = contributions(
        where, col_block, live_count, cotangent, relu_mask, aggregated, weight, tiles, slabs, reps
    )
    aside = lax.ppermute(aside, "blk", pair)
    two_in = lax.ppermute(two, "blk", to_two)
    one = add(one, aside)
    one_in = lax.ppermute(one, "blk", to_one)

    packed = [shift(value, s) for s, value in enumerate(packed)]
    pieces = weight_partial(where, packed, blocks // reps)
    own, pieces = lax.optimization_barrier((own, pieces))
    shares = total_shares(where, aside, [own, one_in, two_in], reps)
    pieces, _ = lax.optimization_barrier((pieces, shares))
    pieces = [shift(value, -s) for s, value in enumerate(pieces)]
    shares = [shift(value, s) for s, value in enumerate(shares)]
    outs = [shift(value, s) for s, value in enumerate(mix(where, shares, packed))]
    input_grad = lay_blocks(where, outs, cotangent.shape)

    grad_w = sum(value.astype(F32) for value in pieces)
    grad_w = grad_w + lax.ppermute(grad_w, "blk", pair)
    parts = [
        lax.ppermute(grad_w, "blk", [(i, i ^ step) for i in range(slabs)])
        for step in range(2, slabs, 2)
    ]
    parts, _ = lax.optimization_barrier((parts, input_grad))
    grad_w = grad_w + sum(parts)
    grad_w = grad_w.transpose(1, 0, 2).reshape(features, width)
    return input_grad, grad_w * (1.0 / math.sqrt(slabs * blocks * nodes))


def solution(mesh):
    placed = (
        P("blk", "rep", None),
        P("blk", "rep", None),
        P("blk", "rep", None),
        P("rep", None),
        P("blk", None, None, None),
        P("blk", None),
        P("blk"),
    )
    return jax.shard_map(
        on_device,
        mesh=mesh,
        in_specs=placed,
        out_specs=(P("blk", "rep", None), P("rep", None)),
        check_vma=False,
    )
```

```python
import functools
import math

import jax
import jax.numpy as jnp
from jax import lax
from jax.experimental import pallas as pl
from jax.experimental.pallas import tpu as pltpu
from jax.sharding import PartitionSpec as P

REACH = 2
GROUP = 4
STEP = 8
BF16 = jnp.bfloat16
F32 = jnp.float32
MIB = 1 << 20


def vmem():
    return pl.BlockSpec(memory_space=pltpu.VMEM)


def smem():
    return pl.BlockSpec(memory_space=pltpu.SMEM)


def hbm():
    return pl.BlockSpec(memory_space=pl.ANY)


def in_hbm(value):
    return pltpu.with_memory_space_constraint(value, pltpu.HBM)


def wrap(value, size):
    if size & (size - 1):
        return lax.rem(value + size, size)
    return value & (size - 1)


def tiles_kernel(slabs, reps, where, cols, live, cot, mask, agg, weight, tiles, *rest):
    outs, packed, rest = rest[:4], rest[4 : 4 + reps], rest[4 + reps :]
    outs = [outs[0].at[pl.ds(0, cols.shape[1])], outs[0].at[pl.ds(cols.shape[1], cols.shape[1])], *outs[1:]]
    cot_in, mask_in, z, held, total, rows, left, sems, z_sems, agg_sems = rest
    share = cols.shape[1] // reps
    slots, blocks = cols.shape
    per_row = slots // GROUP
    window = (2 * REACH + 1) * blocks
    copies = [
        pltpu.make_async_copy(cot, cot_in, z_sems.at[0]),
        pltpu.make_async_copy(mask, mask_in, z_sems.at[1]),
    ]
    for copy in copies:
        copy.start()

    def groups_of(b):
        return lax.shift_right_logical(live[b] + GROUP - 1, GROUP.bit_length() - 1)

    def fetched(b, act):
        groups = groups_of(b)
        for g in range(1, per_row + 1):

            @pl.when(groups == g)
            def _(span=pl.ds(b * slots, g * GROUP)):
                act(pltpu.make_async_copy(tiles.at[span], held.at[span], sems.at[b]))

    def list_row(b, count):
        fetched(b, lambda copy: copy.start())
        for g in range(per_row):
            rows[count + g] = b * per_row + g
            left[count + g] = live[b] - g * GROUP
        return count + groups_of(b)

    count = lax.fori_loop(0, blocks, list_row, jnp.int32(0))
    for u in range(STEP):
        rows[count + u] = 0
        left[count + u] = 0
    steps = lax.div(count + STEP - 1, STEP)

    def wait_row(b, carry):
        fetched(b, lambda copy: copy.wait())
        return carry

    def clear(i, carry):
        total[pl.ds(i * GROUP, GROUP)] = jnp.zeros((GROUP,) + total.shape[1:], F32)
        return carry

    lax.fori_loop(0, window // GROUP, clear, 0)
    for copy in copies:
        copy.wait()

    def mask_row(b, carry):
        z[b] = cot_in[b] * mask_in[b].astype(BF16)
        return carry

    lax.fori_loop(0, blocks, mask_row, 0)
    agg_copies = []
    halves = weight.shape[1] // z.shape[2]
    for s in range(reps):
        span = pl.ds(wrap(where[1] + s, reps) * share, share)
        packed[s][:share] = z[span]
        ends = []
        for h in range(halves):
            columns = pl.ds(h * z.shape[2], z.shape[2])
            ends.append((weight.at[:, columns], packed[s].at[share + h]))
        if s != reps // 2:
            ends.append((agg.at[span], packed[s].at[pl.ds(share + halves, share)]))
        for source, target in ends:
            copy = pltpu.make_async_copy(source, target, agg_sems.at[len(agg_copies)])
            copy.start()
            agg_copies.append(copy)
    shift = REACH * blocks - where[0] * blocks

    def step(i, ready):
        entries = [rows[i * STEP + u] for u in range(STEP)]
        need = lax.div(functools.reduce(jnp.maximum, entries), per_row) + 1
        lax.fori_loop(ready, need, wait_row, 0)
        for u in range(STEP):
            row, remain = entries[u], left[i * STEP + u]
            b, g = lax.div(row, per_row), lax.rem(row, per_row)
            z_row = z[b]
            for j in range(GROUP):
                place = wrap(cols[g * GROUP + j, b] + shift, slabs * blocks)
                place = jnp.where(j < remain, place, window)
                total[place] += jnp.dot(
                    z_row, held[row * GROUP + j], preferred_element_type=F32
                )
        return jnp.maximum(ready, need)

    ready = lax.fori_loop(0, steps, step, jnp.int32(0))
    lax.fori_loop(ready, blocks, wait_row, 0)
    for copy in agg_copies:
        copy.wait()
    sign = 2 * lax.rem(where[0], 2) - 1
    for order, out in enumerate(outs):
        base = ((order - REACH) * sign + REACH) * blocks

        def store(i, carry, out=out, base=base):
            for k in range(GROUP):
                at = i * GROUP + k
                out[at] = total[base + at].astype(BF16)
            return carry

        lax.fori_loop(0, blocks // GROUP, store, 0)


def contributions(where, cols, live, cot, mask, agg, weight, tiles, slabs, reps):
    blocks, slots, nodes = tiles.shape[:3]
    features = cot.shape[1]
    window = (2 * REACH + 1) * blocks
    lists = blocks * (slots // GROUP) + slots // GROUP + STEP
    counts = [2 * blocks, blocks, blocks, blocks]
    halves = weight.shape[1] // nodes
    packs = [(2 - (s == reps // 2)) * blocks // reps + halves for s in range(reps)]
    return pl.pallas_call(
        functools.partial(tiles_kernel, slabs, reps),
        out_shape=[jax.ShapeDtypeStruct((count, features, nodes), BF16) for count in counts]
        + [jax.ShapeDtypeStruct((count, features, nodes), BF16) for count in packs],
        in_specs=[smem()] * 3 + [hbm()] * 5,
        out_specs=[vmem()] * (len(counts) + reps),
        scratch_shapes=[
            pltpu.VMEM(cot.shape, BF16),
            pltpu.VMEM(mask.shape, jnp.int32),
            pltpu.VMEM(cot.shape, BF16),
            pltpu.VMEM((blocks * slots, nodes, nodes), BF16),
            pltpu.VMEM((window + 1, features, nodes), F32),
            pltpu.SMEM((lists,), jnp.int32),
            pltpu.SMEM((lists,), jnp.int32),
            pltpu.SemaphoreType.DMA((blocks,)),
            pltpu.SemaphoreType.DMA((2,)),
            pltpu.SemaphoreType.DMA((reps * (1 + halves),)),
        ],
        compiler_params=pltpu.CompilerParams(vmem_limit_bytes=30 * MIB),
        cost_estimate=pl.CostEstimate(
            flops=2 * blocks * slots * features * nodes * nodes,
            bytes_accessed=tiles.size * 2,
            transcendentals=0,
        ),
    )(
        where,
        in_hbm(cols.T),
        in_hbm(live),
        in_hbm(cot),
        in_hbm(mask),
        in_hbm(agg),
        in_hbm(weight),
        in_hbm(tiles.reshape(blocks * slots, nodes, nodes)),
    )


def lay_features(where, shares, whole):
    reps, blocks = len(shares), whole.shape[0]
    features = shares[0].shape[1]
    for s in range(reps):
        first = pl.multiple_of(wrap(where[1] - s, reps) * features, features)
        whole[:, pl.ds(first, features), :] = shares[s][:blocks]


def mix_kernel(reps, where, *rest):
    shares, packed, outs = rest[:reps], rest[reps : 2 * reps], rest[2 * reps : 3 * reps]
    weights, whole = rest[3 * reps :]
    blocks, features, nodes = outs[0].shape
    lay_features(where, shares, whole)
    for s in range(reps):
        for h in range(weights.shape[1] // nodes):
            rows, columns = pl.ds(s * features, features), pl.ds(h * nodes, nodes)
            weights[rows, columns] = packed[(reps - s) % reps][blocks + h]
    for b in range(blocks):
        mixed = jnp.dot(weights[...], whole[b], preferred_element_type=F32)
        for s in range(reps):
            outs[s][b] = mixed[s * features : (s + 1) * features].astype(BF16)


def mix(where, shares, packed):
    reps = len(shares)
    blocks, features, nodes = shares[0].shape
    width = reps * features
    return pl.pallas_call(
        functools.partial(mix_kernel, reps),
        out_shape=[jax.ShapeDtypeStruct((blocks, features, nodes), BF16)] * reps,
        in_specs=[smem()] + [vmem()] * (2 * reps),
        out_specs=[vmem()] * reps,
        scratch_shapes=[pltpu.VMEM((width, width), BF16), pltpu.VMEM((blocks, width, nodes), BF16)],
        compiler_params=pltpu.CompilerParams(vmem_limit_bytes=4 * MIB),
        cost_estimate=pl.CostEstimate(
            flops=2 * blocks * nodes * width * width,
            bytes_accessed=4 * blocks * nodes * width,
            transcendentals=0,
        ),
    )(where, *shares, *packed)


def weight_kernel(reps, where, *rest):
    agg, packed, outs = rest[0], rest[1 : 1 + reps], rest[1 + reps : 1 + 2 * reps]
    whole_z, whole_a = rest[1 + 2 * reps :]
    blocks, _, nodes = whole_z.shape
    features = packed[0].shape[1]
    lay_features(where, packed, whole_z)
    for s in range(reps):
        part = agg[...] if s == reps // 2 else packed[s][packed[s].shape[0] - blocks :]
        whole_a[:, pl.ds(s * features, features), :] = part
    total = jnp.zeros((whole_a.shape[1], whole_z.shape[1]), F32)
    for b in range(blocks):
        total += lax.dot_general(
            whole_a[b], whole_z[b], (((1,), (1,)), ((), ())), preferred_element_type=F32
        )
    for s in range(reps):
        for h in range(outs[s].shape[0]):
            part = total[s * features : (s + 1) * features, h * nodes : (h + 1) * nodes]
            outs[s][h] = part.astype(BF16)


def weight_partial(where, agg, packed):
    reps = len(packed)
    blocks, features, nodes = agg.shape
    width = reps * features
    return pl.pallas_call(
        functools.partial(weight_kernel, reps),
        out_shape=[jax.ShapeDtypeStruct((width // nodes, features, nodes), BF16)] * reps,
        in_specs=[smem()] + [vmem()] * (1 + reps),
        out_specs=[vmem()] * reps,
        scratch_shapes=[pltpu.VMEM((blocks, width, nodes), BF16)] * 2,
        compiler_params=pltpu.CompilerParams(vmem_limit_bytes=4 * MIB),
        cost_estimate=pl.CostEstimate(
            flops=2 * blocks * nodes * width * width,
            bytes_accessed=4 * blocks * nodes * width + 2 * width * width,
            transcendentals=0,
        ),
    )(where, agg, *packed)


def add_kernel(one, other, out):
    def row(i, carry):
        out[i] = (one[i].astype(F32) + other[i].astype(F32)).astype(BF16)
        return carry

    lax.fori_loop(0, out.shape[0], row, 0)


def add(one, other):
    return pl.pallas_call(
        add_kernel,
        out_shape=jax.ShapeDtypeStruct(one.shape, BF16),
        in_specs=[vmem()] * 2,
        out_specs=vmem(),
        compiler_params=pltpu.CompilerParams(vmem_limit_bytes=2 * MIB),
        cost_estimate=pl.CostEstimate(
            flops=one.size, bytes_accessed=6 * one.size, transcendentals=0
        ),
    )(one, other)


def total_kernel(reps, where, aside, *rest):
    terms, outs = rest[:-reps], rest[-reps:]
    terms = (aside.at[pl.ds(terms[0].shape[0], terms[0].shape[0])], *terms)
    share = outs[0].shape[0]
    for s, out in enumerate(outs):
        first = wrap(where[1] + s, reps) * share
        for i in range(share):
            total = terms[0][first + i].astype(F32)
            for term in terms[1:]:
                total += term[first + i].astype(F32)
            out[i] = total.astype(BF16)


def total_shares(where, aside, terms, reps):
    blocks, features, nodes = terms[0].shape
    return pl.pallas_call(
        functools.partial(total_kernel, reps),
        out_shape=[jax.ShapeDtypeStruct((blocks // reps, features, nodes), BF16)] * reps,
        in_specs=[smem()] + [vmem()] * (1 + len(terms)),
        out_specs=[vmem()] * reps,
        compiler_params=pltpu.CompilerParams(vmem_limit_bytes=2 * MIB),
        cost_estimate=pl.CostEstimate(
            flops=4 * terms[0].size, bytes_accessed=10 * terms[0].size, transcendentals=0
        ),
    )(where, aside, *terms)


def lay_kernel(reps, where, *rest):
    shares, out, sems = rest[:reps], rest[reps], rest[reps + 1]
    blocks = shares[0].shape[0]
    copies = []
    for s in range(reps):
        first = wrap(where[1] - s, reps) * blocks
        copies.append(pltpu.make_async_copy(shares[s], out.at[pl.ds(first, blocks)], sems.at[s]))
        copies[s].start()
    for copy in copies:
        copy.wait()


def lay_blocks(where, shares, shape):
    reps = len(shares)
    return pl.pallas_call(
        functools.partial(lay_kernel, reps),
        out_shape=jax.ShapeDtypeStruct(shape, BF16),
        in_specs=[smem()] + [vmem()] * reps,
        out_specs=hbm(),
        scratch_shapes=[pltpu.SemaphoreType.DMA((reps,))],
        compiler_params=pltpu.CompilerParams(vmem_limit_bytes=2 * MIB),
        cost_estimate=pl.CostEstimate(flops=0, bytes_accessed=32 * MIB, transcendentals=0),
    )(where, *shares)


def shift(value, steps):
    reps = lax.axis_size("rep")
    if steps % reps == 0:
        return value
    return lax.ppermute(value, "rep", [(i, (i + steps) % reps) for i in range(reps)])


def on_device(cotangent, relu_mask, aggregated, weight, tiles, col_block, live_count):
    blocks, features, nodes = cotangent.shape
    slabs, reps = lax.axis_size("blk"), lax.axis_size("rep")
    width = weight.shape[1]
    where = jnp.stack([lax.axis_index("blk"), lax.axis_index("rep")]).astype(jnp.int32)

    pair = [(i, i ^ 1) for i in range(slabs)]
    to_one = [(i, (i + (1 if i % 2 else -1)) % slabs) for i in range(slabs)]
    to_two = [(i, (i + (2 if i % 2 else -2)) % slabs) for i in range(slabs)]
    share = blocks // reps
    first = lax.rem(lax.axis_index("rep") + reps // 2, reps) * share
    middle = shift(lax.dynamic_slice_in_dim(aggregated, first, share, 0), reps // 2)
    aside, own, one, two, *packed = contributions(
        where, col_block, live_count, cotangent, relu_mask, aggregated, weight, tiles, slabs, reps
    )
    aside, middle = lax.optimization_barrier((aside, middle))
    aside = lax.ppermute(aside, "blk", pair)
    two_in = lax.ppermute(two, "blk", to_two)
    one = add(one, aside)
    one_in = lax.ppermute(one, "blk", to_one)

    packed, _ = lax.optimization_barrier((packed, one))
    packed = [shift(value, s) for s, value in enumerate(packed)]
    shares = total_shares(where, aside, [own, one_in, two_in], reps)
    held, _ = lax.optimization_barrier((packed, shares))
    pieces = weight_partial(where, middle, held)
    pieces = [shift(value, -s) for s, value in enumerate(pieces)]
    shares = [shift(value, s) for s, value in enumerate(shares)]
    outs = [shift(value, s) for s, value in enumerate(mix(where, shares, packed))]
    input_grad = lay_blocks(where, outs, cotangent.shape)

    grad_w = sum(value.astype(F32) for value in pieces)
    grad_w = grad_w + lax.ppermute(grad_w, "blk", pair)
    parts = [
        lax.ppermute(grad_w, "blk", [(i, i ^ step) for i in range(slabs)])
        for step in range(2, slabs, 2)
    ]
    parts, _ = lax.optimization_barrier((parts, input_grad))
    grad_w = grad_w + sum(parts)
    grad_w = grad_w.transpose(1, 0, 2).reshape(features, width)
    return input_grad, grad_w * (1.0 / math.sqrt(slabs * blocks * nodes))


def solution(mesh):
    placed = (
        P("blk", "rep", None),
        P("blk", "rep", None),
        P("blk", "rep", None),
        P("rep", None),
        P("blk", None, None, None),
        P("blk", None),
        P("blk"),
    )
    return jax.shard_map(
        on_device,
        mesh=mesh,
        in_specs=placed,
        out_specs=(P("blk", "rep", None), P("rep", None)),
        check_vma=False,
    )
```

```python
import functools
import math

import jax
import jax.numpy as jnp
from jax import lax
from jax.experimental import pallas as pl
from jax.experimental.pallas import tpu as pltpu
from jax.sharding import PartitionSpec as P

REACH = 2
GROUP = 4
STEP = 16
BF16 = jnp.bfloat16
F32 = jnp.float32
MIB = 1 << 20


def vmem():
    return pl.BlockSpec(memory_space=pltpu.VMEM)


def smem():
    return pl.BlockSpec(memory_space=pltpu.SMEM)


def hbm():
    return pl.BlockSpec(memory_space=pl.ANY)


def in_hbm(value):
    return pltpu.with_memory_space_constraint(value, pltpu.HBM)


def wrap(value, size):
    if size & (size - 1):
        return lax.rem(value + size, size)
    return value & (size - 1)


def tiles_kernel(slabs, reps, where, cols, live, cot, mask, agg, weight, tiles, *rest):
    outs, packed, rest = rest[:4], rest[4 : 4 + reps], rest[4 + reps :]
    outs = [outs[0].at[pl.ds(0, cols.shape[1])], outs[0].at[pl.ds(cols.shape[1], cols.shape[1])], *outs[1:]]
    cot_in, mask_in, z, held, total, rows, left, sems, z_sems, agg_sems = rest
    share = cols.shape[1] // reps
    slots, blocks = cols.shape
    per_row = slots // GROUP
    window = (2 * REACH + 1) * blocks
    copies = [
        pltpu.make_async_copy(cot, cot_in, z_sems.at[0]),
        pltpu.make_async_copy(mask, mask_in, z_sems.at[1]),
    ]
    for copy in copies:
        copy.start()

    def groups_of(b):
        return lax.shift_right_logical(live[b] + GROUP - 1, GROUP.bit_length() - 1)

    def fetched(b, act):
        groups = groups_of(b)
        for g in range(1, per_row + 1):

            @pl.when(groups == g)
            def _(span=pl.ds(b * slots, g * GROUP)):
                act(pltpu.make_async_copy(tiles.at[span], held.at[span], sems.at[b]))

    def list_row(b, count):
        fetched(b, lambda copy: copy.start())
        for g in range(per_row):
            rows[count + g] = b * per_row + g
            left[count + g] = live[b] - g * GROUP
        return count + groups_of(b)

    count = lax.fori_loop(0, blocks, list_row, jnp.int32(0))
    for u in range(STEP):
        rows[count + u] = 0
        left[count + u] = 0
    steps = lax.div(count + STEP - 1, STEP)

    def wait_row(b, carry):
        fetched(b, lambda copy: copy.wait())
        return carry

    def clear(i, carry):
        total[pl.ds(i * GROUP, GROUP)] = jnp.zeros((GROUP,) + total.shape[1:], F32)
        return carry

    lax.fori_loop(0, window // GROUP, clear, 0)
    for copy in copies:
        copy.wait()

    def mask_row(b, carry):
        z[b] = cot_in[b] * mask_in[b].astype(BF16)
        return carry

    lax.fori_loop(0, blocks, mask_row, 0)
    agg_copies = []
    for s in range(reps):
        span = pl.ds(wrap(where[1] + s, reps) * share, share)
        packed[s][:share] = z[span]
        end = packed[s].at[pl.ds(share, share)]
        ends = [(agg.at[span], end)]
        for h in range(weight.shape[1] // z.shape[2]):
            columns = pl.ds(h * z.shape[2], z.shape[2])
            ends.append((weight.at[:, columns], packed[s].at[2 * share + h]))
        for source, target in ends:
            copy = pltpu.make_async_copy(source, target, agg_sems.at[len(agg_copies)])
            copy.start()
            agg_copies.append(copy)
    shift = REACH * blocks - where[0] * blocks

    def step(i, ready):
        entries = [rows[i * STEP + u] for u in range(STEP)]
        need = lax.div(functools.reduce(jnp.maximum, entries), per_row) + 1
        lax.fori_loop(ready, need, wait_row, 0)
        for u in range(STEP):
            row, remain = entries[u], left[i * STEP + u]
            b, g = lax.div(row, per_row), lax.rem(row, per_row)
            z_row = z[b]
            for j in range(GROUP):
                place = wrap(cols[g * GROUP + j, b] + shift, slabs * blocks)
                place = jnp.where(j < remain, place, window)
                total[place] += jnp.dot(
                    z_row, held[row * GROUP + j], preferred_element_type=F32
                )
        return jnp.maximum(ready, need)

    ready = lax.fori_loop(0, steps, step, jnp.int32(0))
    lax.fori_loop(ready, blocks, wait_row, 0)
    for copy in agg_copies:
        copy.wait()
    sign = 2 * lax.rem(where[0], 2) - 1
    for order, out in enumerate(outs):
        base = ((order - REACH) * sign + REACH) * blocks

        def store(i, carry, out=out, base=base):
            for k in range(GROUP):
                at = i * GROUP + k
                out[at] = total[base + at].astype(BF16)
            return carry

        lax.fori_loop(0, blocks // GROUP, store, 0)


def contributions(where, cols, live, cot, mask, agg, weight, tiles, slabs, reps):
    blocks, slots, nodes = tiles.shape[:3]
    features = cot.shape[1]
    window = (2 * REACH + 1) * blocks
    lists = blocks * (slots // GROUP) + slots // GROUP + STEP
    counts = [2 * blocks, blocks, blocks, blocks]
    halves = weight.shape[1] // nodes
    packs = 2 * blocks // reps + halves
    return pl.pallas_call(
        functools.partial(tiles_kernel, slabs, reps),
        out_shape=[jax.ShapeDtypeStruct((count, features, nodes), BF16) for count in counts]
        + [jax.ShapeDtypeStruct((packs, features, nodes), BF16)] * reps,
        in_specs=[smem()] * 3 + [hbm()] * 5,
        out_specs=[vmem()] * (len(counts) + reps),
        scratch_shapes=[
            pltpu.VMEM(cot.shape, BF16),
            pltpu.VMEM(mask.shape, jnp.int32),
            pltpu.VMEM(cot.shape, BF16),
            pltpu.VMEM((blocks * slots, nodes, nodes), BF16),
            pltpu.VMEM((window + 1, features, nodes), F32),
            pltpu.SMEM((lists,), jnp.int32),
            pltpu.SMEM((lists,), jnp.int32),
            pltpu.SemaphoreType.DMA((blocks,)),
            pltpu.SemaphoreType.DMA((2,)),
            pltpu.SemaphoreType.DMA((reps * (1 + halves),)),
        ],
        compiler_params=pltpu.CompilerParams(vmem_limit_bytes=30 * MIB),
        cost_estimate=pl.CostEstimate(
            flops=2 * blocks * slots * features * nodes * nodes,
            bytes_accessed=tiles.size * 2,
            transcendentals=0,
        ),
    )(
        where,
        in_hbm(cols.T),
        in_hbm(live),
        in_hbm(cot),
        in_hbm(mask),
        in_hbm(agg),
        in_hbm(weight),
        in_hbm(tiles.reshape(blocks * slots, nodes, nodes)),
    )


def order_of(reps):
    return sorted(range(reps), key=lambda s: (s == 0, abs(2 * s - reps), s))


def in_order(shares):
    return [shares[s] for s in order_of(len(shares))]


def by_distance(refs):
    return [refs[order_of(len(refs)).index(s)] for s in range(len(refs))]


def lay_features(where, shares, whole):
    reps, blocks = len(shares), whole.shape[0]
    features = shares[0].shape[1]
    for s in range(reps):
        first = pl.multiple_of(wrap(where[1] - s, reps) * features, features)
        whole[:, pl.ds(first, features), :] = shares[s][:blocks]


def mix_kernel(reps, where, *rest):
    shares, packed = by_distance(rest[:reps]), by_distance(rest[reps : 2 * reps])
    outs, (weights, whole) = rest[2 * reps : 3 * reps], rest[3 * reps :]
    blocks, features, nodes = outs[0].shape
    lay_features(where, shares, whole)
    for s in range(reps):
        for h in range(weights.shape[1] // nodes):
            rows, columns = pl.ds(s * features, features), pl.ds(h * nodes, nodes)
            weights[rows, columns] = packed[(reps - s) % reps][2 * blocks + h]
    for b in range(blocks):
        mixed = jnp.dot(weights[...], whole[b], preferred_element_type=F32)
        for s in range(reps):
            outs[s][b] = mixed[s * features : (s + 1) * features].astype(BF16)


def mix(where, shares, packed):
    reps = len(shares)
    blocks, features, nodes = shares[0].shape
    width = reps * features
    return pl.pallas_call(
        functools.partial(mix_kernel, reps),
        out_shape=[jax.ShapeDtypeStruct((blocks, features, nodes), BF16)] * reps,
        in_specs=[smem()] + [vmem()] * (2 * reps),
        out_specs=[vmem()] * reps,
        scratch_shapes=[pltpu.VMEM((width, width), BF16), pltpu.VMEM((blocks, width, nodes), BF16)],
        compiler_params=pltpu.CompilerParams(vmem_limit_bytes=4 * MIB),
        cost_estimate=pl.CostEstimate(
            flops=2 * blocks * nodes * width * width,
            bytes_accessed=4 * blocks * nodes * width,
            transcendentals=0,
        ),
    )(where, *in_order(shares), *in_order(packed))


def weight_kernel(reps, where, *rest):
    packed, outs = by_distance(rest[:reps]), rest[reps : 2 * reps]
    whole_z, whole_a = rest[2 * reps :]
    blocks, _, nodes = whole_z.shape
    features = packed[0].shape[1]
    lay_features(where, packed, whole_z)
    for s in range(reps):
        whole_a[:, pl.ds(s * features, features), :] = packed[s][blocks : 2 * blocks]
    total = jnp.zeros((whole_a.shape[1], whole_z.shape[1]), F32)
    for b in range(blocks):
        total += lax.dot_general(
            whole_a[b], whole_z[b], (((1,), (1,)), ((), ())), preferred_element_type=F32
        )
    for s in range(reps):
        for h in range(outs[s].shape[0]):
            part = total[s * features : (s + 1) * features, h * nodes : (h + 1) * nodes]
            outs[s][h] = part.astype(BF16)


def weight_partial(where, packed, blocks):
    reps = len(packed)
    _, features, nodes = packed[0].shape
    width = reps * features
    return pl.pallas_call(
        functools.partial(weight_kernel, reps),
        out_shape=[jax.ShapeDtypeStruct((width // nodes, features, nodes), BF16)] * reps,
        in_specs=[smem()] + [vmem()] * reps,
        out_specs=[vmem()] * reps,
        scratch_shapes=[pltpu.VMEM((blocks, width, nodes), BF16)] * 2,
        compiler_params=pltpu.CompilerParams(vmem_limit_bytes=4 * MIB),
        cost_estimate=pl.CostEstimate(
            flops=2 * blocks * nodes * width * width,
            bytes_accessed=4 * blocks * nodes * width + 2 * width * width,
            transcendentals=0,
        ),
    )(where, *in_order(packed))


def add_kernel(one, other, out):
    def row(i, carry):
        out[i] = (one[i].astype(F32) + other[i].astype(F32)).astype(BF16)
        return carry

    lax.fori_loop(0, out.shape[0], row, 0)


def add(one, other):
    return pl.pallas_call(
        add_kernel,
        out_shape=jax.ShapeDtypeStruct(one.shape, BF16),
        in_specs=[vmem()] * 2,
        out_specs=vmem(),
        compiler_params=pltpu.CompilerParams(vmem_limit_bytes=2 * MIB),
        cost_estimate=pl.CostEstimate(
            flops=one.size, bytes_accessed=6 * one.size, transcendentals=0
        ),
    )(one, other)


def total_kernel(reps, where, aside, *rest):
    terms, outs = rest[:-reps], rest[-reps:]
    terms = (aside.at[pl.ds(terms[0].shape[0], terms[0].shape[0])], *terms)
    share = outs[0].shape[0]
    for s, out in enumerate(outs):
        first = wrap(where[1] + s, reps) * share
        for i in range(share):
            total = terms[0][first + i].astype(F32)
            for term in terms[1:]:
                total += term[first + i].astype(F32)
            out[i] = total.astype(BF16)


def total_shares(where, aside, terms, reps):
    blocks, features, nodes = terms[0].shape
    return pl.pallas_call(
        functools.partial(total_kernel, reps),
        out_shape=[jax.ShapeDtypeStruct((blocks // reps, features, nodes), BF16)] * reps,
        in_specs=[smem()] + [vmem()] * (1 + len(terms)),
        out_specs=[vmem()] * reps,
        compiler_params=pltpu.CompilerParams(vmem_limit_bytes=2 * MIB),
        cost_estimate=pl.CostEstimate(
            flops=4 * terms[0].size, bytes_accessed=10 * terms[0].size, transcendentals=0
        ),
    )(where, aside, *terms)


def lay_kernel(reps, where, *rest):
    shares, out, sems = by_distance(rest[:reps]), rest[reps], rest[reps + 1]
    blocks = shares[0].shape[0]
    copies = []
    for s in range(reps):
        first = wrap(where[1] - s, reps) * blocks
        copies.append(pltpu.make_async_copy(shares[s], out.at[pl.ds(first, blocks)], sems.at[s]))
        copies[s].start()
    for copy in copies:
        copy.wait()


def lay_blocks(where, shares, shape):
    reps = len(shares)
    return pl.pallas_call(
        functools.partial(lay_kernel, reps),
        out_shape=jax.ShapeDtypeStruct(shape, BF16),
        in_specs=[smem()] + [vmem()] * reps,
        out_specs=hbm(),
        scratch_shapes=[pltpu.SemaphoreType.DMA((reps,))],
        compiler_params=pltpu.CompilerParams(vmem_limit_bytes=2 * MIB),
        cost_estimate=pl.CostEstimate(flops=0, bytes_accessed=32 * MIB, transcendentals=0),
    )(where, *in_order(shares))


def shift(value, steps):
    reps = lax.axis_size("rep")
    if steps % reps == 0:
        return value
    return lax.ppermute(value, "rep", [(i, (i + steps) % reps) for i in range(reps)])


def exchange(shares, sign=1):
    return [shift(value, sign * s) for s, value in enumerate(shares)]


def on_device(cotangent, relu_mask, aggregated, weight, tiles, col_block, live_count):
    blocks, features, nodes = cotangent.shape
    slabs, reps = lax.axis_size("blk"), lax.axis_size("rep")
    width = weight.shape[1]
    where = jnp.stack([lax.axis_index("blk"), lax.axis_index("rep")]).astype(jnp.int32)

    pair = [(i, i ^ 1) for i in range(slabs)]
    to_one = [(i, (i + (1 if i % 2 else -1)) % slabs) for i in range(slabs)]
    to_two = [(i, (i + (2 if i % 2 else -2)) % slabs) for i in range(slabs)]
    aside, own, one, two, *packed = contributions(
        where, col_block, live_count, cotangent, relu_mask, aggregated, weight, tiles, slabs, reps
    )
    aside = lax.ppermute(aside, "blk", pair)
    two_in = lax.ppermute(two, "blk", to_two)
    one = add(one, aside)
    one_in = lax.ppermute(one, "blk", to_one)

    packed, _ = lax.optimization_barrier((packed, one))
    packed = exchange(packed)
    shares = total_shares(where, aside, [own, one_in, two_in], reps)
    held, _ = lax.optimization_barrier((packed, shares))
    pieces = weight_partial(where, held, blocks // reps)
    pieces = exchange(pieces, -1)
    shares = exchange(shares)
    outs = exchange(mix(where, shares, packed))
    input_grad = lay_blocks(where, outs, cotangent.shape)

    grad_w = sum(value.astype(F32) for value in pieces)
    grad_w = grad_w + lax.ppermute(grad_w, "blk", pair)
    parts = [
        lax.ppermute(grad_w, "blk", [(i, i ^ step) for i in range(slabs)])
        for step in range(2, slabs, 2)
    ]
    parts, _ = lax.optimization_barrier((parts, input_grad))
    grad_w = grad_w + sum(parts)
    grad_w = grad_w.transpose(1, 0, 2).reshape(features, width)
    return input_grad, grad_w * (1.0 / math.sqrt(slabs * blocks * nodes))


def solution(mesh):
    placed = (
        P("blk", "rep", None),
        P("blk", "rep", None),
        P("blk", "rep", None),
        P("rep", None),
        P("blk", None, None, None),
        P("blk", None),
        P("blk"),
    )
    return jax.shard_map(
        on_device,
        mesh=mesh,
        in_specs=placed,
        out_specs=(P("blk", "rep", None), P("rep", None)),
        check_vma=False,
    )
```

```python
import functools
import math

import jax
import jax.numpy as jnp
from jax import lax
from jax.experimental import pallas as pl
from jax.experimental.pallas import tpu as pltpu
from jax.sharding import PartitionSpec as P

REACH = 2
GROUP = 4
STEP = 8
BF16 = jnp.bfloat16
F32 = jnp.float32
MIB = 1 << 20


def vmem():
    return pl.BlockSpec(memory_space=pltpu.VMEM)


def smem():
    return pl.BlockSpec(memory_space=pltpu.SMEM)


def hbm():
    return pl.BlockSpec(memory_space=pl.ANY)


def in_hbm(value):
    return pltpu.with_memory_space_constraint(value, pltpu.HBM)


def wrap(value, size):
    if size & (size - 1):
        return lax.rem(value + size, size)
    return value & (size - 1)


def tiles_kernel(slabs, reps, where, cols, live, cot, mask, agg, weight, tiles, *rest):
    outs, packed, rest = rest[:4], rest[4 : 4 + reps], rest[4 + reps :]
    outs = [outs[0].at[pl.ds(0, cols.shape[1])], outs[0].at[pl.ds(cols.shape[1], cols.shape[1])], *outs[1:]]
    cot_in, mask_in, z, held, first, second, rows, left, sems, z_sems, agg_sems = rest
    totals = (first, second)
    share = cols.shape[1] // reps
    slots, blocks = cols.shape
    per_row = slots // GROUP
    window = (2 * REACH + 1) * blocks
    copies = [
        pltpu.make_async_copy(cot, cot_in, z_sems.at[0]),
        pltpu.make_async_copy(mask, mask_in, z_sems.at[1]),
    ]
    for copy in copies:
        copy.start()

    def groups_of(b):
        return lax.shift_right_logical(live[b] + GROUP - 1, GROUP.bit_length() - 1)

    def fetched(b, act):
        groups = groups_of(b)
        for g in range(1, per_row + 1):

            @pl.when(groups == g)
            def _(span=pl.ds(b * slots, g * GROUP)):
                act(pltpu.make_async_copy(tiles.at[span], held.at[span], sems.at[b]))

    def list_rows(i, count):
        for k in range(2):
            b = 2 * i + k
            fetched(b, lambda copy, k=k: copy.start(priority=k))
            for g in range(per_row):
                rows[count + g] = b * per_row + g
                left[count + g] = live[b] - g * GROUP
            count += groups_of(b)
        return count

    count = lax.fori_loop(0, blocks // 2, list_rows, jnp.int32(0))
    for u in range(STEP):
        rows[count + u] = 0
        left[count + u] = 0
    steps = lax.div(count + STEP - 1, STEP)

    def wait_row(b, carry):
        fetched(b, lambda copy: copy.wait())
        return carry

    def clear(i, carry):
        for total in totals:
            total[pl.ds(i * GROUP, GROUP)] = jnp.zeros((GROUP,) + total.shape[1:], F32)
        return carry

    lax.fori_loop(0, window // GROUP, clear, 0)
    for copy in copies:
        copy.wait()

    def mask_row(b, carry):
        z[b] = cot_in[b] * mask_in[b].astype(BF16)
        return carry

    lax.fori_loop(0, blocks, mask_row, 0)
    agg_copies = []
    for s in range(reps):
        span = pl.ds(wrap(where[1] + s, reps) * share, share)
        packed[s][:share] = z[span]
        end = packed[s].at[pl.ds(share, share)]
        ends = [(agg.at[span], end)]
        for h in range(weight.shape[1] // z.shape[2]):
            columns = pl.ds(h * z.shape[2], z.shape[2])
            ends.append((weight.at[:, columns], packed[s].at[2 * share + h]))
        for source, target in ends:
            copy = pltpu.make_async_copy(source, target, agg_sems.at[len(agg_copies)])
            copy.start()
            agg_copies.append(copy)
    shift = REACH * blocks - where[0] * blocks

    def step(i, ready):
        entries = [rows[i * STEP + u] for u in range(STEP)]
        need = lax.div(functools.reduce(jnp.maximum, entries), per_row) + 1
        lax.fori_loop(ready, need, wait_row, 0)
        for u in range(STEP):
            row, remain = entries[u], left[i * STEP + u]
            b, g = lax.div(row, per_row), lax.rem(row, per_row)
            z_row = z[b]
            for j in range(GROUP):
                place = wrap(cols[g * GROUP + j, b] + shift, slabs * blocks)
                place = jnp.where(j < remain, place, window)
                totals[j % 2][place] += jnp.dot(
                    z_row, held[row * GROUP + j], preferred_element_type=F32
                )
        return jnp.maximum(ready, need)

    ready = lax.fori_loop(0, steps, step, jnp.int32(0))
    lax.fori_loop(ready, blocks, wait_row, 0)
    for copy in agg_copies:
        copy.wait()
    sign = 2 * lax.rem(where[0], 2) - 1
    for order, out in enumerate(outs):
        base = ((order - REACH) * sign + REACH) * blocks

        def store(i, carry, out=out, base=base):
            for k in range(GROUP):
                at = i * GROUP + k
                out[at] = (first[base + at] + second[base + at]).astype(BF16)
            return carry

        lax.fori_loop(0, blocks // GROUP, store, 0)


def contributions(where, cols, live, cot, mask, agg, weight, tiles, slabs, reps):
    blocks, slots, nodes = tiles.shape[:3]
    features = cot.shape[1]
    window = (2 * REACH + 1) * blocks
    lists = blocks * (slots // GROUP) + slots // GROUP + STEP
    counts = [2 * blocks, blocks, blocks, blocks]
    halves = weight.shape[1] // nodes
    packs = 2 * blocks // reps + halves
    return pl.pallas_call(
        functools.partial(tiles_kernel, slabs, reps),
        out_shape=[jax.ShapeDtypeStruct((count, features, nodes), BF16) for count in counts]
        + [jax.ShapeDtypeStruct((packs, features, nodes), BF16)] * reps,
        in_specs=[smem()] * 3 + [hbm()] * 5,
        out_specs=[vmem()] * (len(counts) + reps),
        scratch_shapes=[
            pltpu.VMEM(cot.shape, BF16),
            pltpu.VMEM(mask.shape, jnp.int32),
            pltpu.VMEM(cot.shape, BF16),
            pltpu.VMEM((blocks * slots, nodes, nodes), BF16),
            pltpu.VMEM((window + 1, features, nodes), F32),
            pltpu.VMEM((window + 1, features, nodes), F32),
            pltpu.SMEM((lists,), jnp.int32),
            pltpu.SMEM((lists,), jnp.int32),
            pltpu.SemaphoreType.DMA((blocks,)),
            pltpu.SemaphoreType.DMA((2,)),
            pltpu.SemaphoreType.DMA((reps * (1 + halves),)),
        ],
        compiler_params=pltpu.CompilerParams(vmem_limit_bytes=36 * MIB),
        cost_estimate=pl.CostEstimate(
            flops=2 * blocks * slots * features * nodes * nodes,
            bytes_accessed=tiles.size * 2,
            transcendentals=0,
        ),
    )(
        where,
        in_hbm(cols.T),
        in_hbm(live),
        in_hbm(cot),
        in_hbm(mask),
        in_hbm(agg),
        in_hbm(weight),
        in_hbm(tiles.reshape(blocks * slots, nodes, nodes)),
    )


def lay_features(where, shares, whole):
    reps, blocks = len(shares), whole.shape[0]
    features = shares[0].shape[1]
    for s in range(reps):
        first = pl.multiple_of(wrap(where[1] - s, reps) * features, features)
        whole[:, pl.ds(first, features), :] = shares[s][:blocks]


def mix_kernel(reps, where, *rest):
    shares, packed, outs = rest[:reps], rest[reps : 2 * reps], rest[2 * reps : 3 * reps]
    weights, whole = rest[3 * reps :]
    blocks, features, nodes = outs[0].shape
    lay_features(where, shares, whole)
    for s in range(reps):
        for h in range(weights.shape[1] // nodes):
            rows, columns = pl.ds(s * features, features), pl.ds(h * nodes, nodes)
            weights[rows, columns] = packed[(reps - s) % reps][2 * blocks + h]
    for b in range(blocks):
        mixed = jnp.dot(weights[...], whole[b], preferred_element_type=F32)
        for s in range(reps):
            outs[s][b] = mixed[s * features : (s + 1) * features].astype(BF16)


def mix(where, shares, packed):
    reps = len(shares)
    blocks, features, nodes = shares[0].shape
    width = reps * features
    return pl.pallas_call(
        functools.partial(mix_kernel, reps),
        out_shape=[jax.ShapeDtypeStruct((blocks, features, nodes), BF16)] * reps,
        in_specs=[smem()] + [vmem()] * (2 * reps),
        out_specs=[vmem()] * reps,
        scratch_shapes=[pltpu.VMEM((width, width), BF16), pltpu.VMEM((blocks, width, nodes), BF16)],
        compiler_params=pltpu.CompilerParams(vmem_limit_bytes=4 * MIB),
        cost_estimate=pl.CostEstimate(
            flops=2 * blocks * nodes * width * width,
            bytes_accessed=4 * blocks * nodes * width,
            transcendentals=0,
        ),
    )(where, *shares, *packed)


def weight_kernel(reps, where, *rest):
    packed, outs, (whole_z, whole_a) = rest[:reps], rest[reps : 2 * reps], rest[2 * reps :]
    blocks, _, nodes = whole_z.shape
    features = packed[0].shape[1]
    lay_features(where, packed, whole_z)
    for s in range(reps):
        whole_a[:, pl.ds(s * features, features), :] = packed[s][blocks : 2 * blocks]
    total = jnp.zeros((whole_a.shape[1], whole_z.shape[1]), F32)
    for b in range(blocks):
        total += lax.dot_general(
            whole_a[b], whole_z[b], (((1,), (1,)), ((), ())), preferred_element_type=F32
        )
    for s in range(reps):
        for h in range(outs[s].shape[0]):
            part = total[s * features : (s + 1) * features, h * nodes : (h + 1) * nodes]
            outs[s][h] = part.astype(BF16)


def weight_partial(where, packed, blocks):
    reps = len(packed)
    _, features, nodes = packed[0].shape
    width = reps * features
    return pl.pallas_call(
        functools.partial(weight_kernel, reps),
        out_shape=[jax.ShapeDtypeStruct((width // nodes, features, nodes), BF16)] * reps,
        in_specs=[smem()] + [vmem()] * reps,
        out_specs=[vmem()] * reps,
        scratch_shapes=[pltpu.VMEM((blocks, width, nodes), BF16)] * 2,
        compiler_params=pltpu.CompilerParams(vmem_limit_bytes=4 * MIB),
        cost_estimate=pl.CostEstimate(
            flops=2 * blocks * nodes * width * width,
            bytes_accessed=4 * blocks * nodes * width + 2 * width * width,
            transcendentals=0,
        ),
    )(where, *packed)


def add_kernel(one, other, out):
    def row(i, carry):
        out[i] = (one[i].astype(F32) + other[i].astype(F32)).astype(BF16)
        return carry

    lax.fori_loop(0, out.shape[0], row, 0)


def add(one, other):
    return pl.pallas_call(
        add_kernel,
        out_shape=jax.ShapeDtypeStruct(one.shape, BF16),
        in_specs=[vmem()] * 2,
        out_specs=vmem(),
        compiler_params=pltpu.CompilerParams(vmem_limit_bytes=2 * MIB),
        cost_estimate=pl.CostEstimate(
            flops=one.size, bytes_accessed=6 * one.size, transcendentals=0
        ),
    )(one, other)


def total_kernel(reps, where, aside, *rest):
    terms, outs = rest[:-reps], rest[-reps:]
    terms = (aside.at[pl.ds(terms[0].shape[0], terms[0].shape[0])], *terms)
    share = outs[0].shape[0]
    for s, out in enumerate(outs):
        first = wrap(where[1] + s, reps) * share
        for i in range(share):
            total = terms[0][first + i].astype(F32)
            for term in terms[1:]:
                total += term[first + i].astype(F32)
            out[i] = total.astype(BF16)


def total_shares(where, aside, terms, reps):
    blocks, features, nodes = terms[0].shape
    return pl.pallas_call(
        functools.partial(total_kernel, reps),
        out_shape=[jax.ShapeDtypeStruct((blocks // reps, features, nodes), BF16)] * reps,
        in_specs=[smem()] + [vmem()] * (1 + len(terms)),
        out_specs=[vmem()] * reps,
        compiler_params=pltpu.CompilerParams(vmem_limit_bytes=2 * MIB),
        cost_estimate=pl.CostEstimate(
            flops=4 * terms[0].size, bytes_accessed=10 * terms[0].size, transcendentals=0
        ),
    )(where, aside, *terms)


def lay_kernel(reps, where, *rest):
    shares, out, sems = rest[:reps], rest[reps], rest[reps + 1]
    blocks = shares[0].shape[0]
    copies = []
    for s in range(reps):
        first = wrap(where[1] - s, reps) * blocks
        copies.append(pltpu.make_async_copy(shares[s], out.at[pl.ds(first, blocks)], sems.at[s]))
        copies[s].start()
    for copy in copies:
        copy.wait()


def lay_blocks(where, shares, shape):
    reps = len(shares)
    return pl.pallas_call(
        functools.partial(lay_kernel, reps),
        out_shape=jax.ShapeDtypeStruct(shape, BF16),
        in_specs=[smem()] + [vmem()] * reps,
        out_specs=hbm(),
        scratch_shapes=[pltpu.SemaphoreType.DMA((reps,))],
        compiler_params=pltpu.CompilerParams(vmem_limit_bytes=2 * MIB),
        cost_estimate=pl.CostEstimate(flops=0, bytes_accessed=32 * MIB, transcendentals=0),
    )(where, *shares)


def shift(value, steps):
    reps = lax.axis_size("rep")
    if steps % reps == 0:
        return value
    return lax.ppermute(value, "rep", [(i, (i + steps) % reps) for i in range(reps)])


def on_device(cotangent, relu_mask, aggregated, weight, tiles, col_block, live_count):
    blocks, features, nodes = cotangent.shape
    slabs, reps = lax.axis_size("blk"), lax.axis_size("rep")
    width = weight.shape[1]
    where = jnp.stack([lax.axis_index("blk"), lax.axis_index("rep")]).astype(jnp.int32)

    pair = [(i, i ^ 1) for i in range(slabs)]
    to_one = [(i, (i + (1 if i % 2 else -1)) % slabs) for i in range(slabs)]
    to_two = [(i, (i + (2 if i % 2 else -2)) % slabs) for i in range(slabs)]
    aside, own, one, two, *packed = contributions(
        where, col_block, live_count, cotangent, relu_mask, aggregated, weight, tiles, slabs, reps
    )
    aside = lax.ppermute(aside, "blk", pair)
    two_in = lax.ppermute(two, "blk", to_two)
    one = add(one, aside)
    one_in = lax.ppermute(one, "blk", to_one)

    packed, _ = lax.optimization_barrier((packed, one))
    packed = [shift(value, s) for s, value in enumerate(packed)]
    shares = total_shares(where, aside, [own, one_in, two_in], reps)
    held, _ = lax.optimization_barrier((packed, shares))
    pieces = weight_partial(where, held, blocks // reps)
    pieces = [shift(value, -s) for s, value in enumerate(pieces)]
    shares = [shift(value, s) for s, value in enumerate(shares)]
    outs = [shift(value, s) for s, value in enumerate(mix(where, shares, packed))]
    input_grad = lay_blocks(where, outs, cotangent.shape)

    grad_w = sum(value.astype(F32) for value in pieces)
    grad_w = grad_w + lax.ppermute(grad_w, "blk", pair)
    parts = [
        lax.ppermute(grad_w, "blk", [(i, i ^ step) for i in range(slabs)])
        for step in range(2, slabs, 2)
    ]
    parts, _ = lax.optimization_barrier((parts, input_grad))
    grad_w = grad_w + sum(parts)
    grad_w = grad_w.transpose(1, 0, 2).reshape(features, width)
    return input_grad, grad_w * (1.0 / math.sqrt(slabs * blocks * nodes))


def solution(mesh):
    placed = (
        P("blk", "rep", None),
        P("blk", "rep", None),
        P("blk", "rep", None),
        P("rep", None),
        P("blk", None, None, None),
        P("blk", None),
        P("blk"),
    )
    return jax.shard_map(
        on_device,
        mesh=mesh,
        in_specs=placed,
        out_specs=(P("blk", "rep", None), P("rep", None)),
        check_vma=False,
    )
```

```python
import functools
import math

import jax
import jax.numpy as jnp
from jax import lax
from jax.experimental import pallas as pl
from jax.experimental.pallas import tpu as pltpu
from jax.sharding import PartitionSpec as P

REACH = 2
GROUP = 4
STEP = 8
BF16 = jnp.bfloat16
F32 = jnp.float32
MIB = 1 << 20


def vmem():
    return pl.BlockSpec(memory_space=pltpu.VMEM)


def smem():
    return pl.BlockSpec(memory_space=pltpu.SMEM)


def hbm():
    return pl.BlockSpec(memory_space=pl.ANY)


def in_hbm(value):
    return pltpu.with_memory_space_constraint(value, pltpu.HBM)


def wrap(value, size):
    if size & (size - 1):
        return lax.rem(value + size, size)
    return value & (size - 1)


def tiles_kernel(slabs, reps, where, cols, live, cot, mask, agg, weight, tiles, *rest):
    outs, packed, rest = rest[:4], rest[4 : 4 + reps], rest[4 + reps :]
    outs = [outs[0].at[pl.ds(0, cols.shape[1])], outs[0].at[pl.ds(cols.shape[1], cols.shape[1])], *outs[1:]]
    cot_in, mask_in, z, held, total, rows, left, sems, z_sems, agg_sems = rest
    share = cols.shape[1] // reps
    slots, blocks = cols.shape
    per_row = slots // GROUP
    window = (2 * REACH + 1) * blocks
    copies = [
        pltpu.make_async_copy(cot, cot_in, z_sems.at[0]),
        pltpu.make_async_copy(mask, mask_in, z_sems.at[1]),
    ]
    for copy in copies:
        copy.start()

    def groups_of(b):
        return lax.shift_right_logical(live[b] + GROUP - 1, GROUP.bit_length() - 1)

    half = slots // 2

    def fetched(b, act):
        span = pl.ds(b * slots, half)
        act(pltpu.make_async_copy(tiles.at[span], held.at[span], sems.at[b, 0]))

        @pl.when(live[b] > half)
        def _():
            span = pl.ds(b * slots + half, half)
            act(pltpu.make_async_copy(tiles.at[span], held.at[span], sems.at[b, 1]))

    def list_row(b, count):
        fetched(b, lambda copy: copy.start())
        for g in range(per_row):
            rows[count + g] = b * per_row + g
            left[count + g] = live[b] - g * GROUP
        return count + groups_of(b)

    count = lax.fori_loop(0, blocks, list_row, jnp.int32(0))
    for u in range(STEP):
        rows[count + u] = 0
        left[count + u] = 0
    steps = lax.div(count + STEP - 1, STEP)

    def wait_row(b, carry):
        fetched(b, lambda copy: copy.wait())
        return carry

    def clear(i, carry):
        total[pl.ds(i * GROUP, GROUP)] = jnp.zeros((GROUP,) + total.shape[1:], F32)
        return carry

    lax.fori_loop(0, window // GROUP, clear, 0)
    for copy in copies:
        copy.wait()

    def mask_row(b, carry):
        z[b] = cot_in[b] * mask_in[b].astype(BF16)
        return carry

    lax.fori_loop(0, blocks, mask_row, 0)
    agg_copies = []
    for s in range(reps):
        span = pl.ds(wrap(where[1] + s, reps) * share, share)
        packed[s][:share] = z[span]
        end = packed[s].at[pl.ds(share, share)]
        ends = [(agg.at[span], end)]
        for h in range(weight.shape[1] // z.shape[2]):
            columns = pl.ds(h * z.shape[2], z.shape[2])
            ends.append((weight.at[:, columns], packed[s].at[2 * share + h]))
        for source, target in ends:
            copy = pltpu.make_async_copy(source, target, agg_sems.at[len(agg_copies)])
            copy.start()
            agg_copies.append(copy)
    shift = REACH * blocks - where[0] * blocks

    def step(i, ready):
        entries = [rows[i * STEP + u] for u in range(STEP)]
        need = lax.div(functools.reduce(jnp.maximum, entries), per_row) + 1
        lax.fori_loop(ready, need, wait_row, 0)
        for u in range(STEP):
            row, remain = entries[u], left[i * STEP + u]
            b, g = lax.div(row, per_row), lax.rem(row, per_row)
            z_row = z[b]
            for j in range(GROUP):
                place = wrap(cols[g * GROUP + j, b] + shift, slabs * blocks)
                place = jnp.where(j < remain, place, window)
                total[place] += jnp.dot(
                    z_row, held[row * GROUP + j], preferred_element_type=F32
                )
        return jnp.maximum(ready, need)

    ready = lax.fori_loop(0, steps, step, jnp.int32(0))
    lax.fori_loop(ready, blocks, wait_row, 0)
    for copy in agg_copies:
        copy.wait()
    sign = 2 * lax.rem(where[0], 2) - 1
    for order, out in enumerate(outs):
        base = ((order - REACH) * sign + REACH) * blocks

        def store(i, carry, out=out, base=base):
            for k in range(GROUP):
                at = i * GROUP + k
                out[at] = total[base + at].astype(BF16)
            return carry

        lax.fori_loop(0, blocks // GROUP, store, 0)


def contributions(where, cols, live, cot, mask, agg, weight, tiles, slabs, reps):
    blocks, slots, nodes = tiles.shape[:3]
    features = cot.shape[1]
    window = (2 * REACH + 1) * blocks
    lists = blocks * (slots // GROUP) + slots // GROUP + STEP
    counts = [2 * blocks, blocks, blocks, blocks]
    halves = weight.shape[1] // nodes
    packs = 2 * blocks // reps + halves
    return pl.pallas_call(
        functools.partial(tiles_kernel, slabs, reps),
        out_shape=[jax.ShapeDtypeStruct((count, features, nodes), BF16) for count in counts]
        + [jax.ShapeDtypeStruct((packs, features, nodes), BF16)] * reps,
        in_specs=[smem()] * 3 + [hbm()] * 5,
        out_specs=[vmem()] * (len(counts) + reps),
        scratch_shapes=[
            pltpu.VMEM(cot.shape, BF16),
            pltpu.VMEM(mask.shape, jnp.int32),
            pltpu.VMEM(cot.shape, BF16),
            pltpu.VMEM((blocks * slots, nodes, nodes), BF16),
            pltpu.VMEM((window + 1, features, nodes), F32),
            pltpu.SMEM((lists,), jnp.int32),
            pltpu.SMEM((lists,), jnp.int32),
            pltpu.SemaphoreType.DMA((blocks, 2)),
            pltpu.SemaphoreType.DMA((2,)),
            pltpu.SemaphoreType.DMA((reps * (1 + halves),)),
        ],
        compiler_params=pltpu.CompilerParams(vmem_limit_bytes=30 * MIB),
        cost_estimate=pl.CostEstimate(
            flops=2 * blocks * slots * features * nodes * nodes,
            bytes_accessed=tiles.size * 2,
            transcendentals=0,
        ),
    )(
        where,
        in_hbm(cols.T),
        in_hbm(live),
        in_hbm(cot),
        in_hbm(mask),
        in_hbm(agg),
        in_hbm(weight),
        in_hbm(tiles.reshape(blocks * slots, nodes, nodes)),
    )


def lay_features(where, shares, whole):
    reps, blocks = len(shares), whole.shape[0]
    features = shares[0].shape[1]
    for s in range(reps):
        first = pl.multiple_of(wrap(where[1] - s, reps) * features, features)
        whole[:, pl.ds(first, features), :] = shares[s][:blocks]


def mix_kernel(reps, where, *rest):
    shares, packed, outs = rest[:reps], rest[reps : 2 * reps], rest[2 * reps : 3 * reps]
    weights, whole = rest[3 * reps :]
    blocks, features, nodes = outs[0].shape
    lay_features(where, shares, whole)
    for s in range(reps):
        for h in range(weights.shape[1] // nodes):
            rows, columns = pl.ds(s * features, features), pl.ds(h * nodes, nodes)
            weights[rows, columns] = packed[(reps - s) % reps][2 * blocks + h]
    for b in range(blocks):
        mixed = jnp.dot(weights[...], whole[b], preferred_element_type=F32)
        for s in range(reps):
            outs[s][b] = mixed[s * features : (s + 1) * features].astype(BF16)


def mix(where, shares, packed):
    reps = len(shares)
    blocks, features, nodes = shares[0].shape
    width = reps * features
    return pl.pallas_call(
        functools.partial(mix_kernel, reps),
        out_shape=[jax.ShapeDtypeStruct((blocks, features, nodes), BF16)] * reps,
        in_specs=[smem()] + [vmem()] * (2 * reps),
        out_specs=[vmem()] * reps,
        scratch_shapes=[pltpu.VMEM((width, width), BF16), pltpu.VMEM((blocks, width, nodes), BF16)],
        compiler_params=pltpu.CompilerParams(vmem_limit_bytes=4 * MIB),
        cost_estimate=pl.CostEstimate(
            flops=2 * blocks * nodes * width * width,
            bytes_accessed=4 * blocks * nodes * width,
            transcendentals=0,
        ),
    )(where, *shares, *packed)


def weight_kernel(reps, where, *rest):
    packed, outs, (whole_z, whole_a) = rest[:reps], rest[reps : 2 * reps], rest[2 * reps :]
    blocks, _, nodes = whole_z.shape
    features = packed[0].shape[1]
    lay_features(where, packed, whole_z)
    for s in range(reps):
        whole_a[:, pl.ds(s * features, features), :] = packed[s][blocks : 2 * blocks]
    total = jnp.zeros((whole_a.shape[1], whole_z.shape[1]), F32)
    for b in range(blocks):
        total += lax.dot_general(
            whole_a[b], whole_z[b], (((1,), (1,)), ((), ())), preferred_element_type=F32
        )
    for s in range(reps):
        for h in range(outs[s].shape[0]):
            part = total[s * features : (s + 1) * features, h * nodes : (h + 1) * nodes]
            outs[s][h] = part.astype(BF16)


def weight_partial(where, packed, blocks):
    reps = len(packed)
    _, features, nodes = packed[0].shape
    width = reps * features
    return pl.pallas_call(
        functools.partial(weight_kernel, reps),
        out_shape=[jax.ShapeDtypeStruct((width // nodes, features, nodes), BF16)] * reps,
        in_specs=[smem()] + [vmem()] * reps,
        out_specs=[vmem()] * reps,
        scratch_shapes=[pltpu.VMEM((blocks, width, nodes), BF16)] * 2,
        compiler_params=pltpu.CompilerParams(vmem_limit_bytes=4 * MIB),
        cost_estimate=pl.CostEstimate(
            flops=2 * blocks * nodes * width * width,
            bytes_accessed=4 * blocks * nodes * width + 2 * width * width,
            transcendentals=0,
        ),
    )(where, *packed)


def add_kernel(one, other, out):
    def row(i, carry):
        out[i] = (one[i].astype(F32) + other[i].astype(F32)).astype(BF16)
        return carry

    lax.fori_loop(0, out.shape[0], row, 0)


def add(one, other):
    return pl.pallas_call(
        add_kernel,
        out_shape=jax.ShapeDtypeStruct(one.shape, BF16),
        in_specs=[vmem()] * 2,
        out_specs=vmem(),
        compiler_params=pltpu.CompilerParams(vmem_limit_bytes=2 * MIB),
        cost_estimate=pl.CostEstimate(
            flops=one.size, bytes_accessed=6 * one.size, transcendentals=0
        ),
    )(one, other)


def total_kernel(reps, where, aside, *rest):
    terms, outs = rest[:-reps], rest[-reps:]
    terms = (aside.at[pl.ds(terms[0].shape[0], terms[0].shape[0])], *terms)
    share = outs[0].shape[0]
    for s, out in enumerate(outs):
        first = wrap(where[1] + s, reps) * share
        for i in range(share):
            total = terms[0][first + i].astype(F32)
            for term in terms[1:]:
                total += term[first + i].astype(F32)
            out[i] = total.astype(BF16)


def total_shares(where, aside, terms, reps):
    blocks, features, nodes = terms[0].shape
    return pl.pallas_call(
        functools.partial(total_kernel, reps),
        out_shape=[jax.ShapeDtypeStruct((blocks // reps, features, nodes), BF16)] * reps,
        in_specs=[smem()] + [vmem()] * (1 + len(terms)),
        out_specs=[vmem()] * reps,
        compiler_params=pltpu.CompilerParams(vmem_limit_bytes=2 * MIB),
        cost_estimate=pl.CostEstimate(
            flops=4 * terms[0].size, bytes_accessed=10 * terms[0].size, transcendentals=0
        ),
    )(where, aside, *terms)


def lay_kernel(reps, where, *rest):
    shares, out, sems = rest[:reps], rest[reps], rest[reps + 1]
    blocks = shares[0].shape[0]
    copies = []
    for s in range(reps):
        first = wrap(where[1] - s, reps) * blocks
        copies.append(pltpu.make_async_copy(shares[s], out.at[pl.ds(first, blocks)], sems.at[s]))
        copies[s].start()
    for copy in copies:
        copy.wait()


def lay_blocks(where, shares, shape):
    reps = len(shares)
    return pl.pallas_call(
        functools.partial(lay_kernel, reps),
        out_shape=jax.ShapeDtypeStruct(shape, BF16),
        in_specs=[smem()] + [vmem()] * reps,
        out_specs=hbm(),
        scratch_shapes=[pltpu.SemaphoreType.DMA((reps,))],
        compiler_params=pltpu.CompilerParams(vmem_limit_bytes=2 * MIB),
        cost_estimate=pl.CostEstimate(flops=0, bytes_accessed=32 * MIB, transcendentals=0),
    )(where, *shares)


def shift(value, steps):
    reps = lax.axis_size("rep")
    if steps % reps == 0:
        return value
    return lax.ppermute(value, "rep", [(i, (i + steps) % reps) for i in range(reps)])


def on_device(cotangent, relu_mask, aggregated, weight, tiles, col_block, live_count):
    blocks, features, nodes = cotangent.shape
    slabs, reps = lax.axis_size("blk"), lax.axis_size("rep")
    width = weight.shape[1]
    where = jnp.stack([lax.axis_index("blk"), lax.axis_index("rep")]).astype(jnp.int32)

    pair = [(i, i ^ 1) for i in range(slabs)]
    to_one = [(i, (i + (1 if i % 2 else -1)) % slabs) for i in range(slabs)]
    to_two = [(i, (i + (2 if i % 2 else -2)) % slabs) for i in range(slabs)]
    aside, own, one, two, *packed = contributions(
        where, col_block, live_count, cotangent, relu_mask, aggregated, weight, tiles, slabs, reps
    )
    aside = lax.ppermute(aside, "blk", pair)
    two_in = lax.ppermute(two, "blk", to_two)
    one = add(one, aside)
    one_in = lax.ppermute(one, "blk", to_one)

    packed, _ = lax.optimization_barrier((packed, one))
    packed = [shift(value, s) for s, value in enumerate(packed)]
    shares = total_shares(where, aside, [own, one_in, two_in], reps)
    held, _ = lax.optimization_barrier((packed, shares))
    pieces = weight_partial(where, held, blocks // reps)
    pieces = [shift(value, -s) for s, value in enumerate(pieces)]
    shares = [shift(value, s) for s, value in enumerate(shares)]
    outs = [shift(value, s) for s, value in enumerate(mix(where, shares, packed))]
    input_grad = lay_blocks(where, outs, cotangent.shape)

    grad_w = sum(value.astype(F32) for value in pieces)
    grad_w = grad_w + lax.ppermute(grad_w, "blk", pair)
    parts = [
        lax.ppermute(grad_w, "blk", [(i, i ^ step) for i in range(slabs)])
        for step in range(2, slabs, 2)
    ]
    parts, _ = lax.optimization_barrier((parts, input_grad))
    grad_w = grad_w + sum(parts)
    grad_w = grad_w.transpose(1, 0, 2).reshape(features, width)
    return input_grad, grad_w * (1.0 / math.sqrt(slabs * blocks * nodes))


def solution(mesh):
    placed = (
        P("blk", "rep", None),
        P("blk", "rep", None),
        P("blk", "rep", None),
        P("rep", None),
        P("blk", None, None, None),
        P("blk", None),
        P("blk"),
    )
    return jax.shard_map(
        on_device,
        mesh=mesh,
        in_specs=placed,
        out_specs=(P("blk", "rep", None), P("rep", None)),
        check_vma=False,
    )
```

```python
import functools
import math

import jax
import jax.numpy as jnp
from jax import lax
from jax.experimental import pallas as pl
from jax.experimental.pallas import tpu as pltpu
from jax.sharding import PartitionSpec as P

REACH = 2
GROUP = 4
STEP = 8
PARTS = 2
BF16 = jnp.bfloat16
F32 = jnp.float32
MIB = 1 << 20


def vmem():
    return pl.BlockSpec(memory_space=pltpu.VMEM)


def smem():
    return pl.BlockSpec(memory_space=pltpu.SMEM)


def hbm():
    return pl.BlockSpec(memory_space=pl.ANY)


def in_hbm(value):
    return pltpu.with_memory_space_constraint(value, pltpu.HBM)


def wrap(value, size):
    if size & (size - 1):
        return lax.rem(value + size, size)
    return value & (size - 1)


def tiles_kernel(slabs, reps, where, cols, live, cot, mask, agg, weight, tiles, *rest):
    outs, packed, rest = rest[:4], rest[4 : 4 + reps], rest[4 + reps :]
    outs = [outs[0].at[pl.ds(0, cols.shape[1])], outs[0].at[pl.ds(cols.shape[1], cols.shape[1])], *outs[1:]]
    cot_in, mask_in, z, held, total, rows, left, sems, z_sems, agg_sems = rest
    share = cols.shape[1] // reps
    slots, blocks = cols.shape
    per_row = slots // GROUP
    window = (2 * REACH + 1) * blocks
    copies = [
        pltpu.make_async_copy(cot, cot_in, z_sems.at[0]),
        pltpu.make_async_copy(mask, mask_in, z_sems.at[1]),
    ]
    for copy in copies:
        copy.start()

    def groups_of(b):
        return lax.shift_right_logical(live[b] + GROUP - 1, GROUP.bit_length() - 1)

    half = slots // 2

    def fetched(b, act):
        span = pl.ds(b * slots, half)
        act(pltpu.make_async_copy(tiles.at[span], held.at[span], sems.at[b, 0]))

        @pl.when(live[b] > half)
        def _():
            span = pl.ds(b * slots + half, half)
            act(pltpu.make_async_copy(tiles.at[span], held.at[span], sems.at[b, 1]))

    def list_row(b, count):
        fetched(b, lambda copy: copy.start())
        for g in range(per_row):
            rows[count + g] = b * per_row + g
            left[count + g] = live[b] - g * GROUP
        return count + groups_of(b)

    count = lax.fori_loop(0, blocks, list_row, jnp.int32(0))
    for u in range(STEP):
        rows[count + u] = 0
        left[count + u] = 0
    steps = lax.div(count + STEP - 1, STEP)

    def wait_row(b, carry):
        fetched(b, lambda copy: copy.wait())
        return carry

    def clear(i, carry):
        total[pl.ds(i * GROUP, GROUP)] = jnp.zeros((GROUP,) + total.shape[1:], F32)
        return carry

    lax.fori_loop(0, window // GROUP, clear, 0)
    for copy in copies:
        copy.wait()

    def mask_row(b, carry):
        z[b] = cot_in[b] * mask_in[b].astype(BF16)
        return carry

    lax.fori_loop(0, blocks, mask_row, 0)
    agg_copies = []
    for s in range(reps):
        span = pl.ds(wrap(where[1] + s, reps) * share, share)
        packed[s][:share] = z[span]
        end = packed[s].at[pl.ds(share, share)]
        ends = [(agg.at[span], end)]
        for h in range(weight.shape[1] // z.shape[2]):
            columns = pl.ds(h * z.shape[2], z.shape[2])
            ends.append((weight.at[:, columns], packed[s].at[2 * share + h]))
        for source, target in ends:
            copy = pltpu.make_async_copy(source, target, agg_sems.at[len(agg_copies)])
            copy.start()
            agg_copies.append(copy)
    shift = REACH * blocks - where[0] * blocks

    def step(i, ready):
        entries = [rows[i * STEP + u] for u in range(STEP)]
        need = lax.div(functools.reduce(jnp.maximum, entries), per_row) + 1
        lax.fori_loop(ready, need, wait_row, 0)
        for u in range(STEP):
            row, remain = entries[u], left[i * STEP + u]
            b, g = lax.div(row, per_row), lax.rem(row, per_row)
            z_row = z[b]
            for j in range(GROUP):
                place = wrap(cols[g * GROUP + j, b] + shift, slabs * blocks)
                place = jnp.where(j < remain, place, window)
                total[place] += jnp.dot(
                    z_row, held[row * GROUP + j], preferred_element_type=F32
                )
        return jnp.maximum(ready, need)

    ready = lax.fori_loop(0, steps, step, jnp.int32(0))
    lax.fori_loop(ready, blocks, wait_row, 0)
    for copy in agg_copies:
        copy.wait()
    sign = 2 * lax.rem(where[0], 2) - 1
    for order, out in enumerate(outs):
        base = ((order - REACH) * sign + REACH) * blocks

        def store(i, carry, out=out, base=base):
            for k in range(GROUP):
                at = i * GROUP + k
                out[at] = total[base + at].astype(BF16)
            return carry

        lax.fori_loop(0, blocks // GROUP, store, 0)


def contributions(where, cols, live, cot, mask, agg, weight, tiles, slabs, reps):
    blocks, slots, nodes = tiles.shape[:3]
    features = cot.shape[1]
    window = (2 * REACH + 1) * blocks
    lists = blocks * (slots // GROUP) + slots // GROUP + STEP
    counts = [2 * blocks, blocks, blocks, blocks]
    halves = weight.shape[1] // nodes
    packs = 2 * blocks // reps + halves
    return pl.pallas_call(
        functools.partial(tiles_kernel, slabs, reps),
        out_shape=[jax.ShapeDtypeStruct((count, features, nodes), BF16) for count in counts]
        + [jax.ShapeDtypeStruct((packs, features, nodes), BF16)] * reps,
        in_specs=[smem()] * 3 + [hbm()] * 5,
        out_specs=[vmem()] * (len(counts) + reps),
        scratch_shapes=[
            pltpu.VMEM(cot.shape, BF16),
            pltpu.VMEM(mask.shape, jnp.int32),
            pltpu.VMEM(cot.shape, BF16),
            pltpu.VMEM((blocks * slots, nodes, nodes), BF16),
            pltpu.VMEM((window + 1, features, nodes), F32),
            pltpu.SMEM((lists,), jnp.int32),
            pltpu.SMEM((lists,), jnp.int32),
            pltpu.SemaphoreType.DMA((blocks, 2)),
            pltpu.SemaphoreType.DMA((2,)),
            pltpu.SemaphoreType.DMA((reps * (1 + halves),)),
        ],
        compiler_params=pltpu.CompilerParams(vmem_limit_bytes=30 * MIB),
        cost_estimate=pl.CostEstimate(
            flops=2 * blocks * slots * features * nodes * nodes,
            bytes_accessed=tiles.size * 2,
            transcendentals=0,
        ),
    )(
        where,
        in_hbm(cols.T),
        in_hbm(live),
        in_hbm(cot),
        in_hbm(mask),
        in_hbm(agg),
        in_hbm(weight),
        in_hbm(tiles.reshape(blocks * slots, nodes, nodes)),
    )


def lay_features(where, shares, whole):
    reps, blocks = len(shares), whole.shape[0]
    features = shares[0].shape[1]
    for s in range(reps):
        first = pl.multiple_of(wrap(where[1] - s, reps) * features, features)
        whole[:, pl.ds(first, features), :] = shares[s][:blocks]


def mix_kernel(reps, where, *rest):
    shares, packed, outs = rest[:reps], rest[reps : 2 * reps], rest[2 * reps : 3 * reps]
    weights, whole = rest[3 * reps :]
    blocks, features, nodes = outs[0].shape
    lay_features(where, shares, whole)
    for s in range(reps):
        for h in range(weights.shape[1] // nodes):
            rows, columns = pl.ds(s * features, features), pl.ds(h * nodes, nodes)
            weights[rows, columns] = packed[(reps - s) % reps][2 * blocks + h]
    for b in range(blocks):
        mixed = jnp.dot(weights[...], whole[b], preferred_element_type=F32)
        for s in range(reps):
            outs[s][b] = mixed[s * features : (s + 1) * features].astype(BF16)


def mix(where, shares, packed):
    reps = len(shares)
    blocks, features, nodes = shares[0].shape
    width = reps * features
    return pl.pallas_call(
        functools.partial(mix_kernel, reps),
        out_shape=[jax.ShapeDtypeStruct((blocks, features, nodes), BF16)] * reps,
        in_specs=[smem()] + [vmem()] * (2 * reps),
        out_specs=[vmem()] * reps,
        scratch_shapes=[pltpu.VMEM((width, width), BF16), pltpu.VMEM((blocks, width, nodes), BF16)],
        compiler_params=pltpu.CompilerParams(vmem_limit_bytes=4 * MIB),
        cost_estimate=pl.CostEstimate(
            flops=2 * blocks * nodes * width * width,
            bytes_accessed=4 * blocks * nodes * width,
            transcendentals=0,
        ),
    )(where, *shares, *packed)


def weight_kernel(reps, where, *rest):
    packed, outs, (whole_z, whole_a) = rest[:reps], rest[reps : 2 * reps], rest[2 * reps :]
    blocks, _, nodes = whole_z.shape
    features = packed[0].shape[1]
    lay_features(where, packed, whole_z)
    for s in range(reps):
        whole_a[:, pl.ds(s * features, features), :] = packed[s][blocks : 2 * blocks]
    total = jnp.zeros((whole_a.shape[1], whole_z.shape[1]), F32)
    for b in range(blocks):
        total += lax.dot_general(
            whole_a[b], whole_z[b], (((1,), (1,)), ((), ())), preferred_element_type=F32
        )
    for s in range(reps):
        for h in range(outs[s].shape[0]):
            part = total[s * features : (s + 1) * features, h * nodes : (h + 1) * nodes]
            outs[s][h] = part.astype(BF16)


def weight_partial(where, packed, blocks):
    reps = len(packed)
    _, features, nodes = packed[0].shape
    width = reps * features
    return pl.pallas_call(
        functools.partial(weight_kernel, reps),
        out_shape=[jax.ShapeDtypeStruct((width // nodes, features, nodes), BF16)] * reps,
        in_specs=[smem()] + [vmem()] * reps,
        out_specs=[vmem()] * reps,
        scratch_shapes=[pltpu.VMEM((blocks, width, nodes), BF16)] * 2,
        compiler_params=pltpu.CompilerParams(vmem_limit_bytes=4 * MIB),
        cost_estimate=pl.CostEstimate(
            flops=2 * blocks * nodes * width * width,
            bytes_accessed=4 * blocks * nodes * width + 2 * width * width,
            transcendentals=0,
        ),
    )(where, *packed)


def add_kernel(one, other, *outs):
    for part, out in enumerate(outs):
        base = part * out.shape[0]

        def row(i, carry, out=out, base=base):
            out[i] = (one[base + i].astype(F32) + other[base + i].astype(F32)).astype(BF16)
            return carry

        lax.fori_loop(0, out.shape[0], row, 0)


def add(one, other):
    blocks, features, nodes = one.shape
    part = jax.ShapeDtypeStruct((blocks // PARTS, features, nodes), BF16)
    return pl.pallas_call(
        add_kernel,
        out_shape=[part] * PARTS,
        in_specs=[vmem()] * 2,
        out_specs=[vmem()] * PARTS,
        compiler_params=pltpu.CompilerParams(vmem_limit_bytes=2 * MIB),
        cost_estimate=pl.CostEstimate(
            flops=one.size, bytes_accessed=6 * one.size, transcendentals=0
        ),
    )(one, other)


def total_kernel(reps, where, aside, own, two, *rest):
    one, outs = rest[:-reps], rest[-reps:]
    share = outs[0].shape[0]
    blocks, span = own.shape[0], one[0].shape[0]

    def add_up(s, part):
        first = wrap(where[1] + s, reps) * share
        for i in range(share):
            at = first + i
            total = own[at].astype(F32) + aside[blocks + at].astype(F32)
            total += two[at].astype(F32) + one[part][at - part * span].astype(F32)
            outs[s][i] = total.astype(BF16)

    for s in range(reps):
        for part in range(PARTS):
            pl.when(lax.div(wrap(where[1] + s, reps) * share, span) == part)(
                functools.partial(add_up, s, part)
            )


def total_shares(where, aside, own, two, one, reps):
    blocks, features, nodes = own.shape
    return pl.pallas_call(
        functools.partial(total_kernel, reps),
        out_shape=[jax.ShapeDtypeStruct((blocks // reps, features, nodes), BF16)] * reps,
        in_specs=[smem()] + [vmem()] * (3 + PARTS),
        out_specs=[vmem()] * reps,
        compiler_params=pltpu.CompilerParams(vmem_limit_bytes=2 * MIB),
        cost_estimate=pl.CostEstimate(
            flops=4 * own.size, bytes_accessed=10 * own.size, transcendentals=0
        ),
    )(where, aside, own, two, *one)


def lay_kernel(reps, where, *rest):
    shares, out, sems = rest[:reps], rest[reps], rest[reps + 1]
    blocks = shares[0].shape[0]
    copies = []
    for s in range(reps):
        first = wrap(where[1] - s, reps) * blocks
        copies.append(pltpu.make_async_copy(shares[s], out.at[pl.ds(first, blocks)], sems.at[s]))
        copies[s].start()
    for copy in copies:
        copy.wait()


def lay_blocks(where, shares, shape):
    reps = len(shares)
    return pl.pallas_call(
        functools.partial(lay_kernel, reps),
        out_shape=jax.ShapeDtypeStruct(shape, BF16),
        in_specs=[smem()] + [vmem()] * reps,
        out_specs=hbm(),
        scratch_shapes=[pltpu.SemaphoreType.DMA((reps,))],
        compiler_params=pltpu.CompilerParams(vmem_limit_bytes=2 * MIB),
        cost_estimate=pl.CostEstimate(flops=0, bytes_accessed=32 * MIB, transcendentals=0),
    )(where, *shares)


def shift(value, steps):
    reps = lax.axis_size("rep")
    if steps % reps == 0:
        return value
    return lax.ppermute(value, "rep", [(i, (i + steps) % reps) for i in range(reps)])


def on_device(cotangent, relu_mask, aggregated, weight, tiles, col_block, live_count):
    blocks, features, nodes = cotangent.shape
    slabs, reps = lax.axis_size("blk"), lax.axis_size("rep")
    width = weight.shape[1]
    where = jnp.stack([lax.axis_index("blk"), lax.axis_index("rep")]).astype(jnp.int32)

    pair = [(i, i ^ 1) for i in range(slabs)]
    to_one = [(i, (i + (1 if i % 2 else -1)) % slabs) for i in range(slabs)]
    to_two = [(i, (i + (2 if i % 2 else -2)) % slabs) for i in range(slabs)]
    aside, own, one, two, *packed = contributions(
        where, col_block, live_count, cotangent, relu_mask, aggregated, weight, tiles, slabs, reps
    )
    aside = lax.ppermute(aside, "blk", pair)
    two_in = lax.ppermute(two, "blk", to_two)
    one = add(one, aside)
    one_in = [lax.ppermute(part, "blk", to_one) for part in one]

    packed = [shift(value, s) for s, value in enumerate(packed)]
    shares = total_shares(where, aside, own, two_in, one_in, reps)
    held, _ = lax.optimization_barrier((packed, shares))
    pieces = weight_partial(where, held, blocks // reps)
    pieces = [shift(value, -s) for s, value in enumerate(pieces)]
    shares = [shift(value, s) for s, value in enumerate(shares)]
    outs = [shift(value, s) for s, value in enumerate(mix(where, shares, packed))]
    input_grad = lay_blocks(where, outs, cotangent.shape)

    grad_w = sum(value.astype(F32) for value in pieces)
    grad_w = grad_w + lax.ppermute(grad_w, "blk", pair)
    parts = [
        lax.ppermute(grad_w, "blk", [(i, i ^ step) for i in range(slabs)])
        for step in range(2, slabs, 2)
    ]
    parts, _ = lax.optimization_barrier((parts, input_grad))
    grad_w = grad_w + sum(parts)
    grad_w = grad_w.transpose(1, 0, 2).reshape(features, width)
    return input_grad, grad_w * (1.0 / math.sqrt(slabs * blocks * nodes))


def solution(mesh):
    placed = (
        P("blk", "rep", None),
        P("blk", "rep", None),
        P("blk", "rep", None),
        P("rep", None),
        P("blk", None, None, None),
        P("blk", None),
        P("blk"),
    )
    return jax.shard_map(
        on_device,
        mesh=mesh,
        in_specs=placed,
        out_specs=(P("blk", "rep", None), P("rep", None)),
        check_vma=False,
    )
```

```python
import functools
import math

import jax
import jax.numpy as jnp
from jax import lax
from jax.experimental import pallas as pl
from jax.experimental.pallas import tpu as pltpu
from jax.sharding import PartitionSpec as P

REACH = 2
GROUP = 4
STEP = 8
PARTS = 2
BF16 = jnp.bfloat16
F32 = jnp.float32
MIB = 1 << 20


def vmem():
    return pl.BlockSpec(memory_space=pltpu.VMEM)


def smem():
    return pl.BlockSpec(memory_space=pltpu.SMEM)


def hbm():
    return pl.BlockSpec(memory_space=pl.ANY)


def in_hbm(value):
    return pltpu.with_memory_space_constraint(value, pltpu.HBM)


def wrap(value, size):
    if size & (size - 1):
        return lax.rem(value + size, size)
    return value & (size - 1)


def tiles_kernel(slabs, reps, where, cols, live, cot, mask, agg, weight, tiles, *rest):
    outs, packed, rest = rest[:4], rest[4 : 4 + reps], rest[4 + reps :]
    outs = [outs[0].at[pl.ds(0, cols.shape[1])], outs[0].at[pl.ds(cols.shape[1], cols.shape[1])], *outs[1:]]
    cot_in, mask_in, z, held, total, rows, left, sems, z_sems, agg_sems = rest
    share = cols.shape[1] // reps
    slots, blocks = cols.shape
    per_row = slots // GROUP
    window = (2 * REACH + 1) * blocks
    copies = [
        pltpu.make_async_copy(cot, cot_in, z_sems.at[0]),
        pltpu.make_async_copy(mask, mask_in, z_sems.at[1]),
    ]
    for copy in copies:
        copy.start()

    def groups_of(b):
        return lax.shift_right_logical(live[b] + GROUP - 1, GROUP.bit_length() - 1)

    half = slots // 2

    def fetched(b, act):
        span = pl.ds(b * slots, half)
        act(pltpu.make_async_copy(tiles.at[span], held.at[span], sems.at[b, 0]))
        for i, start in enumerate(range(half, slots, GROUP)):

            @pl.when(live[b] > start)
            def _(i=i, span=pl.ds(b * slots + start, GROUP)):
                act(pltpu.make_async_copy(tiles.at[span], held.at[span], sems.at[b, 1 + i]))

    def list_row(b, count):
        fetched(b, lambda copy: copy.start())
        for g in range(per_row):
            rows[count + g] = b * per_row + g
            left[count + g] = live[b] - g * GROUP
        return count + groups_of(b)

    count = lax.fori_loop(0, blocks, list_row, jnp.int32(0))
    for u in range(STEP):
        rows[count + u] = 0
        left[count + u] = 0
    steps = lax.div(count + STEP - 1, STEP)

    def wait_row(b, carry):
        fetched(b, lambda copy: copy.wait())
        return carry

    def clear(i, carry):
        total[pl.ds(i * GROUP, GROUP)] = jnp.zeros((GROUP,) + total.shape[1:], F32)
        return carry

    lax.fori_loop(0, window // GROUP, clear, 0)
    for copy in copies:
        copy.wait()

    def mask_row(b, carry):
        z[b] = cot_in[b] * mask_in[b].astype(BF16)
        return carry

    lax.fori_loop(0, blocks, mask_row, 0)
    agg_copies = []
    for s in range(reps):
        span = pl.ds(wrap(where[1] + s, reps) * share, share)
        packed[s][:share] = z[span]
        end = packed[s].at[pl.ds(share, share)]
        ends = [(agg.at[span], end)]
        for h in range(weight.shape[1] // z.shape[2]):
            columns = pl.ds(h * z.shape[2], z.shape[2])
            ends.append((weight.at[:, columns], packed[s].at[2 * share + h]))
        for source, target in ends:
            copy = pltpu.make_async_copy(source, target, agg_sems.at[len(agg_copies)])
            copy.start()
            agg_copies.append(copy)
    shift = REACH * blocks - where[0] * blocks

    def step(i, ready):
        entries = [rows[i * STEP + u] for u in range(STEP)]
        need = lax.div(functools.reduce(jnp.maximum, entries), per_row) + 1
        lax.fori_loop(ready, need, wait_row, 0)
        for u in range(STEP):
            row, remain = entries[u], left[i * STEP + u]
            b, g = lax.div(row, per_row), lax.rem(row, per_row)
            z_row = z[b]
            for j in range(GROUP):
                place = wrap(cols[g * GROUP + j, b] + shift, slabs * blocks)
                place = jnp.where(j < remain, place, window)
                total[place] += jnp.dot(
                    z_row, held[row * GROUP + j], preferred_element_type=F32
                )
        return jnp.maximum(ready, need)

    ready = lax.fori_loop(0, steps, step, jnp.int32(0))
    lax.fori_loop(ready, blocks, wait_row, 0)
    for copy in agg_copies:
        copy.wait()
    sign = 2 * lax.rem(where[0], 2) - 1
    for order, out in enumerate(outs):
        base = ((order - REACH) * sign + REACH) * blocks

        def store(i, carry, out=out, base=base):
            for k in range(GROUP):
                at = i * GROUP + k
                out[at] = total[base + at].astype(BF16)
            return carry

        lax.fori_loop(0, blocks // GROUP, store, 0)


def contributions(where, cols, live, cot, mask, agg, weight, tiles, slabs, reps):
    blocks, slots, nodes = tiles.shape[:3]
    features = cot.shape[1]
    window = (2 * REACH + 1) * blocks
    lists = blocks * (slots // GROUP) + slots // GROUP + STEP
    counts = [2 * blocks, blocks, blocks, blocks]
    halves = weight.shape[1] // nodes
    packs = 2 * blocks // reps + halves
    return pl.pallas_call(
        functools.partial(tiles_kernel, slabs, reps),
        out_shape=[jax.ShapeDtypeStruct((count, features, nodes), BF16) for count in counts]
        + [jax.ShapeDtypeStruct((packs, features, nodes), BF16)] * reps,
        in_specs=[smem()] * 3 + [hbm()] * 5,
        out_specs=[vmem()] * (len(counts) + reps),
        scratch_shapes=[
            pltpu.VMEM(cot.shape, BF16),
            pltpu.VMEM(mask.shape, jnp.int32),
            pltpu.VMEM(cot.shape, BF16),
            pltpu.VMEM((blocks * slots, nodes, nodes), BF16),
            pltpu.VMEM((window + 1, features, nodes), F32),
            pltpu.SMEM((lists,), jnp.int32),
            pltpu.SMEM((lists,), jnp.int32),
            pltpu.SemaphoreType.DMA((blocks, 1 + slots // 2 // GROUP)),
            pltpu.SemaphoreType.DMA((2,)),
            pltpu.SemaphoreType.DMA((reps * (1 + halves),)),
        ],
        compiler_params=pltpu.CompilerParams(vmem_limit_bytes=30 * MIB),
        cost_estimate=pl.CostEstimate(
            flops=2 * blocks * slots * features * nodes * nodes,
            bytes_accessed=tiles.size * 2,
            transcendentals=0,
        ),
    )(
        where,
        in_hbm(cols.T),
        in_hbm(live),
        in_hbm(cot),
        in_hbm(mask),
        in_hbm(agg),
        in_hbm(weight),
        in_hbm(tiles.reshape(blocks * slots, nodes, nodes)),
    )


def lay_features(where, shares, whole):
    reps, blocks = len(shares), whole.shape[0]
    features = shares[0].shape[1]
    for s in range(reps):
        first = pl.multiple_of(wrap(where[1] - s, reps) * features, features)
        whole[:, pl.ds(first, features), :] = shares[s][:blocks]


def mix_kernel(reps, where, *rest):
    shares, packed, outs = rest[:reps], rest[reps : 2 * reps], rest[2 * reps : 3 * reps]
    weights, whole = rest[3 * reps :]
    blocks, features, nodes = outs[0].shape
    lay_features(where, shares, whole)
    for s in range(reps):
        for h in range(weights.shape[1] // nodes):
            rows, columns = pl.ds(s * features, features), pl.ds(h * nodes, nodes)
            weights[rows, columns] = packed[(reps - s) % reps][2 * blocks + h]
    for b in range(blocks):
        mixed = jnp.dot(weights[...], whole[b], preferred_element_type=F32)
        for s in range(reps):
            outs[s][b] = mixed[s * features : (s + 1) * features].astype(BF16)


def mix(where, shares, packed):
    reps = len(shares)
    blocks, features, nodes = shares[0].shape
    width = reps * features
    return pl.pallas_call(
        functools.partial(mix_kernel, reps),
        out_shape=[jax.ShapeDtypeStruct((blocks, features, nodes), BF16)] * reps,
        in_specs=[smem()] + [vmem()] * (2 * reps),
        out_specs=[vmem()] * reps,
        scratch_shapes=[pltpu.VMEM((width, width), BF16), pltpu.VMEM((blocks, width, nodes), BF16)],
        compiler_params=pltpu.CompilerParams(vmem_limit_bytes=4 * MIB),
        cost_estimate=pl.CostEstimate(
            flops=2 * blocks * nodes * width * width,
            bytes_accessed=4 * blocks * nodes * width,
            transcendentals=0,
        ),
    )(where, *shares, *packed)


def weight_kernel(reps, where, *rest):
    packed, outs, (whole_z, whole_a) = rest[:reps], rest[reps : 2 * reps], rest[2 * reps :]
    blocks, _, nodes = whole_z.shape
    features = packed[0].shape[1]
    lay_features(where, packed, whole_z)
    for s in range(reps):
        whole_a[:, pl.ds(s * features, features), :] = packed[s][blocks : 2 * blocks]
    total = jnp.zeros((whole_a.shape[1], whole_z.shape[1]), F32)
    for b in range(blocks):
        total += lax.dot_general(
            whole_a[b], whole_z[b], (((1,), (1,)), ((), ())), preferred_element_type=F32
        )
    for s in range(reps):
        for h in range(outs[s].shape[0]):
            part = total[s * features : (s + 1) * features, h * nodes : (h + 1) * nodes]
            outs[s][h] = part.astype(BF16)


def weight_partial(where, packed, blocks):
    reps = len(packed)
    _, features, nodes = packed[0].shape
    width = reps * features
    return pl.pallas_call(
        functools.partial(weight_kernel, reps),
        out_shape=[jax.ShapeDtypeStruct((width // nodes, features, nodes), BF16)] * reps,
        in_specs=[smem()] + [vmem()] * reps,
        out_specs=[vmem()] * reps,
        scratch_shapes=[pltpu.VMEM((blocks, width, nodes), BF16)] * 2,
        compiler_params=pltpu.CompilerParams(vmem_limit_bytes=4 * MIB),
        cost_estimate=pl.CostEstimate(
            flops=2 * blocks * nodes * width * width,
            bytes_accessed=4 * blocks * nodes * width + 2 * width * width,
            transcendentals=0,
        ),
    )(where, *packed)


def add_kernel(one, other, *outs):
    for part, out in enumerate(outs):
        base = part * out.shape[0]

        def row(i, carry, out=out, base=base):
            out[i] = (one[base + i].astype(F32) + other[base + i].astype(F32)).astype(BF16)
            return carry

        lax.fori_loop(0, out.shape[0], row, 0)


def add(one, other):
    blocks, features, nodes = one.shape
    part = jax.ShapeDtypeStruct((blocks // PARTS, features, nodes), BF16)
    return pl.pallas_call(
        add_kernel,
        out_shape=[part] * PARTS,
        in_specs=[vmem()] * 2,
        out_specs=[vmem()] * PARTS,
        compiler_params=pltpu.CompilerParams(vmem_limit_bytes=2 * MIB),
        cost_estimate=pl.CostEstimate(
            flops=one.size, bytes_accessed=6 * one.size, transcendentals=0
        ),
    )(one, other)


def total_kernel(reps, where, aside, own, two, *rest):
    one, outs = rest[:-reps], rest[-reps:]
    share = outs[0].shape[0]
    blocks, span = own.shape[0], one[0].shape[0]

    def add_up(s, part):
        first = wrap(where[1] + s, reps) * share
        for i in range(share):
            at = first + i
            total = own[at].astype(F32) + aside[blocks + at].astype(F32)
            total += two[at].astype(F32) + one[part][at - part * span].astype(F32)
            outs[s][i] = total.astype(BF16)

    for s in range(reps):
        for part in range(PARTS):
            pl.when(lax.div(wrap(where[1] + s, reps) * share, span) == part)(
                functools.partial(add_up, s, part)
            )


def total_shares(where, aside, own, two, one, reps):
    blocks, features, nodes = own.shape
    return pl.pallas_call(
        functools.partial(total_kernel, reps),
        out_shape=[jax.ShapeDtypeStruct((blocks // reps, features, nodes), BF16)] * reps,
        in_specs=[smem()] + [vmem()] * (3 + PARTS),
        out_specs=[vmem()] * reps,
        compiler_params=pltpu.CompilerParams(vmem_limit_bytes=2 * MIB),
        cost_estimate=pl.CostEstimate(
            flops=4 * own.size, bytes_accessed=10 * own.size, transcendentals=0
        ),
    )(where, aside, own, two, *one)


def lay_kernel(reps, where, *rest):
    shares, out, sems = rest[:reps], rest[reps], rest[reps + 1]
    blocks = shares[0].shape[0]
    copies = []
    for s in range(reps):
        first = wrap(where[1] - s, reps) * blocks
        copies.append(pltpu.make_async_copy(shares[s], out.at[pl.ds(first, blocks)], sems.at[s]))
        copies[s].start()
    for copy in copies:
        copy.wait()


def lay_blocks(where, shares, shape):
    reps = len(shares)
    return pl.pallas_call(
        functools.partial(lay_kernel, reps),
        out_shape=jax.ShapeDtypeStruct(shape, BF16),
        in_specs=[smem()] + [vmem()] * reps,
        out_specs=hbm(),
        scratch_shapes=[pltpu.SemaphoreType.DMA((reps,))],
        compiler_params=pltpu.CompilerParams(vmem_limit_bytes=2 * MIB),
        cost_estimate=pl.CostEstimate(flops=0, bytes_accessed=32 * MIB, transcendentals=0),
    )(where, *shares)


def shift(value, steps):
    reps = lax.axis_size("rep")
    if steps % reps == 0:
        return value
    return lax.ppermute(value, "rep", [(i, (i + steps) % reps) for i in range(reps)])


def on_device(cotangent, relu_mask, aggregated, weight, tiles, col_block, live_count):
    blocks, features, nodes = cotangent.shape
    slabs, reps = lax.axis_size("blk"), lax.axis_size("rep")
    width = weight.shape[1]
    where = jnp.stack([lax.axis_index("blk"), lax.axis_index("rep")]).astype(jnp.int32)

    pair = [(i, i ^ 1) for i in range(slabs)]
    to_one = [(i, (i + (1 if i % 2 else -1)) % slabs) for i in range(slabs)]
    to_two = [(i, (i + (2 if i % 2 else -2)) % slabs) for i in range(slabs)]
    aside, own, one, two, *packed = contributions(
        where, col_block, live_count, cotangent, relu_mask, aggregated, weight, tiles, slabs, reps
    )
    aside = lax.ppermute(aside, "blk", pair)
    two_in = lax.ppermute(two, "blk", to_two)
    one = add(one, aside)
    one_in = [lax.ppermute(part, "blk", to_one) for part in one]

    packed = [shift(value, s) for s, value in enumerate(packed)]
    shares = total_shares(where, aside, own, two_in, one_in, reps)
    held, _ = lax.optimization_barrier((packed, shares))
    pieces = weight_partial(where, held, blocks // reps)
    pieces = [shift(value, -s) for s, value in enumerate(pieces)]
    shares = [shift(value, s) for s, value in enumerate(shares)]
    shares, _ = lax.optimization_barrier((shares, pieces[1:]))
    outs = [shift(value, s) for s, value in enumerate(mix(where, shares, packed))]
    input_grad = lay_blocks(where, outs, cotangent.shape)

    grad_w = sum(value.astype(F32) for value in pieces)
    grad_w = grad_w + lax.ppermute(grad_w, "blk", pair)
    parts = [
        lax.ppermute(grad_w, "blk", [(i, i ^ step) for i in range(slabs)])
        for step in range(2, slabs, 2)
    ]
    parts, _ = lax.optimization_barrier((parts, input_grad))
    grad_w = grad_w + sum(parts)
    grad_w = grad_w.transpose(1, 0, 2).reshape(features, width)
    return input_grad, grad_w * (1.0 / math.sqrt(slabs * blocks * nodes))


def solution(mesh):
    placed = (
        P("blk", "rep", None),
        P("blk", "rep", None),
        P("blk", "rep", None),
        P("rep", None),
        P("blk", None, None, None),
        P("blk", None),
        P("blk"),
    )
    return jax.shard_map(
        on_device,
        mesh=mesh,
        in_specs=placed,
        out_specs=(P("blk", "rep", None), P("rep", None)),
        check_vma=False,
    )
```

```python
import functools
import math

import jax
import jax.numpy as jnp
from jax import lax
from jax.experimental import pallas as pl
from jax.experimental.pallas import tpu as pltpu
from jax.sharding import PartitionSpec as P

REACH = 2
GROUP = 4
STEP = 8
PARTS = 2
BF16 = jnp.bfloat16
F32 = jnp.float32
MIB = 1 << 20


def vmem():
    return pl.BlockSpec(memory_space=pltpu.VMEM)


def smem():
    return pl.BlockSpec(memory_space=pltpu.SMEM)


def hbm():
    return pl.BlockSpec(memory_space=pl.ANY)


def in_hbm(value):
    return pltpu.with_memory_space_constraint(value, pltpu.HBM)


def wrap(value, size):
    if size & (size - 1):
        return lax.rem(value + size, size)
    return value & (size - 1)


def tiles_kernel(slabs, reps, where, cols, live, cot, mask, agg, weight, tiles, *rest):
    outs, packed, rest = rest[:4], rest[4 : 4 + reps], rest[4 + reps :]
    outs = [outs[0].at[pl.ds(0, cols.shape[1])], outs[0].at[pl.ds(cols.shape[1], cols.shape[1])], *outs[1:]]
    cot_in, mask_in, z, held, total, rows, left, sems, z_sems, agg_sems = rest
    share = cols.shape[1] // reps
    slots, blocks = cols.shape
    per_row = slots // GROUP
    window = (2 * REACH + 1) * blocks
    copies = [
        pltpu.make_async_copy(cot, cot_in, z_sems.at[0]),
        pltpu.make_async_copy(mask, mask_in, z_sems.at[1]),
    ]
    for copy in copies:
        copy.start()

    def groups_of(b):
        return lax.shift_right_logical(live[b] + GROUP - 1, GROUP.bit_length() - 1)

    half = slots // 2

    def fetched(b, act):
        span = pl.ds(b * slots, half)
        act(pltpu.make_async_copy(tiles.at[span], held.at[span], sems.at[b, 0]))

        @pl.when(live[b] > half)
        def _():
            span = pl.ds(b * slots + half, half)
            act(pltpu.make_async_copy(tiles.at[span], held.at[span], sems.at[b, 1]))

    def list_row(b, count):
        fetched(b, lambda copy: copy.start())
        for g in range(per_row):
            rows[count + g] = b * per_row + g
            left[count + g] = live[b] - g * GROUP
        return count + groups_of(b)

    count = lax.fori_loop(0, blocks, list_row, jnp.int32(0))
    for u in range(STEP):
        rows[count + u] = 0
        left[count + u] = 0
    steps = lax.div(count + STEP - 1, STEP)

    def wait_row(b, carry):
        fetched(b, lambda copy: copy.wait())
        return carry

    def clear(i, carry):
        total[pl.ds(i * GROUP, GROUP)] = jnp.zeros((GROUP,) + total.shape[1:], F32)
        return carry

    lax.fori_loop(0, window // GROUP, clear, 0)
    for copy in copies:
        copy.wait()

    def mask_row(b, carry):
        z[b] = cot_in[b] * mask_in[b].astype(BF16)
        return carry

    lax.fori_loop(0, blocks, mask_row, 0)
    agg_copies = []
    for s in range(reps):
        span = pl.ds(wrap(where[1] + s, reps) * share, share)
        packed[s][:share] = z[span]
        end = packed[s].at[pl.ds(share, share)]
        ends = [(agg.at[span], end)]
        for h in range(weight.shape[1] // z.shape[2]):
            columns = pl.ds(h * z.shape[2], z.shape[2])
            ends.append((weight.at[:, columns], packed[s].at[2 * share + h]))
        for source, target in ends:
            copy = pltpu.make_async_copy(source, target, agg_sems.at[len(agg_copies)])
            copy.start()
            agg_copies.append(copy)
    shift = REACH * blocks - where[0] * blocks

    def step(i, ready):
        entries = [rows[i * STEP + u] for u in range(STEP)]
        need = lax.div(functools.reduce(jnp.maximum, entries), per_row) + 1
        lax.fori_loop(ready, need, wait_row, 0)
        for u in range(STEP):
            row, remain = entries[u], left[i * STEP + u]
            b, g = lax.div(row, per_row), lax.rem(row, per_row)
            z_row = z[b]
            for j in range(GROUP):
                place = wrap(cols[g * GROUP + j, b] + shift, slabs * blocks)
                place = jnp.where(j < remain, place, window)
                total[place] += jnp.dot(
                    z_row, held[row * GROUP + j], preferred_element_type=F32
                )
        return jnp.maximum(ready, need)

    ready = lax.fori_loop(0, steps, step, jnp.int32(0))
    lax.fori_loop(ready, blocks, wait_row, 0)
    for copy in agg_copies:
        copy.wait()
    sign = 2 * lax.rem(where[0], 2) - 1
    for order, out in enumerate(outs):
        base = ((order - REACH) * sign + REACH) * blocks

        def store(i, carry, out=out, base=base):
            for k in range(GROUP):
                at = i * GROUP + k
                out[at] = total[base + at].astype(BF16)
            return carry

        lax.fori_loop(0, blocks // GROUP, store, 0)


def contributions(where, cols, live, cot, mask, agg, weight, tiles, slabs, reps):
    blocks, slots, nodes = tiles.shape[:3]
    features = cot.shape[1]
    window = (2 * REACH + 1) * blocks
    lists = blocks * (slots // GROUP) + slots // GROUP + STEP
    counts = [2 * blocks, blocks, blocks, blocks]
    halves = weight.shape[1] // nodes
    packs = 2 * blocks // reps + halves
    return pl.pallas_call(
        functools.partial(tiles_kernel, slabs, reps),
        out_shape=[jax.ShapeDtypeStruct((count, features, nodes), BF16) for count in counts]
        + [jax.ShapeDtypeStruct((packs, features, nodes), BF16)] * reps,
        in_specs=[smem()] * 3 + [hbm()] * 5,
        out_specs=[vmem()] * (len(counts) + reps),
        scratch_shapes=[
            pltpu.VMEM(cot.shape, BF16),
            pltpu.VMEM(mask.shape, jnp.int32),
            pltpu.VMEM(cot.shape, BF16),
            pltpu.VMEM((blocks * slots, nodes, nodes), BF16),
            pltpu.VMEM((window + 1, features, nodes), F32),
            pltpu.SMEM((lists,), jnp.int32),
            pltpu.SMEM((lists,), jnp.int32),
            pltpu.SemaphoreType.DMA((blocks, 2)),
            pltpu.SemaphoreType.DMA((2,)),
            pltpu.SemaphoreType.DMA((reps * (1 + halves),)),
        ],
        compiler_params=pltpu.CompilerParams(vmem_limit_bytes=30 * MIB),
        cost_estimate=pl.CostEstimate(
            flops=2 * blocks * slots * features * nodes * nodes,
            bytes_accessed=tiles.size * 2,
            transcendentals=0,
        ),
    )(
        where,
        in_hbm(cols.T),
        in_hbm(live),
        in_hbm(cot),
        in_hbm(mask),
        in_hbm(agg),
        in_hbm(weight),
        in_hbm(tiles.reshape(blocks * slots, nodes, nodes)),
    )


def lay_features(where, shares, whole):
    reps, blocks = len(shares), whole.shape[0]
    features = shares[0].shape[1]
    for s in range(reps):
        first = pl.multiple_of(wrap(where[1] - s, reps) * features, features)
        whole[:, pl.ds(first, features), :] = shares[s][:blocks]


def mix_kernel(reps, where, *rest):
    shares, packed, outs = rest[:reps], rest[reps : 2 * reps], rest[2 * reps : 3 * reps]
    weights, whole = rest[3 * reps :]
    blocks, features, nodes = outs[0].shape
    lay_features(where, shares, whole)
    for s in range(reps):
        for h in range(weights.shape[1] // nodes):
            rows, columns = pl.ds(s * features, features), pl.ds(h * nodes, nodes)
            weights[rows, columns] = packed[(reps - s) % reps][2 * blocks + h]
    for b in range(blocks):
        mixed = jnp.dot(weights[...], whole[b], preferred_element_type=F32)
        for s in range(reps):
            outs[s][b] = mixed[s * features : (s + 1) * features].astype(BF16)


def mix(where, shares, packed):
    reps = len(shares)
    blocks, features, nodes = shares[0].shape
    width = reps * features
    return pl.pallas_call(
        functools.partial(mix_kernel, reps),
        out_shape=[jax.ShapeDtypeStruct((blocks, features, nodes), BF16)] * reps,
        in_specs=[smem()] + [vmem()] * (2 * reps),
        out_specs=[vmem()] * reps,
        scratch_shapes=[pltpu.VMEM((width, width), BF16), pltpu.VMEM((blocks, width, nodes), BF16)],
        compiler_params=pltpu.CompilerParams(vmem_limit_bytes=4 * MIB),
        cost_estimate=pl.CostEstimate(
            flops=2 * blocks * nodes * width * width,
            bytes_accessed=4 * blocks * nodes * width,
            transcendentals=0,
        ),
    )(where, *shares, *packed)


def weight_kernel(reps, where, *rest):
    packed, (out, whole_z, whole_a) = rest[:reps], rest[reps:]
    blocks, _, nodes = whole_z.shape
    features = packed[0].shape[1]
    lay_features(where, packed, whole_z)
    for s in range(reps):
        whole_a[:, pl.ds(s * features, features), :] = packed[s][blocks : 2 * blocks]
    total = jnp.zeros((whole_a.shape[1], whole_z.shape[1]), F32)
    for b in range(blocks):
        total += lax.dot_general(
            whole_a[b], whole_z[b], (((1,), (1,)), ((), ())), preferred_element_type=F32
        )
    for s in range(reps):
        for h in range(out.shape[1]):
            part = total[s * features : (s + 1) * features, h * nodes : (h + 1) * nodes]
            out[wrap(where[1] - s, reps), h] = part.astype(BF16)


def weight_partial(where, packed, blocks):
    reps = len(packed)
    _, features, nodes = packed[0].shape
    width = reps * features
    return pl.pallas_call(
        functools.partial(weight_kernel, reps),
        out_shape=jax.ShapeDtypeStruct((reps, width // nodes, features, nodes), BF16),
        in_specs=[smem()] + [vmem()] * reps,
        out_specs=vmem(),
        scratch_shapes=[pltpu.VMEM((blocks, width, nodes), BF16)] * 2,
        compiler_params=pltpu.CompilerParams(vmem_limit_bytes=4 * MIB),
        cost_estimate=pl.CostEstimate(
            flops=2 * blocks * nodes * width * width,
            bytes_accessed=4 * blocks * nodes * width + 2 * width * width,
            transcendentals=0,
        ),
    )(where, *packed)


def add_kernel(one, other, *outs):
    for part, out in enumerate(outs):
        base = part * out.shape[0]

        def row(i, carry, out=out, base=base):
            out[i] = (one[base + i].astype(F32) + other[base + i].astype(F32)).astype(BF16)
            return carry

        lax.fori_loop(0, out.shape[0], row, 0)


def add(one, other):
    blocks, features, nodes = one.shape
    part = jax.ShapeDtypeStruct((blocks // PARTS, features, nodes), BF16)
    return pl.pallas_call(
        add_kernel,
        out_shape=[part] * PARTS,
        in_specs=[vmem()] * 2,
        out_specs=[vmem()] * PARTS,
        compiler_params=pltpu.CompilerParams(vmem_limit_bytes=2 * MIB),
        cost_estimate=pl.CostEstimate(
            flops=one.size, bytes_accessed=6 * one.size, transcendentals=0
        ),
    )(one, other)


def total_kernel(reps, where, aside, own, two, *rest):
    one, outs = rest[:-reps], rest[-reps:]
    share = outs[0].shape[0]
    blocks, span = own.shape[0], one[0].shape[0]

    def add_up(s, part):
        first = wrap(where[1] + s, reps) * share
        for i in range(share):
            at = first + i
            total = own[at].astype(F32) + aside[blocks + at].astype(F32)
            total += two[at].astype(F32) + one[part][at - part * span].astype(F32)
            outs[s][i] = total.astype(BF16)

    for s in range(reps):
        for part in range(PARTS):
            pl.when(lax.div(wrap(where[1] + s, reps) * share, span) == part)(
                functools.partial(add_up, s, part)
            )


def total_shares(where, aside, own, two, one, reps):
    blocks, features, nodes = own.shape
    return pl.pallas_call(
        functools.partial(total_kernel, reps),
        out_shape=[jax.ShapeDtypeStruct((blocks // reps, features, nodes), BF16)] * reps,
        in_specs=[smem()] + [vmem()] * (3 + PARTS),
        out_specs=[vmem()] * reps,
        compiler_params=pltpu.CompilerParams(vmem_limit_bytes=2 * MIB),
        cost_estimate=pl.CostEstimate(
            flops=4 * own.size, bytes_accessed=10 * own.size, transcendentals=0
        ),
    )(where, aside, own, two, *one)


def lay_kernel(reps, where, *rest):
    shares, out, sems = rest[:reps], rest[reps], rest[reps + 1]
    blocks = shares[0].shape[0]
    copies = []
    for s in range(reps):
        first = wrap(where[1] - s, reps) * blocks
        copies.append(pltpu.make_async_copy(shares[s], out.at[pl.ds(first, blocks)], sems.at[s]))
        copies[s].start()
    for copy in copies:
        copy.wait()


def lay_blocks(where, shares, shape):
    reps = len(shares)
    return pl.pallas_call(
        functools.partial(lay_kernel, reps),
        out_shape=jax.ShapeDtypeStruct(shape, BF16),
        in_specs=[smem()] + [vmem()] * reps,
        out_specs=hbm(),
        scratch_shapes=[pltpu.SemaphoreType.DMA((reps,))],
        compiler_params=pltpu.CompilerParams(vmem_limit_bytes=2 * MIB),
        cost_estimate=pl.CostEstimate(flops=0, bytes_accessed=32 * MIB, transcendentals=0),
    )(where, *shares)


def shift(value, steps):
    reps = lax.axis_size("rep")
    if steps % reps == 0:
        return value
    return lax.ppermute(value, "rep", [(i, (i + steps) % reps) for i in range(reps)])


def on_device(cotangent, relu_mask, aggregated, weight, tiles, col_block, live_count):
    blocks, features, nodes = cotangent.shape
    slabs, reps = lax.axis_size("blk"), lax.axis_size("rep")
    width = weight.shape[1]
    where = jnp.stack([lax.axis_index("blk"), lax.axis_index("rep")]).astype(jnp.int32)

    pair = [(i, i ^ 1) for i in range(slabs)]
    to_one = [(i, (i + (1 if i % 2 else -1)) % slabs) for i in range(slabs)]
    to_two = [(i, (i + (2 if i % 2 else -2)) % slabs) for i in range(slabs)]
    aside, own, one, two, *packed = contributions(
        where, col_block, live_count, cotangent, relu_mask, aggregated, weight, tiles, slabs, reps
    )
    aside = lax.ppermute(aside, "blk", pair)
    two_in = lax.ppermute(two, "blk", to_two)
    one = add(one, aside)
    one_in = [lax.ppermute(part, "blk", to_one) for part in one]

    packed = [shift(value, s) for s, value in enumerate(packed)]
    shares = total_shares(where, aside, own, two_in, one_in, reps)
    held, _ = lax.optimization_barrier((packed, shares))
    pieces = weight_partial(where, held, blocks // reps)
    pieces = lax.all_to_all(pieces, "rep", 0, 0, tiled=True)
    shares = [shift(value, s) for s, value in enumerate(shares)]
    outs = [shift(value, s) for s, value in enumerate(mix(where, shares, packed))]
    input_grad = lay_blocks(where, outs, cotangent.shape)

    grad_w = pieces.astype(F32).sum(0)
    grad_w = grad_w + lax.ppermute(grad_w, "blk", pair)
    parts = [
        lax.ppermute(grad_w, "blk", [(i, i ^ step) for i in range(slabs)])
        for step in range(2, slabs, 2)
    ]
    parts, _ = lax.optimization_barrier((parts, input_grad))
    grad_w = grad_w + sum(parts)
    grad_w = grad_w.transpose(1, 0, 2).reshape(features, width)
    return input_grad, grad_w * (1.0 / math.sqrt(slabs * blocks * nodes))


def solution(mesh):
    placed = (
        P("blk", "rep", None),
        P("blk", "rep", None),
        P("blk", "rep", None),
        P("rep", None),
        P("blk", None, None, None),
        P("blk", None),
        P("blk"),
    )
    return jax.shard_map(
        on_device,
        mesh=mesh,
        in_specs=placed,
        out_specs=(P("blk", "rep", None), P("rep", None)),
        check_vma=False,
    )
```

```python
import functools
import math

import jax
import jax.numpy as jnp
from jax import lax
from jax.experimental import pallas as pl
from jax.experimental.pallas import tpu as pltpu
from jax.sharding import PartitionSpec as P

REACH = 2
GROUP = 4
STEP = 4
PARTS = 2
BF16 = jnp.bfloat16
F32 = jnp.float32
MIB = 1 << 20


def vmem():
    return pl.BlockSpec(memory_space=pltpu.VMEM)


def smem():
    return pl.BlockSpec(memory_space=pltpu.SMEM)


def hbm():
    return pl.BlockSpec(memory_space=pl.ANY)


def in_hbm(value):
    return pltpu.with_memory_space_constraint(value, pltpu.HBM)


def wrap(value, size):
    if size & (size - 1):
        return lax.rem(value + size, size)
    return value & (size - 1)


def tiles_kernel(slabs, reps, where, cols, live, cot, mask, agg, weight, tiles, *rest):
    outs, packed, rest = rest[:4], rest[4 : 4 + reps], rest[4 + reps :]
    outs = [outs[0].at[pl.ds(0, cols.shape[1])], outs[0].at[pl.ds(cols.shape[1], cols.shape[1])], *outs[1:]]
    cot_in, mask_in, z, held, total, rows, left, sems, z_sems, agg_sems = rest
    share = cols.shape[1] // reps
    slots, blocks = cols.shape
    per_row = slots // GROUP
    window = (2 * REACH + 1) * blocks
    copies = [
        pltpu.make_async_copy(cot, cot_in, z_sems.at[0]),
        pltpu.make_async_copy(mask, mask_in, z_sems.at[1]),
    ]
    for copy in copies:
        copy.start()

    def groups_of(b):
        return lax.shift_right_logical(live[b] + GROUP - 1, GROUP.bit_length() - 1)

    half = slots // 2

    def fetched(b, act):
        span = pl.ds(b * slots, half)
        act(pltpu.make_async_copy(tiles.at[span], held.at[span], sems.at[b, 0]))

        @pl.when(live[b] > half)
        def _():
            span = pl.ds(b * slots + half, half)
            act(pltpu.make_async_copy(tiles.at[span], held.at[span], sems.at[b, 1]))

    def list_row(b, count):
        fetched(b, lambda copy: copy.start())
        for g in range(per_row):
            rows[count + g] = b * per_row + g
            left[count + g] = live[b] - g * GROUP
        return count + groups_of(b)

    count = lax.fori_loop(0, blocks, list_row, jnp.int32(0))
    for u in range(STEP):
        rows[count + u] = 0
        left[count + u] = 0
    steps = lax.div(count + STEP - 1, STEP)

    def wait_row(b, carry):
        fetched(b, lambda copy: copy.wait())
        return carry

    def clear(i, carry):
        total[pl.ds(i * GROUP, GROUP)] = jnp.zeros((GROUP,) + total.shape[1:], F32)
        return carry

    lax.fori_loop(0, window // GROUP, clear, 0)
    for copy in copies:
        copy.wait()

    def mask_row(b, carry):
        z[b] = cot_in[b] * mask_in[b].astype(BF16)
        return carry

    lax.fori_loop(0, blocks, mask_row, 0)
    agg_copies = []
    for s in range(reps):
        span = pl.ds(wrap(where[1] + s, reps) * share, share)
        packed[s][:share] = z[span]
        end = packed[s].at[pl.ds(share, share)]
        ends = [(agg.at[span], end)]
        for h in range(weight.shape[1] // z.shape[2]):
            columns = pl.ds(h * z.shape[2], z.shape[2])
            ends.append((weight.at[:, columns], packed[s].at[2 * share + h]))
        for source, target in ends:
            copy = pltpu.make_async_copy(source, target, agg_sems.at[len(agg_copies)])
            copy.start()
            agg_copies.append(copy)
    shift = REACH * blocks - where[0] * blocks

    def step(i, ready):
        entries = [rows[i * STEP + u] for u in range(STEP)]
        need = lax.div(functools.reduce(jnp.maximum, entries), per_row) + 1
        lax.fori_loop(ready, need, wait_row, 0)
        for u in range(STEP):
            row, remain = entries[u], left[i * STEP + u]
            b, g = lax.div(row, per_row), lax.rem(row, per_row)
            z_row = z[b]
            for j in range(GROUP):
                place = wrap(cols[g * GROUP + j, b] + shift, slabs * blocks)
                place = jnp.where(j < remain, place, window)
                total[place] += jnp.dot(
                    z_row, held[row * GROUP + j], preferred_element_type=F32
                )
        return jnp.maximum(ready, need)

    ready = lax.fori_loop(0, steps, step, jnp.int32(0))
    lax.fori_loop(ready, blocks, wait_row, 0)
    for copy in agg_copies:
        copy.wait()
    sign = 2 * lax.rem(where[0], 2) - 1
    for order, out in enumerate(outs):
        base = ((order - REACH) * sign + REACH) * blocks

        def store(i, carry, out=out, base=base):
            for k in range(GROUP):
                at = i * GROUP + k
                out[at] = total[base + at].astype(BF16)
            return carry

        lax.fori_loop(0, blocks // GROUP, store, 0)


def contributions(where, cols, live, cot, mask, agg, weight, tiles, slabs, reps):
    blocks, slots, nodes = tiles.shape[:3]
    features = cot.shape[1]
    window = (2 * REACH + 1) * blocks
    lists = blocks * (slots // GROUP) + slots // GROUP + STEP
    counts = [2 * blocks, blocks, blocks, blocks]
    halves = weight.shape[1] // nodes
    packs = 2 * blocks // reps + halves
    return pl.pallas_call(
        functools.partial(tiles_kernel, slabs, reps),
        out_shape=[jax.ShapeDtypeStruct((count, features, nodes), BF16) for count in counts]
        + [jax.ShapeDtypeStruct((packs, features, nodes), BF16)] * reps,
        in_specs=[smem()] * 3 + [hbm()] * 5,
        out_specs=[vmem()] * (len(counts) + reps),
        scratch_shapes=[
            pltpu.VMEM(cot.shape, BF16),
            pltpu.VMEM(mask.shape, jnp.int32),
            pltpu.VMEM(cot.shape, BF16),
            pltpu.VMEM((blocks * slots, nodes, nodes), BF16),
            pltpu.VMEM((window + 1, features, nodes), F32),
            pltpu.SMEM((lists,), jnp.int32),
            pltpu.SMEM((lists,), jnp.int32),
            pltpu.SemaphoreType.DMA((blocks, 2)),
            pltpu.SemaphoreType.DMA((2,)),
            pltpu.SemaphoreType.DMA((reps * (1 + halves),)),
        ],
        compiler_params=pltpu.CompilerParams(vmem_limit_bytes=30 * MIB),
        cost_estimate=pl.CostEstimate(
            flops=2 * blocks * slots * features * nodes * nodes,
            bytes_accessed=tiles.size * 2,
            transcendentals=0,
        ),
    )(
        where,
        in_hbm(cols.T),
        in_hbm(live),
        in_hbm(cot),
        in_hbm(mask),
        in_hbm(agg),
        in_hbm(weight),
        in_hbm(tiles.reshape(blocks * slots, nodes, nodes)),
    )


def lay_features(where, shares, whole):
    reps, blocks = len(shares), whole.shape[0]
    features = shares[0].shape[1]
    for s in range(reps):
        first = pl.multiple_of(wrap(where[1] - s, reps) * features, features)
        whole[:, pl.ds(first, features), :] = shares[s][:blocks]


def mix_kernel(reps, where, *rest):
    shares, packed, outs = rest[:reps], rest[reps : 2 * reps], rest[2 * reps : 3 * reps]
    weights, whole = rest[3 * reps :]
    blocks, features, nodes = outs[0].shape
    lay_features(where, shares, whole)
    for s in range(reps):
        for h in range(weights.shape[1] // nodes):
            rows, columns = pl.ds(s * features, features), pl.ds(h * nodes, nodes)
            weights[rows, columns] = packed[(reps - s) % reps][2 * blocks + h]
    for b in range(blocks):
        mixed = jnp.dot(weights[...], whole[b], preferred_element_type=F32)
        for s in range(reps):
            outs[s][b] = mixed[s * features : (s + 1) * features].astype(BF16)


def mix(where, shares, packed):
    reps = len(shares)
    blocks, features, nodes = shares[0].shape
    width = reps * features
    return pl.pallas_call(
        functools.partial(mix_kernel, reps),
        out_shape=[jax.ShapeDtypeStruct((blocks, features, nodes), BF16)] * reps,
        in_specs=[smem()] + [vmem()] * (2 * reps),
        out_specs=[vmem()] * reps,
        scratch_shapes=[pltpu.VMEM((width, width), BF16), pltpu.VMEM((blocks, width, nodes), BF16)],
        compiler_params=pltpu.CompilerParams(vmem_limit_bytes=4 * MIB),
        cost_estimate=pl.CostEstimate(
            flops=2 * blocks * nodes * width * width,
            bytes_accessed=4 * blocks * nodes * width,
            transcendentals=0,
        ),
    )(where, *shares, *packed)


def weight_kernel(reps, where, *rest):
    packed, outs, (whole_z, whole_a) = rest[:reps], rest[reps : 2 * reps], rest[2 * reps :]
    blocks, _, nodes = whole_z.shape
    features = packed[0].shape[1]
    lay_features(where, packed, whole_z)
    for s in range(reps):
        whole_a[:, pl.ds(s * features, features), :] = packed[s][blocks : 2 * blocks]
    total = jnp.zeros((whole_a.shape[1], whole_z.shape[1]), F32)
    for b in range(blocks):
        total += lax.dot_general(
            whole_a[b], whole_z[b], (((1,), (1,)), ((), ())), preferred_element_type=F32
        )
    for s in range(reps):
        for h in range(outs[s].shape[0]):
            part = total[s * features : (s + 1) * features, h * nodes : (h + 1) * nodes]
            outs[s][h] = part.astype(BF16)


def weight_partial(where, packed, blocks):
    reps = len(packed)
    _, features, nodes = packed[0].shape
    width = reps * features
    return pl.pallas_call(
        functools.partial(weight_kernel, reps),
        out_shape=[jax.ShapeDtypeStruct((width // nodes, features, nodes), BF16)] * reps,
        in_specs=[smem()] + [vmem()] * reps,
        out_specs=[vmem()] * reps,
        scratch_shapes=[pltpu.VMEM((blocks, width, nodes), BF16)] * 2,
        compiler_params=pltpu.CompilerParams(vmem_limit_bytes=4 * MIB),
        cost_estimate=pl.CostEstimate(
            flops=2 * blocks * nodes * width * width,
            bytes_accessed=4 * blocks * nodes * width + 2 * width * width,
            transcendentals=0,
        ),
    )(where, *packed)


def add_kernel(one, other, *outs):
    for part, out in enumerate(outs):
        base = part * out.shape[0]

        def row(i, carry, out=out, base=base):
            out[i] = (one[base + i].astype(F32) + other[base + i].astype(F32)).astype(BF16)
            return carry

        lax.fori_loop(0, out.shape[0], row, 0)


def add(one, other):
    blocks, features, nodes = one.shape
    part = jax.ShapeDtypeStruct((blocks // PARTS, features, nodes), BF16)
    return pl.pallas_call(
        add_kernel,
        out_shape=[part] * PARTS,
        in_specs=[vmem()] * 2,
        out_specs=[vmem()] * PARTS,
        compiler_params=pltpu.CompilerParams(vmem_limit_bytes=2 * MIB),
        cost_estimate=pl.CostEstimate(
            flops=one.size, bytes_accessed=6 * one.size, transcendentals=0
        ),
    )(one, other)


def total_kernel(reps, where, aside, own, two, *rest):
    one, outs = rest[:-reps], rest[-reps:]
    share = outs[0].shape[0]
    blocks, span = own.shape[0], one[0].shape[0]

    def add_up(s, part):
        first = wrap(where[1] + s, reps) * share
        for i in range(share):
            at = first + i
            total = own[at].astype(F32) + aside[blocks + at].astype(F32)
            total += two[at].astype(F32) + one[part][at - part * span].astype(F32)
            outs[s][i] = total.astype(BF16)

    for s in range(reps):
        for part in range(PARTS):
            pl.when(lax.div(wrap(where[1] + s, reps) * share, span) == part)(
                functools.partial(add_up, s, part)
            )


def total_shares(where, aside, own, two, one, reps):
    blocks, features, nodes = own.shape
    return pl.pallas_call(
        functools.partial(total_kernel, reps),
        out_shape=[jax.ShapeDtypeStruct((blocks // reps, features, nodes), BF16)] * reps,
        in_specs=[smem()] + [vmem()] * (3 + PARTS),
        out_specs=[vmem()] * reps,
        compiler_params=pltpu.CompilerParams(vmem_limit_bytes=2 * MIB),
        cost_estimate=pl.CostEstimate(
            flops=4 * own.size, bytes_accessed=10 * own.size, transcendentals=0
        ),
    )(where, aside, own, two, *one)


def lay_kernel(reps, where, *rest):
    shares, out, sems = rest[:reps], rest[reps], rest[reps + 1]
    blocks = shares[0].shape[0]
    copies = []
    for s in range(reps):
        first = wrap(where[1] - s, reps) * blocks
        copies.append(pltpu.make_async_copy(shares[s], out.at[pl.ds(first, blocks)], sems.at[s]))
        copies[s].start()
    for copy in copies:
        copy.wait()


def lay_blocks(where, shares, shape):
    reps = len(shares)
    return pl.pallas_call(
        functools.partial(lay_kernel, reps),
        out_shape=jax.ShapeDtypeStruct(shape, BF16),
        in_specs=[smem()] + [vmem()] * reps,
        out_specs=hbm(),
        scratch_shapes=[pltpu.SemaphoreType.DMA((reps,))],
        compiler_params=pltpu.CompilerParams(vmem_limit_bytes=2 * MIB),
        cost_estimate=pl.CostEstimate(flops=0, bytes_accessed=32 * MIB, transcendentals=0),
    )(where, *shares)


def shift(value, steps):
    reps = lax.axis_size("rep")
    if steps % reps == 0:
        return value
    return lax.ppermute(value, "rep", [(i, (i + steps) % reps) for i in range(reps)])


def on_device(cotangent, relu_mask, aggregated, weight, tiles, col_block, live_count):
    blocks, features, nodes = cotangent.shape
    slabs, reps = lax.axis_size("blk"), lax.axis_size("rep")
    width = weight.shape[1]
    where = jnp.stack([lax.axis_index("blk"), lax.axis_index("rep")]).astype(jnp.int32)

    pair = [(i, i ^ 1) for i in range(slabs)]
    to_one = [(i, (i + (1 if i % 2 else -1)) % slabs) for i in range(slabs)]
    to_two = [(i, (i + (2 if i % 2 else -2)) % slabs) for i in range(slabs)]
    aside, own, one, two, *packed = contributions(
        where, col_block, live_count, cotangent, relu_mask, aggregated, weight, tiles, slabs, reps
    )
    aside = lax.ppermute(aside, "blk", pair)
    two_in = lax.ppermute(two, "blk", to_two)
    one = add(one, aside)
    one_in = [lax.ppermute(part, "blk", to_one) for part in one]

    packed = [shift(value, s) for s, value in enumerate(packed)]
    shares = total_shares(where, aside, own, two_in, one_in, reps)
    held, _ = lax.optimization_barrier((packed, shares))
    pieces = weight_partial(where, held, blocks // reps)
    pieces = [shift(value, -s) for s, value in enumerate(pieces)]
    shares = [shift(value, s) for s, value in enumerate(shares)]
    outs = [shift(value, s) for s, value in enumerate(mix(where, shares, packed))]
    input_grad = lay_blocks(where, outs, cotangent.shape)

    grad_w = sum(value.astype(F32) for value in pieces)
    grad_w = grad_w + lax.ppermute(grad_w, "blk", pair)
    parts = [
        lax.ppermute(grad_w, "blk", [(i, i ^ step) for i in range(slabs)])
        for step in range(2, slabs, 2)
    ]
    parts, _ = lax.optimization_barrier((parts, input_grad))
    grad_w = grad_w + sum(parts)
    grad_w = grad_w.transpose(1, 0, 2).reshape(features, width)
    return input_grad, grad_w * (1.0 / math.sqrt(slabs * blocks * nodes))


def solution(mesh):
    placed = (
        P("blk", "rep", None),
        P("blk", "rep", None),
        P("blk", "rep", None),
        P("rep", None),
        P("blk", None, None, None),
        P("blk", None),
        P("blk"),
    )
    return jax.shard_map(
        on_device,
        mesh=mesh,
        in_specs=placed,
        out_specs=(P("blk", "rep", None), P("rep", None)),
        check_vma=False,
    )
```
